32 devices in a mesh: seq: 16 (over z, y, core), head: 2 (over x).
Axes of the slice: x: 2, y: 2, z: 4, core: 2. Of those that a mesh axis runs over, the one named last changes fastest.
Arguments:
- layer_input: bfloat16 [4, 1024, 1024], P(None, 'seq'), may hold values from -6 to 6
- output_grad: bfloat16 [4, 1024, 1024], P(None, 'seq'), may hold values from -6 to 6
- random_pick: int32 [4, 16, 16, 3], P(None, 'seq', 'head'), may hold values from 0 to 65519
- doc_blocks: int32 [8], replicated, may hold values from 1 to 32, 64 in all
- last_fill: int32 [8], replicated, may hold values from 1 to 64
- shard_owner: int32 [16], replicated, may hold values from 0 to 15, each once
- qkv_weight: float32 [3, 1024, 1024], P(None, 'seq', 'head'), may hold values from -0.1875 to 0.1875
- qkv_first: float32 [3, 1024, 1024], P(None, 'seq', 'head'), may hold values from -40 to 40
- qkv_second: float32 [3, 1024, 1024], P(None, 'seq', 'head'), may hold values from 4.096 to 16.384
- proj_weight: float32 [1024, 1024], P('head', 'seq'), may hold values from -3 to 3
- proj_first: float32 [1024, 1024], P('head', 'seq'), may hold values from -6 to 6
- proj_second: float32 [1024, 1024], P('head', 'seq'), may hold values from 0.016 to 0.064
- up_weight: float32 [1024, 4096], P('seq', 'head'), may hold values from -0.1875 to 0.1875
- up_first: float32 [1024, 4096], P('seq', 'head'), may hold values from -6 to 6
- up_second: float32 [1024, 4096], P('seq', 'head'), may hold values from 0.256 to 1.024
- down_weight: float32 [4096, 1024], P('head', 'seq'), may hold values from -0.09375 to 0.09375
- down_first: float32 [4096, 1024], P('head', 'seq'), may hold values from -20 to 20
- down_second: float32 [4096, 1024], P('head', 'seq'), may hold values from 1.024 to 4.096
- vec_params: float32 [9, 1024], replicated, may hold values from -1 to 1.83, as said below
- vec_first: float32 [9, 1024], replicated, may hold values from -40 to 40
- vec_second: float32 [9, 1024], replicated, may hold values from 4.096 to 16.384
Outputs:
- layer_output: bfloat16 [4, 1024, 1024], P(None, 'seq')
- input_grad: float32 [4, 1024, 1024], P(None, 'seq')
- qkv_new: float32 [3, 1024, 1024], P(None, 'seq', 'head')
- qkv_first_new: float32 [3, 1024, 1024], P(None, 'seq', 'head')
- qkv_second_new: float32 [3, 1024, 1024], P(None, 'seq', 'head')
- qkv_copy: bfloat16 [3, 1024, 1024], P(None, 'seq', 'head')
- proj_new: float32 [1024, 1024], P('head', 'seq')
- proj_first_new: float32 [1024, 1024], P('head', 'seq')
- proj_second_new: float32 [1024, 1024], P('head', 'seq')
- proj_copy: bfloat16 [1024, 1024], P('head', 'seq')
- up_new: float32 [1024, 4096], P('seq', 'head')
- up_first_new: float32 [1024, 4096], P('seq', 'head')
- up_second_new: float32 [1024, 4096], P('seq', 'head')
- up_copy: bfloat16 [1024, 4096], P('seq', 'head')
- down_new: float32 [4096, 1024], P('head', 'seq')
- down_first_new: float32 [4096, 1024], P('head', 'seq')
- down_second_new: float32 [4096, 1024], P('head', 'seq')
- down_copy: bfloat16 [4096, 1024], P('head', 'seq')
- vec_new: float32 [9, 1024], replicated
- vec_first_new: float32 [9, 1024], replicated
- vec_second_new: float32 [9, 1024], replicated
The draws below stay inside these ranges and needn't reach their ends.
Inputs may be any that keep to these rules, and one draw needn't show every extreme that they name: `doc_blocks`: blocks taken by each of 8 documents packed in order; they sum to 64, and one document has exactly 32. `last_fill`: tokens of a document's last block that belong to it. `shard_owner`: A permutation: every index of seq owns exactly one block of weight rows. `vec_params`: rows 0 and 2 are the two norms' gains, rows 1 and 3 their shifts, row 4 the bias of the second feed-forward projection, rows 5 to 8 the bias of the first, 1024 values to a row; gains are positive.
All inputs are finite; a program needn't handle non-finite values.
Results may differ from the reference program's by a relative error of at most 0.015.
Values may be sent and summed in bfloat16 or wider, within the bound.
No kernel may reach another device: no remote copies, remote signals or barrier semaphores. Data moves between devices by JAX's collectives and lax.ppermute only.
A program may use at most 256 MiB of HBM per device.

```python
import math
import jax
import jax.numpy as jnp
import numpy as np
from jax import lax

D = 1024
H = 16
DH = 64
FF = 4096
BLOCK = 64
RAND = 3
STEP = 10
BPD = 4
LANES = 16
SEQ_ROWS = 1024
NBLK = 64
TOKENS = 4096
SEQS = 8
LONGB = 32
VECS = 9
N_SEQ = 16
N_HEAD = 2


def draw_vec_params(key, part):
    key = jax.random.fold_in(key, 7)
    key_gain, key_shift = jax.random.split(key)
    gain_rows = jnp.exp(jax.random.uniform(key_gain, (VECS, D), jnp.float32, -0.5, 0.5))
    shift_rows = jnp.clip(0.3 * jax.random.normal(key_shift, (VECS, D), jnp.float32), -1.0, 1.0)
    row_ids = jnp.arange(VECS)[:, None]
    return jnp.where((row_ids == 0) | (row_ids == 2), gain_rows, shift_rows)


def place_ends(array, stream_key, low, high):
    place = [jax.random.randint(jax.random.fold_in(stream_key, axis), (), 0, length) for axis, length in enumerate(array.shape)]
    widest = array.shape.index(max(array.shape))
    neighbour = place[:widest] + [(place[widest] + 1) % array.shape[widest]] + place[widest + 1:]
    return array.at[tuple(place)].set(low).at[tuple(neighbour)].set(high)


def block_scale(stream_key, shape, cuts, low, largest):
    factor_of = 1.0
    for dim, blocks in cuts:
        heights = jax.random.uniform(jax.random.fold_in(jax.random.fold_in(stream_key, 6), dim), (blocks,), jnp.float32, low / len(cuts), largest / len(cuts))
        factor_of = factor_of * jnp.repeat(jnp.exp(heights), shape[dim] // blocks).reshape((-1,) + (1,) * (len(shape) - 1 - dim))
    return factor_of


def length_profile(number_of, total, most, slope):
    loads = [(1 << 20) // math.isqrt(standing ** slope) + 1 for standing in range(2, number_of + 1)]
    surplus, holding = total - most - (number_of - 1), [1] * (number_of - 1)
    while surplus > 0:
        movable = [i for i in range(number_of - 1) if holding[i] < most]
        whole, budget = sum([loads[i] for i in movable]), surplus
        for i in movable:
            more = min(most - holding[i], max(1, budget * loads[i] // whole), surplus)
            holding[i] = holding[i] + more
            surplus = surplus - more
    return np.array([most] + holding)


def uneven_parts(own_key, amount, total, most, slope):
    if amount == 2:
        one = jax.random.randint(own_key, (), max(1, total - most), min(most, total - 1) + 1)
        return jnp.stack([one, total - one])
    sizes = jnp.asarray(length_profile(amount, total, most, slope), jnp.int32)
    twos = (amount - 1) // 2
    giver, sink = sizes[1:1 + 2 * twos:2], sizes[2:2 + 2 * twos:2]
    slack = jnp.minimum(giver - 1, most - sink)
    moved = jax.random.randint(jax.random.fold_in(own_key, 1), (twos,), 0, 1 << 20) % (slack + 1)
    sizes = sizes.at[1:1 + 2 * twos:2].set(giver - moved).at[2:2 + 2 * twos:2].set(sink + moved)
    return sizes[jax.random.permutation(jax.random.fold_in(own_key, 2), amount)]


def bell_draw(own_key, shape, width, bound, shards=(), held_as=jnp.bfloat16):
    array = width * jax.random.normal(own_key, shape, jnp.float32)
    if shards:
        array = array * block_scale(own_key, shape, shards, -0.22, 0.18)
    return jnp.clip(array, -bound, bound).astype(held_as)


def setup_inputs(seed: int = 0) -> dict:
    key_list = jax.random.split(jax.random.key(seed), 22)
    return {
        "layer_input": bell_draw(key_list[0], (BPD, SEQ_ROWS, D), 1.0, 6.0, ((1, 16),)),
        "output_grad": bell_draw(key_list[1], (BPD, SEQ_ROWS, D), 1.0, 6.0, ((1, 16),)),
        "random_pick": place_ends(jax.random.randint(key_list[2], (BPD, LANES, H, RAND), 0, 65520), jax.random.fold_in(key_list[2], 1), 0, 65519).astype(jnp.int32),
        "doc_blocks": uneven_parts(key_list[3], SEQS, NBLK, LONGB, 2).astype(jnp.int32),
        "last_fill": place_ends(jax.random.randint(key_list[4], (SEQS,), 1, BLOCK + 1), jax.random.fold_in(key_list[4], 1), 1, BLOCK).astype(jnp.int32),
        "shard_owner": jax.random.permutation(key_list[5], LANES).astype(jnp.int32),
        "qkv_weight": bell_draw(key_list[6], (3, D, D), D ** -0.5, 0.1875, ((1, 16), (2, 2)), jnp.float32),
        "qkv_first": bell_draw(key_list[7], (3, D, D), (0.11 * TOKENS ** 0.5), 40.0, ((1, 16), (2, 2)), jnp.float32),
        "qkv_second": jnp.clip(jnp.exp(math.log(16.384) - 1.3862944 * jax.random.uniform(key_list[8], (3, D, D), jnp.float32) ** block_scale(key_list[8], (3, D, D), ((1, 16), (2, 2)), -0.2, 0.2)), 4.096, 16.384),
        "proj_weight": bell_draw(key_list[9], (D, D), (max(D // 256, 1)) ** -0.5, 3.0, ((0, 2), (1, 16)), jnp.float32),
        "proj_first": bell_draw(key_list[10], (D, D), (0.11 * TOKENS ** 0.5 / 16), 6.0, ((0, 2), (1, 16)), jnp.float32),
        "proj_second": jnp.clip(jnp.exp(math.log(0.064) - 1.3862944 * jax.random.uniform(key_list[11], (D, D), jnp.float32) ** block_scale(key_list[11], (D, D), ((0, 2), (1, 16)), -0.2, 0.2)), 0.016, 0.064),
        "up_weight": bell_draw(key_list[12], (D, FF), D ** -0.5, 0.1875, ((0, 16), (1, 2)), jnp.float32),
        "up_first": bell_draw(key_list[13], (D, FF), (0.11 * TOKENS ** 0.5 / 4), 6.0, ((0, 16), (1, 2)), jnp.float32),
        "up_second": jnp.clip(jnp.exp(math.log(1.024) - 1.3862944 * jax.random.uniform(key_list[14], (D, FF), jnp.float32) ** block_scale(key_list[14], (D, FF), ((0, 16), (1, 2)), -0.2, 0.2)), 0.256, 1.024),
        "down_weight": bell_draw(key_list[15], (FF, D), FF ** -0.5, 0.09375, ((0, 2), (1, 16)), jnp.float32),
        "down_first": bell_draw(key_list[16], (FF, D), (0.055 * TOKENS ** 0.5), 20.0, ((0, 2), (1, 16)), jnp.float32),
        "down_second": jnp.clip(jnp.exp(math.log(4.096) - 1.3862944 * jax.random.uniform(key_list[17], (FF, D), jnp.float32) ** block_scale(key_list[17], (FF, D), ((0, 2), (1, 16)), -0.2, 0.2)), 1.024, 4.096),
        "vec_params": draw_vec_params(jax.random.fold_in(key_list[21], 71), 0),
        "vec_first": bell_draw(key_list[19], (VECS, D), (0.11 * TOKENS ** 0.5), 40.0, (), jnp.float32),
        "vec_second": jnp.clip(jnp.exp(jax.random.uniform(key_list[20], (VECS, D), jnp.float32, math.log(4.096), math.log(16.384))), 4.096, 16.384),
    }


@jax.custom_vjp
def low(v):
    return lax.optimization_barrier(v.astype(jnp.bfloat16)).astype(jnp.float32)

@jax.custom_vjp
def low_back(v):
    return v

def low_keep(v):
    return (low(v), None)

def low_pass(kept, grad):
    return (grad,)

def back_keep(v):
    return (v, None)

def back_low(kept, grad):
    return (low(grad),)
low.defvjp(low_keep, low_pass)
low_back.defvjp(back_keep, back_low)
eps_norm = 1e-05
masked_score = -1e+30
beta_one = 0.9
beta_two = 0.999
eps_adam = 1e-08
decay_rate = 0.01
rate_qkv = 0.1
rate_proj = 1.0
rate_up = 0.1
rate_down = 0.05
rate_vector = 2.0
highest = lax.Precision.HIGHEST

def lookup(index_table, index_rows):
    matches = index_rows[..., None] == jnp.arange(index_table.shape[0], dtype=jnp.int32)
    return lax.optimization_barrier(jnp.sum(jnp.where(matches, index_table, 0), axis=-1)).astype(jnp.int32)

def owning_doc(doc_end, block_ids):
    return lax.optimization_barrier(jnp.sum((block_ids[..., None] >= doc_end).astype(jnp.int32), axis=-1)).astype(jnp.int32)

def doc_tables(doc_blocks, last_fill):
    doc_end = jnp.cumsum(doc_blocks).astype(jnp.int32)
    doc_start = (doc_end - doc_blocks).astype(jnp.int32)
    doc_length = ((doc_blocks - 1) * BLOCK + last_fill).astype(jnp.int32)
    return (doc_end, doc_start, doc_length)

def key_lists(query_ids, pick_table, doc_blocks, last_fill, block_total):
    doc_end, doc_start, doc_length = doc_tables(doc_blocks, last_fill)
    query_doc = owning_doc(doc_end, query_ids)
    doc_first = lookup(doc_start, query_doc)
    doc_count = lookup(doc_blocks, query_doc)
    query_length = lookup(doc_length, query_doc)
    head_count = pick_table.shape[1]
    fixed_ids = jnp.stack([(query_ids - 1) % block_total, query_ids, (query_ids + 1) % block_total, doc_first, (doc_first + 1) % block_total], axis=-1)
    random_ids = doc_first[:, None, None] + pick_table % doc_count[:, None, None]
    key_ids = jnp.concatenate([jnp.broadcast_to(fixed_ids[:, None, :], (query_ids.shape[0], head_count, 5)), random_ids], axis=-1).astype(jnp.int32)
    key_pos = (key_ids - doc_first[:, None, None])[..., None] * BLOCK + jnp.arange(BLOCK, dtype=jnp.int32)
    same_doc = owning_doc(doc_end, key_ids) == query_doc[:, None, None]
    key_live = same_doc[..., None] & (key_pos < query_length[:, None, None, None])
    return (key_ids, key_live)

def norm_rows(token_rows, gain_row, bias_row):
    row_mean = lax.optimization_barrier(jnp.mean(token_rows, axis=-1, keepdims=True))
    centred = token_rows - row_mean
    row_var = lax.optimization_barrier(jnp.mean(centred * centred, axis=-1, keepdims=True))
    return centred * lax.rsqrt(row_var + eps_norm) * gain_row + bias_row

def to_true(weight, dim_pos, shard_owner):
    moved_axis = jnp.moveaxis(weight, dim_pos, 0)
    shaped = moved_axis.reshape((N_SEQ, moved_axis.shape[0] // N_SEQ) + moved_axis.shape[1:])
    picked = shaped[shard_owner]
    return jnp.moveaxis(picked.reshape(moved_axis.shape), 0, dim_pos)

def to_stored(weight, dim_pos, shard_owner):
    moved_axis = jnp.moveaxis(weight, dim_pos, 0)
    shaped = moved_axis.reshape((N_SEQ, moved_axis.shape[0] // N_SEQ) + moved_axis.shape[1:])
    placed = jnp.zeros_like(shaped).at[shard_owner].set(shaped)
    return jnp.moveaxis(placed.reshape(moved_axis.shape), 0, dim_pos)

def ffn_group(group_in, up_cols, bias_cols, down_rows):
    hidden = low_back(jnp.dot(group_in, up_cols, precision=highest)) + bias_cols
    active = low(jax.nn.gelu(hidden, approximate=True))
    return low(jnp.dot(active, down_rows, precision=highest))

def forward(token_rows, qkv_full, proj_full, up_full, down_full, vec_full, key_ids, key_live):
    block_total = key_ids.shape[0]
    group_cols = D // N_HEAD
    group_units = FF // N_HEAD
    score_scale = DH ** (-0.5)
    low_one = low(norm_rows(token_rows, vec_full[0], vec_full[1]))
    qkv_parts = []
    for group_index in range(N_HEAD):
        cols_here = slice(group_index * group_cols, (group_index + 1) * group_cols)
        group_in = low_back(low_one)
        projected = jnp.einsum('td,cde->cte', group_in, qkv_full[:, :, cols_here], precision=highest)
        qkv_parts.append(low_back(low(projected)))
    qkv_rows = jnp.concatenate(qkv_parts, axis=-1)
    queries = qkv_rows[0].reshape(block_total, BLOCK, H, DH)
    keys_table = qkv_rows[1].reshape(block_total, BLOCK, H, DH).transpose(0, 2, 1, 3)
    vals_table = qkv_rows[2].reshape(block_total, BLOCK, H, DH).transpose(0, 2, 1, 3)
    group_span = math.gcd(block_total, 64)
    steps_count = block_total // group_span
    head_pick = jnp.arange(H, dtype=jnp.int32)[None, :, None]

    def attend(pieces):
        query_block, id_block, live_block = pieces
        key_sel = keys_table[id_block, head_pick]
        val_sel = vals_table[id_block, head_pick]
        scores = low_back(jnp.einsum('bthd,bhckd->bhtck', query_block, key_sel, precision=highest) * score_scale)
        masked = jnp.where(live_block[:, :, None], scores, masked_score)
        row_max = lax.optimization_barrier(jnp.max(masked, axis=(3, 4), keepdims=True))
        exp_scores = jnp.exp(masked - row_max)
        attn_probs = exp_scores / lax.optimization_barrier(jnp.sum(exp_scores, axis=(3, 4), keepdims=True))
        return jnp.einsum('bhtck,bhckd->bthd', low(attn_probs), val_sel, precision=highest)
    context = lax.map(jax.checkpoint(attend), (queries.reshape(steps_count, group_span, BLOCK, H, DH), key_ids.reshape(steps_count, group_span, H, 8), key_live.reshape(steps_count, group_span, H, 8, BLOCK)))
    context = low_back(low(context.reshape(block_total * BLOCK, D)))
    attn_total = jnp.zeros_like(token_rows)
    for group_index in range(N_HEAD):
        cols_here = slice(group_index * group_cols, (group_index + 1) * group_cols)
        attn_total = attn_total + low(jnp.dot(context[:, cols_here], proj_full[cols_here], precision=highest))
    mid_rows = token_rows + low_back(attn_total)
    low_two = low(norm_rows(mid_rows, vec_full[2], vec_full[3]))
    up_bias = vec_full[5:].reshape(FF)
    ffn_total = jnp.zeros_like(token_rows)
    for group_index in range(N_HEAD):
        units_here = slice(group_index * group_units, (group_index + 1) * group_units)
        ffn_total = ffn_total + jax.checkpoint(ffn_group)(low_back(low_two), up_full[:, units_here], up_bias[units_here], down_full[units_here])
    return mid_rows + low_back(ffn_total) + vec_full[4]

def adam_step(param_old, gradient, first_old, second_old, step_rate):
    first_new = beta_one * first_old + (1.0 - beta_one) * gradient
    second_new = beta_two * second_old + (1.0 - beta_two) * gradient * gradient
    first_hat = first_new / (1.0 - beta_one ** STEP)
    second_hat = second_new / (1.0 - beta_two ** STEP)
    updated = param_old - step_rate * (first_hat / (jnp.sqrt(second_hat) + eps_adam) + decay_rate * param_old)
    return (updated, first_new, second_new)

def reference(layer_input, output_grad, random_pick, doc_blocks, last_fill, shard_owner, qkv_weight, qkv_first, qkv_second, proj_weight, proj_first, proj_second, up_weight, up_first, up_second, down_weight, down_first, down_second, vec_params, vec_first, vec_second):
    block_total = BPD * N_SEQ
    token_rows = layer_input.reshape(block_total * BLOCK, D).astype(jnp.float32)
    grad_rows = output_grad.reshape(block_total * BLOCK, D).astype(jnp.float32)
    pick_table = random_pick.reshape(block_total, H, RAND)
    key_ids, key_live = key_lists(jnp.arange(block_total, dtype=jnp.int32), pick_table, doc_blocks, last_fill, block_total)

    def rounded(weight, dim_pos):
        return to_true(weight.astype(jnp.bfloat16).astype(jnp.float32), dim_pos, shard_owner)
    qkv_full = rounded(qkv_weight, 1)
    proj_full = rounded(proj_weight, 1)
    up_full = rounded(up_weight, 0)
    down_full = rounded(down_weight, 1)

    def layer(rows_in, qkv_in, proj_in, up_in, down_in, vec_in):
        return forward(rows_in, qkv_in, proj_in, up_in, down_in, vec_in, key_ids, key_live)
    layer_out, pullback = jax.vjp(layer, token_rows, qkv_full, proj_full, up_full, down_full, vec_params)
    all_grads = pullback(grad_rows)
    qkv_grad = to_stored(all_grads[1], 1, shard_owner)
    proj_grad = to_stored(all_grads[2], 1, shard_owner)
    up_grad = to_stored(all_grads[3], 0, shard_owner)
    down_grad = to_stored(all_grads[4], 1, shard_owner)
    qkv_new, qkv_first_new, qkv_second_new = adam_step(qkv_weight, qkv_grad, qkv_first, qkv_second, rate_qkv)
    proj_new, proj_first_new, proj_second_new = adam_step(proj_weight, proj_grad, proj_first, proj_second, rate_proj)
    up_new, up_first_new, up_second_new = adam_step(up_weight, up_grad, up_first, up_second, rate_up)
    down_new, down_first_new, down_second_new = adam_step(down_weight, down_grad, down_first, down_second, rate_down)
    vec_new, vec_first_new, vec_second_new = adam_step(vec_params, all_grads[5], vec_first, vec_second, rate_vector)
    layer_output = layer_out.astype(jnp.bfloat16).reshape(BPD, N_SEQ * BLOCK, D)
    input_grad = all_grads[0].reshape(BPD, N_SEQ * BLOCK, D)
    return (layer_output, input_grad, qkv_new, qkv_first_new, qkv_second_new, qkv_new.astype(jnp.bfloat16), proj_new, proj_first_new, proj_second_new, proj_new.astype(jnp.bfloat16), up_new, up_first_new, up_second_new, up_new.astype(jnp.bfloat16), down_new, down_first_new, down_second_new, down_new.astype(jnp.bfloat16), vec_new, vec_first_new, vec_second_new)
```

```python
import functools

import jax
import jax.numpy as jnp
from jax import lax
from jax.experimental import pallas as pl
from jax.experimental.pallas import tpu as pltpu
from jax.sharding import PartitionSpec as P

D = 1024
DH = 64
FF = 4096
BLOCK = 64
STEP = 10
LISTED = 8

eps_norm = 1e-05
masked_score = -1e30
beta_one = 0.9
beta_two = 0.999
eps_adam = 1e-08
decay_rate = 0.01
rate_qkv = 0.1
rate_proj = 1.0
rate_up = 0.1
rate_down = 0.05
rate_vector = 2.0

bf16 = jnp.bfloat16
f32 = jnp.float32


def lookup(index_table, index_rows):
    matches = index_rows[..., None] == jnp.arange(index_table.shape[0], dtype=jnp.int32)
    return jnp.sum(jnp.where(matches, index_table, 0), axis=-1)


def owning_doc(doc_end, block_ids):
    return jnp.sum((block_ids[..., None] >= doc_end).astype(jnp.int32), axis=-1)


def dot(lhs, rhs, lhs_dim, rhs_dim):
    return lax.dot_general(
        lhs, rhs, (((lhs_dim,), (rhs_dim,)), ((), ())), preferred_element_type=f32
    )


def norm_rows(token_rows, gain_row, bias_row):
    row_mean = jnp.mean(token_rows, axis=-1, keepdims=True)
    centred = token_rows - row_mean
    row_var = jnp.mean(centred * centred, axis=-1, keepdims=True)
    inv_scale = lax.rsqrt(row_var + eps_norm)
    unit_rows = centred * inv_scale
    return (unit_rows * gain_row + bias_row, unit_rows, inv_scale)


def norm_back(grad_in, unit_rows, inv_scale, gain_row):
    scaled = grad_in * gain_row
    first_mean = jnp.mean(scaled, axis=-1, keepdims=True)
    second_mean = jnp.mean(scaled * unit_rows, axis=-1, keepdims=True)
    return inv_scale * (scaled - first_mean - unit_rows * second_mean)


def gelu_tanh(values):
    return jax.nn.gelu(values, approximate=True)


def adam_step(param_old, gradient, first_old, second_old, step_rate):
    first_new = beta_one * first_old + (1.0 - beta_one) * gradient
    second_new = beta_two * second_old + (1.0 - beta_two) * gradient * gradient
    first_hat = first_new / (1.0 - beta_one**STEP)
    second_hat = second_new / (1.0 - beta_two**STEP)
    updated = param_old - step_rate * (
        first_hat / (jnp.sqrt(second_hat) + eps_adam) + decay_rate * param_old
    )
    return (updated, first_new, second_new)


def xor_permute(value, axis, mask):
    count = lax.axis_size(axis)
    return lax.ppermute(value, axis, [(i, i ^ mask) for i in range(count)])


def head_sum(partial_low):
    count = lax.axis_size("head")
    if count & (count - 1):
        return lax.psum(partial_low.astype(f32), "head")
    total = partial_low
    step = 1
    while step < count:
        other = xor_permute(total.astype(bf16), "head", step)
        total = total.astype(f32) + other.astype(f32)
        step *= 2
    return total.astype(f32)


def total_sum(value):
    for axis in ("seq", "head"):
        count = lax.axis_size(axis)
        if count & (count - 1):
            value = lax.psum(value, axis)
            continue
        step = 1
        while step < count:
            value = value + xor_permute(value, axis, step)
            step *= 2
    return value


def attend_kernel(off_ref, q_ref, kv_ref, bias_ref, ctx_ref, prob_ref):
    lanes, rows = q_ref.shape[0], q_ref.shape[1]
    left = lax.broadcasted_iota(jnp.int32, (rows, 2 * DH), 1) < DH
    scale = DH**-0.5

    def step(i, carry):
        q_pair = q_ref[i].astype(f32) * scale
        outs = []
        for half in range(2):
            q_one = q_pair if half == 0 else pltpu.roll(q_pair, DH, 1)
            q_one = jnp.where(left, q_one, 0.0).astype(bf16)
            listed = jnp.concatenate(
                [
                    kv_ref[pl.ds(pl.multiple_of(off_ref[2 * i + half, j], BLOCK), BLOCK), :]
                    for j in range(LISTED)
                ],
                axis=0,
            )
            scores = dot(q_one, listed, 1, 1) + bias_ref[i, half : half + 1, :]
            row_max = jnp.max(scores, axis=1, keepdims=True)
            grown = jnp.exp(scores - row_max)
            total = jnp.sum(grown, axis=1, keepdims=True)
            probs = (grown * (1.0 / total)).astype(bf16)
            prob_ref[i, half] = probs
            outs.append(dot(probs, listed, 1, 0))
        ctx_ref[i] = jnp.where(left, pltpu.roll(outs[0], DH, 1), outs[1]).astype(bf16)
        return carry

    lax.fori_loop(0, lanes, step, 0)


def attend_back_kernel(off_ref, q_ref, kv_ref, prob_ref, dctx_ref, dq_ref, dkv_ref):
    lanes, rows = q_ref.shape[0], q_ref.shape[1]
    left = lax.broadcasted_iota(jnp.int32, (rows, 2 * DH), 1) < DH
    scale = DH**-0.5
    dkv_ref[...] = jnp.zeros_like(dkv_ref)

    def step(i, carry):
        q_pair = q_ref[i].astype(f32) * scale
        d_pair = dctx_ref[i].astype(f32)
        outs = []
        for half in range(2):
            q_one = q_pair if half == 0 else pltpu.roll(q_pair, DH, 1)
            q_one = jnp.where(left, q_one, 0.0).astype(bf16)
            d_one = pltpu.roll(d_pair, DH, 1) if half == 0 else d_pair
            d_one = jnp.where(left, 0.0, d_one).astype(bf16)
            offs = [
                pl.multiple_of(off_ref[2 * i + half, j], BLOCK) for j in range(LISTED)
            ]
            listed = jnp.concatenate([kv_ref[pl.ds(o, BLOCK), :] for o in offs], axis=0)
            probs_low = prob_ref[i, half]
            probs = probs_low.astype(f32)
            prob_grad = dot(d_one, listed, 1, 1)
            weighted = probs * prob_grad
            row_dot = jnp.sum(weighted, axis=1, keepdims=True)
            score_low = (weighted - probs * row_dot).astype(bf16)
            outs.append(dot(score_low, listed, 1, 0) * scale)
            both = jnp.concatenate([score_low, probs_low], axis=0)
            mates = jnp.concatenate([q_one, d_one], axis=0)
            kv_grad = dot(both, mates, 0, 0)
            for j in range(LISTED):
                at = pl.ds(offs[j], BLOCK)
                dkv_ref[at, :] += kv_grad[j * BLOCK : (j + 1) * BLOCK]
        dq_ref[i] = jnp.where(left, outs[0], pltpu.roll(outs[1], DH, 1)).astype(bf16)
        return carry

    lax.fori_loop(0, lanes, step, 0)


VMEM_LIMIT = 48 * 1024 * 1024


def in_vmem():
    return pl.BlockSpec(memory_space=pltpu.VMEM)


def in_smem():
    return pl.BlockSpec(memory_space=pltpu.SMEM)


def attend(offsets, q_pairs, kv_rows, bias):
    lanes, rows, width = q_pairs.shape
    return pl.pallas_call(
        attend_kernel,
        out_shape=(
            jax.ShapeDtypeStruct((lanes, rows, width), bf16),
            jax.ShapeDtypeStruct((lanes, 2, rows, LISTED * BLOCK), bf16),
        ),
        in_specs=[in_smem(), in_vmem(), in_vmem(), in_vmem()],
        out_specs=(in_vmem(), in_vmem()),
        compiler_params=pltpu.CompilerParams(vmem_limit_bytes=VMEM_LIMIT),
    )(offsets, q_pairs, kv_rows, bias)


def attend_back(offsets, q_pairs, kv_rows, probs, dctx_pairs):
    lanes, rows, width = q_pairs.shape
    return pl.pallas_call(
        attend_back_kernel,
        out_shape=(
            jax.ShapeDtypeStruct((lanes, rows, width), bf16),
            jax.ShapeDtypeStruct(kv_rows.shape, f32),
        ),
        in_specs=[in_smem(), in_vmem(), in_vmem(), in_vmem(), in_vmem()],
        out_specs=(in_vmem(), in_vmem()),
        compiler_params=pltpu.CompilerParams(vmem_limit_bytes=VMEM_LIMIT),
    )(offsets, q_pairs, kv_rows, probs, dctx_pairs)


def body(
    layer_input,
    output_grad,
    random_pick,
    doc_blocks,
    last_fill,
    shard_owner,
    qkv_weight,
    qkv_first,
    qkv_second,
    proj_weight,
    proj_first,
    proj_second,
    up_weight,
    up_first,
    up_second,
    down_weight,
    down_first,
    down_second,
    vec_params,
    vec_first,
    vec_second,
):
    lanes = lax.axis_size("seq")
    lane_index = lax.axis_index("seq")
    head_groups = lax.axis_size("head")
    head_index = lax.axis_index("head")
    slots = layer_input.shape[0]
    heads = random_pick.shape[2]
    feat = heads * DH
    units = up_weight.shape[1]
    rows = slots * BLOCK
    block_total = slots * lanes
    share = lanes // heads
    part_rows = rows // share
    pair_rows = part_rows // 2
    my_part = lane_index % share
    width = D // lanes

    picks = random_pick[:, 0].transpose(1, 0, 2).reshape(heads, slots * 3)
    picks = jnp.broadcast_to(picks[:, None], (heads, share, slots * 3)).reshape(lanes, slots * 3)
    picks = lax.all_to_all(picks, "seq", 0, 0, tiled=True).reshape(lanes, slots, 3)

    doc_end = jnp.cumsum(doc_blocks)
    doc_start = doc_end - doc_blocks
    doc_length = (doc_blocks - 1) * BLOCK + last_fill
    half_slot = (my_part * part_rows + jnp.arange(2, dtype=jnp.int32) * pair_rows) // BLOCK
    query_ids = half_slot[None, :] * lanes + jnp.arange(lanes, dtype=jnp.int32)[:, None]
    pick_half = jnp.sum(
        jnp.where(
            (half_slot[:, None] == jnp.arange(slots, dtype=jnp.int32)[None, :])[None, :, :, None],
            picks[:, None],
            0,
        ),
        axis=2,
    )
    query_doc = owning_doc(doc_end, query_ids)
    doc_first = lookup(doc_start, query_doc)
    doc_count = lookup(doc_blocks, query_doc)
    query_length = lookup(doc_length, query_doc)
    key_ids = jnp.concatenate(
        [
            jnp.stack(
                [
                    (query_ids - 1) % block_total,
                    query_ids,
                    (query_ids + 1) % block_total,
                    doc_first,
                    (doc_first + 1) % block_total,
                ],
                axis=-1,
            ),
            doc_first[..., None] + pick_half % doc_count[..., None],
        ],
        axis=-1,
    )
    same_doc = owning_doc(doc_end, key_ids) == query_doc[..., None]
    live_count = jnp.where(
        same_doc, query_length[..., None] - (key_ids - doc_first[..., None]) * BLOCK, 0
    )
    token = jnp.arange(BLOCK, dtype=jnp.int32)
    bias = jnp.where(token < live_count[..., None], 0.0, masked_score).astype(f32)
    bias = bias.reshape(lanes, 2, LISTED * BLOCK)
    key_lane = key_ids % lanes
    key_slot = key_ids // lanes
    if part_rows >= BLOCK:
        part_slots = part_rows // BLOCK
        offsets = ((key_slot // part_slots) * lanes + key_lane) * part_rows + (
            key_slot % part_slots
        ) * BLOCK
    else:
        offsets = (key_lane * slots + key_slot) * BLOCK
    offsets = offsets.reshape(lanes * 2, LISTED)

    qkv_mine = qkv_weight.astype(bf16).transpose(1, 0, 2).reshape(width, 3 * feat)
    rest_mine = jnp.concatenate(
        [proj_weight.astype(bf16).T, up_weight.astype(bf16), down_weight.astype(bf16).T], axis=1
    )
    qkv_full = lax.all_gather(qkv_mine, "seq", axis=0, tiled=True)
    rest_full = lax.all_gather(rest_mine, "seq", axis=0, tiled=True)
    proj_full = rest_full[:, :feat]
    up_full = rest_full[:, feat : feat + units]
    down_full = rest_full[:, feat + units :]

    column = jnp.arange(D, dtype=jnp.int32)
    stored_at = lookup(shard_owner, column // width) * width + column % width
    place = (stored_at[:, None] == column[None, :]).astype(bf16)
    token_rows = dot(layer_input.reshape(rows, D), place, 1, 0)
    grad_low = dot(output_grad.reshape(rows, D), place, 1, 0).astype(bf16)
    grad_rows = grad_low.astype(f32)
    vec_rows = lax.dot_general(
        vec_params[:5],
        place.astype(f32),
        (((1,), (0,)), ((), ())),
        precision=lax.Precision.HIGHEST,
    )
    up_bias = lax.dynamic_slice_in_dim(vec_params[5:].reshape(FF), head_index * units, units)

    normed_one, unit_one, scale_one = norm_rows(token_rows, vec_rows[0], vec_rows[1])
    low_one = normed_one.astype(bf16)
    qkv_rows = dot(low_one, qkv_full, 1, 0).astype(bf16)
    by_head = qkv_rows.reshape(rows, 3, heads, DH)
    kv_send = by_head[:, 1:].transpose(2, 0, 1, 3).reshape(lanes, part_rows, 2 * DH)
    q_send = (
        by_head[:, 0]
        .reshape(share, 2, pair_rows, heads, DH)
        .transpose(3, 0, 2, 1, 4)
        .reshape(lanes, pair_rows, 2 * DH)
    )
    received = lax.all_to_all(
        jnp.concatenate([kv_send, q_send], axis=1), "seq", 0, 0, tiled=True
    )
    q_pairs = received[:, part_rows:]
    kv_parts = received[:, :part_rows][None]
    step = 1
    while step < share:
        other = xor_permute(kv_parts, "seq", step)
        high = (my_part & step) != 0
        kv_parts = jnp.where(
            high,
            jnp.concatenate([other, kv_parts], axis=0),
            jnp.concatenate([kv_parts, other], axis=0),
        )
        step *= 2
    if part_rows >= BLOCK:
        kv_rows = kv_parts.reshape(block_total * BLOCK, 2 * DH)
    else:
        kv_rows = kv_parts.transpose(1, 0, 2, 3).reshape(block_total * BLOCK, 2 * DH)
    ctx_pairs, probs = attend(offsets, q_pairs, kv_rows, bias)

    def pairs_to_rows(pairs):
        return (
            pairs.reshape(heads, share, pair_rows, 2, DH)
            .transpose(1, 3, 2, 0, 4)
            .reshape(rows, feat)
        )

    def rows_to_pairs(low_rows):
        return (
            low_rows.reshape(share, 2, pair_rows, heads, DH)
            .transpose(3, 0, 2, 1, 4)
            .reshape(lanes, pair_rows, 2 * DH)
        )

    context = pairs_to_rows(lax.all_to_all(ctx_pairs, "seq", 0, 0, tiled=True))
    attn_sum = head_sum(dot(context, proj_full, 1, 1).astype(bf16))
    mid_rows = token_rows + attn_sum
    normed_two, unit_two, scale_two = norm_rows(mid_rows, vec_rows[2], vec_rows[3])
    low_two = normed_two.astype(bf16)
    hidden = dot(low_two, up_full, 1, 0) + up_bias
    active = gelu_tanh(hidden).astype(bf16)
    act_grad = dot(grad_low, down_full, 1, 0)
    hidden_grad = jax.vjp(gelu_tanh, hidden)[1](act_grad)[0]
    hidden_low = hidden_grad.astype(bf16)
    two_grad = head_sum(dot(hidden_low, up_full, 1, 1).astype(bf16))
    ffn_sum = head_sum(dot(active, down_full, 1, 1).astype(bf16))
    result = (mid_rows + ffn_sum + vec_rows[4]).astype(bf16)
    up_bias_grad = jnp.sum(hidden_grad, axis=0)
    ffn_grads = jnp.concatenate(
        [dot(low_two, hidden_low, 0, 0).astype(bf16), dot(grad_low, active, 0, 0).astype(bf16)],
        axis=1,
    )
    ffn_owned = lax.psum_scatter(ffn_grads, "seq", scatter_dimension=0, tiled=True).astype(f32)

    mid_grad = grad_rows + norm_back(two_grad, unit_two, scale_two, vec_rows[2])
    attn_low = mid_grad.astype(bf16)
    ctx_grad = dot(attn_low, proj_full, 1, 0).astype(bf16)
    dctx_pairs = lax.all_to_all(rows_to_pairs(ctx_grad), "seq", 0, 0, tiled=True)
    dq_pairs, dkv_rows = attend_back(offsets, q_pairs, kv_rows, probs, dctx_pairs)
    if part_rows >= BLOCK:
        dkv_parts = dkv_rows.reshape(share, lanes, part_rows, 2 * DH)
    else:
        dkv_parts = dkv_rows.reshape(lanes, share, part_rows, 2 * DH).transpose(1, 0, 2, 3)
    step = share // 2
    while step >= 1:
        high = (my_part & step) != 0
        first, second = dkv_parts[:step], dkv_parts[step:]
        away = jnp.where(high, first, second).astype(bf16)
        stay = jnp.where(high, second, first)
        dkv_parts = stay + xor_permute(away, "seq", step).astype(f32)
        step //= 2
    returned = lax.all_to_all(
        jnp.concatenate([dkv_parts[0].astype(bf16), dq_pairs], axis=1),
        "seq",
        0,
        0,
        tiled=True,
    )
    dkv_back = (
        returned[:, :part_rows]
        .reshape(heads, rows, 2, DH)
        .transpose(1, 2, 0, 3)
        .reshape(rows, 2 * feat)
    )
    dqkv = jnp.concatenate([pairs_to_rows(returned[:, part_rows:]), dkv_back], axis=1)
    one_grad = head_sum(dot(dqkv, qkv_full, 1, 1).astype(bf16))
    attn_grads = jnp.concatenate(
        [dot(low_one, dqkv, 0, 0).astype(bf16), dot(attn_low, context, 0, 0).astype(bf16)],
        axis=1,
    )
    attn_owned = lax.psum_scatter(attn_grads, "seq", scatter_dimension=0, tiled=True).astype(f32)
    input_grad = mid_grad + norm_back(one_grad, unit_one, scale_one, vec_rows[0])

    shared_rows = jnp.stack(
        [
            jnp.sum(one_grad * unit_one, axis=0),
            jnp.sum(one_grad, axis=0),
            jnp.sum(two_grad * unit_two, axis=0),
            jnp.sum(two_grad, axis=0),
            jnp.sum(grad_rows, axis=0),
        ]
    )
    column_group = column // (D // head_groups)
    shared_rows = jnp.where((column_group == head_index)[None, :], shared_rows, 0.0)
    bias_rows = lax.dynamic_update_slice_in_dim(
        jnp.zeros((FF,), f32), up_bias_grad, head_index * units, 0
    ).reshape(FF // D, D)
    vec_grad = total_sum(jnp.concatenate([shared_rows, bias_rows], axis=0))

    back = (((1,), (1,)), ((), ()))
    layer_output = lax.dot_general(result, place, back, preferred_element_type=f32).astype(bf16)
    exact = functools.partial(lax.dot_general, precision=lax.Precision.HIGHEST)
    input_grad = exact(input_grad, place.astype(f32), back)
    vec_grad = jnp.concatenate([exact(vec_grad[:5], place.astype(f32), back), vec_grad[5:]], axis=0)

    qkv_grad = attn_owned[:, : 3 * feat].reshape(width, 3, feat).transpose(1, 0, 2)
    proj_grad = attn_owned[:, 3 * feat :].T
    up_grad = ffn_owned[:, :units]
    down_grad = ffn_owned[:, units:].T
    qkv_new, qkv_first_new, qkv_second_new = adam_step(
        qkv_weight, qkv_grad, qkv_first, qkv_second, rate_qkv
    )
    proj_new, proj_first_new, proj_second_new = adam_step(
        proj_weight, proj_grad, proj_first, proj_second, rate_proj
    )
    up_new, up_first_new, up_second_new = adam_step(up_weight, up_grad, up_first, up_second, rate_up)
    down_new, down_first_new, down_second_new = adam_step(
        down_weight, down_grad, down_first, down_second, rate_down
    )
    vec_new, vec_first_new, vec_second_new = adam_step(
        vec_params, vec_grad, vec_first, vec_second, rate_vector
    )
    return (
        layer_output.reshape(slots, BLOCK, D),
        input_grad.reshape(slots, BLOCK, D),
        qkv_new,
        qkv_first_new,
        qkv_second_new,
        qkv_new.astype(bf16),
        proj_new,
        proj_first_new,
        proj_second_new,
        proj_new.astype(bf16),
        up_new,
        up_first_new,
        up_second_new,
        up_new.astype(bf16),
        down_new,
        down_first_new,
        down_second_new,
        down_new.astype(bf16),
        vec_new,
        vec_first_new,
        vec_second_new,
    )


def solution(mesh):
    rows_by_seq = P(None, "seq", None)
    cols = P("head", "seq")
    ups = P("seq", "head")
    qkvs = P(None, "seq", "head")
    placed = (
        (rows_by_seq, rows_by_seq, P(None, "seq", "head", None), P(), P(), P())
        + (qkvs,) * 3
        + (cols,) * 3
        + (ups,) * 3
        + (cols,) * 3
        + (P(),) * 3
    )
    return jax.shard_map(
        body,
        mesh=mesh,
        in_specs=placed,
        out_specs=(rows_by_seq, rows_by_seq)
        + (qkvs,) * 4
        + (cols,) * 4
        + (ups,) * 4
        + (cols,) * 4
        + (P(),) * 3,
        check_vma=False,
    )
```

```python
import functools

import jax
import jax.numpy as jnp
from jax import lax
from jax.experimental import pallas as pl
from jax.experimental.pallas import tpu as pltpu
from jax.sharding import PartitionSpec as P

D = 1024
DH = 64
FF = 4096
BLOCK = 64
STEP = 10
LISTED = 8

eps_norm = 1e-05
masked_score = -1e30
beta_one = 0.9
beta_two = 0.999
eps_adam = 1e-08
decay_rate = 0.01
rate_qkv = 0.1
rate_proj = 1.0
rate_up = 0.1
rate_down = 0.05
rate_vector = 2.0

bf16 = jnp.bfloat16
f32 = jnp.float32


def lookup(index_table, index_rows):
    matches = index_rows[..., None] == jnp.arange(index_table.shape[0], dtype=jnp.int32)
    return jnp.sum(jnp.where(matches, index_table, 0), axis=-1)


def owning_doc(doc_end, block_ids):
    return jnp.sum((block_ids[..., None] >= doc_end).astype(jnp.int32), axis=-1)


def dot(lhs, rhs, lhs_dim, rhs_dim):
    return lax.dot_general(
        lhs, rhs, (((lhs_dim,), (rhs_dim,)), ((), ())), preferred_element_type=f32
    )


def norm_rows(token_rows, gain_row, bias_row):
    row_mean = jnp.mean(token_rows, axis=-1, keepdims=True)
    centred = token_rows - row_mean
    row_var = jnp.mean(centred * centred, axis=-1, keepdims=True)
    inv_scale = lax.rsqrt(row_var + eps_norm)
    unit_rows = centred * inv_scale
    return (unit_rows * gain_row + bias_row, unit_rows, inv_scale)


def norm_back(grad_in, unit_rows, inv_scale, gain_row):
    scaled = grad_in * gain_row
    first_mean = jnp.mean(scaled, axis=-1, keepdims=True)
    second_mean = jnp.mean(scaled * unit_rows, axis=-1, keepdims=True)
    return inv_scale * (scaled - first_mean - unit_rows * second_mean)


def gelu_tanh(values):
    return jax.nn.gelu(values, approximate=True)


def adam_step(param_old, gradient, first_old, second_old, step_rate):
    first_new = beta_one * first_old + (1.0 - beta_one) * gradient
    second_new = beta_two * second_old + (1.0 - beta_two) * gradient * gradient
    first_hat = first_new / (1.0 - beta_one**STEP)
    second_hat = second_new / (1.0 - beta_two**STEP)
    updated = param_old - step_rate * (
        first_hat / (jnp.sqrt(second_hat) + eps_adam) + decay_rate * param_old
    )
    return (updated, first_new, second_new)


def xor_permute(value, axis, mask):
    count = lax.axis_size(axis)
    return lax.ppermute(value, axis, [(i, i ^ mask) for i in range(count)])


def head_sum(partial_low):
    count = lax.axis_size("head")
    if count & (count - 1):
        return lax.psum(partial_low.astype(f32), "head")
    total = partial_low
    step = 1
    while step < count:
        other = xor_permute(total.astype(bf16), "head", step)
        total = total.astype(f32) + other.astype(f32)
        step *= 2
    return total.astype(f32)


def seq_sum(value):
    step = 1
    while step < lax.axis_size("seq"):
        value = value + xor_permute(value, "seq", step)
        step *= 2
    return value


def lane_cuts(lanes):
    chips = lanes // 2
    ys = 1 << ((chips.bit_length() - 1) // 2)
    return 2, ys, chips // ys


def relative_lanes(lanes):
    cores, ys, zs = lane_cuts(lanes)
    return [(kz * ys + ky) * cores + kc for kc in range(cores) for ky in range(ys) for kz in range(zs)]


def relative_gather(mine):
    cores, ys, zs = lane_cuts(lax.axis_size("seq"))
    column = [mine] + [xor_permute(mine, "seq", kz * ys * cores) for kz in range(1, zs)]
    pieces = list(column)
    for ky in range(1, ys):
        pieces += [xor_permute(piece, "seq", ky * cores) for piece in column]
    near = jnp.concatenate(pieces, axis=0)
    return near, xor_permute(near, "seq", 1)


def relative_scatter(near, far):
    cores, ys, zs = lane_cuts(lax.axis_size("seq"))
    total = near + xor_permute(far, "seq", 1).astype(f32)
    for shift, count in ((cores, ys), (ys * cores, zs)):
        size = total.shape[0] // count
        kept = total[:size]
        sent = total[size:].astype(bf16)
        for k in range(1, count):
            kept = kept + xor_permute(sent[(k - 1) * size : k * size], "seq", k * shift).astype(f32)
        total = kept
    return total


def attend_kernel(off_ref, q_ref, kv_ref, bias_ref, ctx_ref, prob_ref):
    lanes, rows = q_ref.shape[0], q_ref.shape[1]
    left = lax.broadcasted_iota(jnp.int32, (rows, 2 * DH), 1) < DH
    scale = DH**-0.5

    def step(i, carry):
        q_pair = q_ref[i].astype(f32) * scale
        outs = []
        for half in range(2):
            q_one = q_pair if half == 0 else pltpu.roll(q_pair, DH, 1)
            q_one = jnp.where(left, q_one, 0.0).astype(bf16)
            listed = jnp.concatenate(
                [
                    kv_ref[pl.ds(pl.multiple_of(off_ref[2 * i + half, j], BLOCK), BLOCK), :]
                    for j in range(LISTED)
                ],
                axis=0,
            )
            scores = dot(q_one, listed, 1, 1) + bias_ref[i, half : half + 1, :]
            row_max = jnp.max(scores, axis=1, keepdims=True)
            grown = jnp.exp(scores - row_max)
            total = jnp.sum(grown, axis=1, keepdims=True)
            probs = (grown * (1.0 / total)).astype(bf16)
            prob_ref[i, half] = probs
            outs.append(dot(probs, listed, 1, 0))
        ctx_ref[i] = jnp.where(left, pltpu.roll(outs[0], DH, 1), outs[1]).astype(bf16)
        return carry

    lax.fori_loop(0, lanes, step, 0)


def attend_back_kernel(off_ref, q_ref, kv_ref, prob_ref, dctx_ref, dq_ref, dkv_ref):
    lanes, rows = q_ref.shape[0], q_ref.shape[1]
    left = lax.broadcasted_iota(jnp.int32, (rows, 2 * DH), 1) < DH
    scale = DH**-0.5
    dkv_ref[...] = jnp.zeros_like(dkv_ref)

    def step(i, carry):
        q_pair = q_ref[i].astype(f32) * scale
        d_pair = dctx_ref[i].astype(f32)
        outs = []
        for half in range(2):
            q_one = q_pair if half == 0 else pltpu.roll(q_pair, DH, 1)
            q_one = jnp.where(left, q_one, 0.0).astype(bf16)
            d_one = pltpu.roll(d_pair, DH, 1) if half == 0 else d_pair
            d_one = jnp.where(left, 0.0, d_one).astype(bf16)
            offs = [
                pl.multiple_of(off_ref[2 * i + half, j], BLOCK) for j in range(LISTED)
            ]
            listed = jnp.concatenate([kv_ref[pl.ds(o, BLOCK), :] for o in offs], axis=0)
            probs_low = prob_ref[i, half]
            probs = probs_low.astype(f32)
            prob_grad = dot(d_one, listed, 1, 1)
            weighted = probs * prob_grad
            row_dot = jnp.sum(weighted, axis=1, keepdims=True)
            score_low = (weighted - probs * row_dot).astype(bf16)
            outs.append(dot(score_low, listed, 1, 0) * scale)
            both = jnp.concatenate([score_low, probs_low], axis=0)
            mates = jnp.concatenate([q_one, d_one], axis=0)
            kv_grad = dot(both, mates, 0, 0)
            for j in range(LISTED):
                at = pl.ds(offs[j], BLOCK)
                dkv_ref[at, :] += kv_grad[j * BLOCK : (j + 1) * BLOCK]
        dq_ref[i] = jnp.where(left, outs[0], pltpu.roll(outs[1], DH, 1)).astype(bf16)
        return carry

    lax.fori_loop(0, lanes, step, 0)


VMEM_LIMIT = 48 * 1024 * 1024


def in_vmem():
    return pl.BlockSpec(memory_space=pltpu.VMEM)


def in_smem():
    return pl.BlockSpec(memory_space=pltpu.SMEM)


def attend(offsets, q_pairs, kv_rows, bias):
    lanes, rows, width = q_pairs.shape
    return pl.pallas_call(
        attend_kernel,
        out_shape=(
            jax.ShapeDtypeStruct((lanes, rows, width), bf16),
            jax.ShapeDtypeStruct((lanes, 2, rows, LISTED * BLOCK), bf16),
        ),
        in_specs=[in_smem(), in_vmem(), in_vmem(), in_vmem()],
        out_specs=(in_vmem(), in_vmem()),
        compiler_params=pltpu.CompilerParams(vmem_limit_bytes=VMEM_LIMIT),
    )(offsets, q_pairs, kv_rows, bias)


def attend_back(offsets, q_pairs, kv_rows, probs, dctx_pairs):
    lanes, rows, width = q_pairs.shape
    return pl.pallas_call(
        attend_back_kernel,
        out_shape=(
            jax.ShapeDtypeStruct((lanes, rows, width), bf16),
            jax.ShapeDtypeStruct(kv_rows.shape, f32),
        ),
        in_specs=[in_smem(), in_vmem(), in_vmem(), in_vmem(), in_vmem()],
        out_specs=(in_vmem(), in_vmem()),
        compiler_params=pltpu.CompilerParams(vmem_limit_bytes=VMEM_LIMIT),
    )(offsets, q_pairs, kv_rows, probs, dctx_pairs)


def body(
    layer_input,
    output_grad,
    random_pick,
    doc_blocks,
    last_fill,
    shard_owner,
    qkv_weight,
    qkv_first,
    qkv_second,
    proj_weight,
    proj_first,
    proj_second,
    up_weight,
    up_first,
    up_second,
    down_weight,
    down_first,
    down_second,
    vec_params,
    vec_first,
    vec_second,
):
    lanes = lax.axis_size("seq")
    lane_index = lax.axis_index("seq")
    head_groups = lax.axis_size("head")
    head_index = lax.axis_index("head")
    slots = layer_input.shape[0]
    heads = random_pick.shape[2]
    feat = heads * DH
    units = up_weight.shape[1]
    rows = slots * BLOCK
    block_total = slots * lanes
    share = lanes // heads
    part_rows = rows // share
    pair_rows = part_rows // 2
    my_part = lane_index % share
    width = D // lanes

    picks = random_pick[:, 0].transpose(1, 0, 2).reshape(heads, slots * 3)
    picks = jnp.broadcast_to(picks[:, None], (heads, share, slots * 3)).reshape(lanes, slots * 3)
    picks = lax.all_to_all(picks, "seq", 0, 0, tiled=True).reshape(lanes, slots, 3)

    doc_end = jnp.cumsum(doc_blocks)
    doc_start = doc_end - doc_blocks
    doc_length = (doc_blocks - 1) * BLOCK + last_fill
    half_slot = (my_part * part_rows + jnp.arange(2, dtype=jnp.int32) * pair_rows) // BLOCK
    query_ids = half_slot[None, :] * lanes + jnp.arange(lanes, dtype=jnp.int32)[:, None]
    pick_half = jnp.sum(
        jnp.where(
            (half_slot[:, None] == jnp.arange(slots, dtype=jnp.int32)[None, :])[None, :, :, None],
            picks[:, None],
            0,
        ),
        axis=2,
    )
    query_doc = owning_doc(doc_end, query_ids)
    doc_first = lookup(doc_start, query_doc)
    doc_count = lookup(doc_blocks, query_doc)
    query_length = lookup(doc_length, query_doc)
    key_ids = jnp.concatenate(
        [
            jnp.stack(
                [
                    (query_ids - 1) % block_total,
                    query_ids,
                    (query_ids + 1) % block_total,
                    doc_first,
                    (doc_first + 1) % block_total,
                ],
                axis=-1,
            ),
            doc_first[..., None] + pick_half % doc_count[..., None],
        ],
        axis=-1,
    )
    same_doc = owning_doc(doc_end, key_ids) == query_doc[..., None]
    live_count = jnp.where(
        same_doc, query_length[..., None] - (key_ids - doc_first[..., None]) * BLOCK, 0
    )
    token = jnp.arange(BLOCK, dtype=jnp.int32)
    bias = jnp.where(token < live_count[..., None], 0.0, masked_score).astype(f32)
    bias = bias.reshape(lanes, 2, LISTED * BLOCK)
    key_lane = key_ids % lanes
    key_slot = key_ids // lanes
    if part_rows >= BLOCK:
        part_slots = part_rows // BLOCK
        offsets = ((key_slot // part_slots) * lanes + key_lane) * part_rows + (
            key_slot % part_slots
        ) * BLOCK
    else:
        offsets = (key_lane * slots + key_slot) * BLOCK
    offsets = offsets.reshape(lanes * 2, LISTED)

    qkv_mine = qkv_weight.astype(bf16).transpose(1, 0, 2).reshape(width, 3 * feat)
    qkv_near, qkv_far = relative_gather(qkv_mine)
    rest_mine = jnp.concatenate(
        [proj_weight.astype(bf16).T, up_weight.astype(bf16), down_weight.astype(bf16).T], axis=1
    )
    rest_mine, picks = lax.optimization_barrier((rest_mine, picks))
    rest_full = lax.all_gather(rest_mine, "seq", axis=0, tiled=True)
    proj_full = rest_full[:, :feat]
    up_full = rest_full[:, feat : feat + units]
    down_full = rest_full[:, feat + units :]

    column = jnp.arange(D, dtype=jnp.int32)
    owner = lookup(shard_owner, column // width)
    masks = jnp.array(relative_lanes(lanes), jnp.int32)
    position = jnp.sum(
        jnp.where(
            masks[None, :] == (owner ^ lane_index)[:, None], jnp.arange(lanes, dtype=jnp.int32), 0
        ),
        axis=1,
    )
    place = (owner * width + column % width)[:, None] == column[None, :]
    place_near = (position * width + column % width)[:, None] == column[None, :]
    place, place_near = place.astype(bf16), place_near.astype(bf16)
    rows_in = layer_input.reshape(rows, D)
    token_rows = dot(rows_in, place, 1, 0)
    grad_low = dot(output_grad.reshape(rows, D), place, 1, 0).astype(bf16)
    grad_rows = grad_low.astype(f32)
    exact = functools.partial(
        lax.dot_general, precision=lax.Precision.HIGHEST, preferred_element_type=f32
    )
    ahead = (((1,), (0,)), ((), ()))
    back = (((1,), (1,)), ((), ()))
    vec_rows = exact(vec_params[:5], place.astype(f32), ahead)
    vec_near = exact(vec_params[:2], place_near.astype(f32), ahead)
    up_bias = lax.dynamic_slice_in_dim(vec_params[5:].reshape(FF), head_index * units, units)

    normed_one, unit_one, scale_one = norm_rows(
        dot(rows_in, place_near, 1, 0), vec_near[0], vec_near[1]
    )
    low_one = normed_one.astype(bf16)
    half = D // 2
    qkv_rows = (dot(low_one[:, :half], qkv_near, 1, 0) + dot(low_one[:, half:], qkv_far, 1, 0)).astype(bf16)
    by_head = qkv_rows.reshape(rows, 3, heads, DH)
    kv_send = by_head[:, 1:].transpose(2, 0, 1, 3).reshape(lanes, part_rows, 2 * DH)
    q_send = (
        by_head[:, 0]
        .reshape(share, 2, pair_rows, heads, DH)
        .transpose(3, 0, 2, 1, 4)
        .reshape(lanes, pair_rows, 2 * DH)
    )
    received = lax.all_to_all(
        jnp.concatenate([kv_send, q_send], axis=1), "seq", 0, 0, tiled=True
    )
    q_pairs = received[:, part_rows:]
    kv_parts = received[:, :part_rows][None]
    step = 1
    while step < share:
        other = xor_permute(kv_parts, "seq", step)
        high = (my_part & step) != 0
        kv_parts = jnp.where(
            high,
            jnp.concatenate([other, kv_parts], axis=0),
            jnp.concatenate([kv_parts, other], axis=0),
        )
        step *= 2
    if part_rows >= BLOCK:
        kv_rows = kv_parts.reshape(block_total * BLOCK, 2 * DH)
    else:
        kv_rows = kv_parts.transpose(1, 0, 2, 3).reshape(block_total * BLOCK, 2 * DH)
    ctx_pairs, probs = attend(offsets, q_pairs, kv_rows, bias)

    def pairs_to_rows(pairs):
        return (
            pairs.reshape(heads, share, pair_rows, 2, DH)
            .transpose(1, 3, 2, 0, 4)
            .reshape(rows, feat)
        )

    def rows_to_pairs(low_rows):
        return (
            low_rows.reshape(share, 2, pair_rows, heads, DH)
            .transpose(3, 0, 2, 1, 4)
            .reshape(lanes, pair_rows, 2 * DH)
        )

    context = pairs_to_rows(lax.all_to_all(ctx_pairs, "seq", 0, 0, tiled=True))
    attn_sum = head_sum(dot(context, proj_full, 1, 1).astype(bf16))
    mid_rows = token_rows + attn_sum
    normed_two, unit_two, scale_two = norm_rows(mid_rows, vec_rows[2], vec_rows[3])
    low_two = normed_two.astype(bf16)
    hidden = dot(low_two, up_full, 1, 0) + up_bias
    active = gelu_tanh(hidden).astype(bf16)
    act_grad = dot(grad_low, down_full, 1, 0)
    hidden_grad = jax.vjp(gelu_tanh, hidden)[1](act_grad)[0]
    hidden_low = hidden_grad.astype(bf16)
    two_grad = head_sum(dot(hidden_low, up_full, 1, 1).astype(bf16))
    ffn_sum = head_sum(dot(active, down_full, 1, 1).astype(bf16))
    result = (mid_rows + ffn_sum + vec_rows[4]).astype(bf16)
    up_bias_grad = jnp.sum(hidden_grad, axis=0)
    ffn_grads = jnp.concatenate(
        [dot(low_two, hidden_low, 0, 0).astype(bf16), dot(grad_low, active, 0, 0).astype(bf16)],
        axis=1,
    )

    mid_grad = grad_rows + norm_back(two_grad, unit_two, scale_two, vec_rows[2])
    attn_low = mid_grad.astype(bf16)
    ctx_grad = dot(attn_low, proj_full, 1, 0).astype(bf16)
    ffn_grads, ctx_grad = lax.optimization_barrier((ffn_grads, ctx_grad))
    ffn_owned = lax.psum_scatter(ffn_grads, "seq", scatter_dimension=0, tiled=True).astype(f32)
    attn_near = dot(attn_low, dot(place, place_near, 0, 0).astype(bf16), 1, 0).astype(bf16)
    proj_owned = relative_scatter(
        dot(attn_near[:, :half], context, 0, 0), dot(attn_near[:, half:], context, 0, 0).astype(bf16)
    )
    dctx_pairs = lax.all_to_all(rows_to_pairs(ctx_grad), "seq", 0, 0, tiled=True)
    dq_pairs, dkv_rows = attend_back(offsets, q_pairs, kv_rows, probs, dctx_pairs)
    if part_rows >= BLOCK:
        dkv_parts = dkv_rows.reshape(share, lanes, part_rows, 2 * DH)
    else:
        dkv_parts = dkv_rows.reshape(lanes, share, part_rows, 2 * DH).transpose(1, 0, 2, 3)
    step = share // 2
    while step >= 1:
        high = (my_part & step) != 0
        first, second = dkv_parts[:step], dkv_parts[step:]
        away = jnp.where(high, first, second).astype(bf16)
        stay = jnp.where(high, second, first)
        dkv_parts = stay + xor_permute(away, "seq", step).astype(f32)
        step //= 2
    returned = lax.all_to_all(
        jnp.concatenate([dkv_parts[0].astype(bf16), dq_pairs], axis=1),
        "seq",
        0,
        0,
        tiled=True,
    )
    dkv_back = (
        returned[:, :part_rows]
        .reshape(heads, rows, 2, DH)
        .transpose(1, 2, 0, 3)
        .reshape(rows, 2 * feat)
    )
    dqkv = jnp.concatenate([pairs_to_rows(returned[:, part_rows:]), dkv_back], axis=1)
    one_part = jnp.concatenate([dot(dqkv, qkv_near, 1, 1), dot(dqkv, qkv_far, 1, 1)], axis=1)
    one_grad = head_sum(one_part.astype(bf16))
    qkv_owned = []
    for cols in (dqkv[:, : 3 * feat // 2], dqkv[:, 3 * feat // 2 :]):
        far = dot(low_one[:, half:], cols, 0, 0).astype(bf16)
        qkv_owned.append(relative_scatter(dot(low_one[:, :half], cols, 0, 0), far))
    qkv_owned = jnp.concatenate(qkv_owned, axis=1)

    layer_output = lax.dot_general(result, place, back, preferred_element_type=f32).astype(bf16)
    input_grad = exact(mid_grad, place.astype(f32), back) + exact(
        norm_back(one_grad, unit_one, scale_one, vec_near[0]), place_near.astype(f32), back
    )
    early_rows = jnp.stack(
        [jnp.sum(two_grad * unit_two, axis=0), jnp.sum(two_grad, axis=0), jnp.sum(grad_rows, axis=0)]
    )
    early_rows = exact(early_rows, place.astype(f32), back)
    early_rows = seq_sum(jnp.concatenate([early_rows, up_bias_grad.reshape(units // D, D)], axis=0))
    late_rows = jnp.stack([jnp.sum(one_grad * unit_one, axis=0), jnp.sum(one_grad, axis=0)])
    late_rows = seq_sum(exact(late_rows, place_near.astype(f32), back))
    bias_rows = early_rows[3:]
    step = 1
    while step < head_groups:
        other = xor_permute(bias_rows, "head", step)
        high = (head_index & step) != 0
        bias_rows = jnp.where(
            high,
            jnp.concatenate([other, bias_rows], axis=0),
            jnp.concatenate([bias_rows, other], axis=0),
        )
        step *= 2
    vec_grad = jnp.concatenate([late_rows, early_rows[:3], bias_rows], axis=0)

    qkv_grad = qkv_owned.reshape(width, 3, feat).transpose(1, 0, 2)
    proj_grad = proj_owned.T
    up_grad = ffn_owned[:, :units]
    down_grad = ffn_owned[:, units:].T
    qkv_new, qkv_first_new, qkv_second_new = adam_step(
        qkv_weight, qkv_grad, qkv_first, qkv_second, rate_qkv
    )
    proj_new, proj_first_new, proj_second_new = adam_step(
        proj_weight, proj_grad, proj_first, proj_second, rate_proj
    )
    up_new, up_first_new, up_second_new = adam_step(up_weight, up_grad, up_first, up_second, rate_up)
    down_new, down_first_new, down_second_new = adam_step(
        down_weight, down_grad, down_first, down_second, rate_down
    )
    vec_new, vec_first_new, vec_second_new = adam_step(
        vec_params, vec_grad, vec_first, vec_second, rate_vector
    )
    return (
        layer_output.reshape(slots, BLOCK, D),
        input_grad.reshape(slots, BLOCK, D),
        qkv_new,
        qkv_first_new,
        qkv_second_new,
        qkv_new.astype(bf16),
        proj_new,
        proj_first_new,
        proj_second_new,
        proj_new.astype(bf16),
        up_new,
        up_first_new,
        up_second_new,
        up_new.astype(bf16),
        down_new,
        down_first_new,
        down_second_new,
        down_new.astype(bf16),
        vec_new,
        vec_first_new,
        vec_second_new,
    )


def solution(mesh):
    rows_by_seq = P(None, "seq", None)
    cols = P("head", "seq")
    ups = P("seq", "head")
    qkvs = P(None, "seq", "head")
    placed = (
        (rows_by_seq, rows_by_seq, P(None, "seq", "head", None), P(), P(), P())
        + (qkvs,) * 3
        + (cols,) * 3
        + (ups,) * 3
        + (cols,) * 3
        + (P(),) * 3
    )
    return jax.shard_map(
        body,
        mesh=mesh,
        in_specs=placed,
        out_specs=(rows_by_seq, rows_by_seq)
        + (qkvs,) * 4
        + (cols,) * 4
        + (ups,) * 4
        + (cols,) * 4
        + (P(),) * 3,
        check_vma=False,
    )
```

```python
import functools

import jax
import jax.numpy as jnp
from jax import lax
from jax.experimental import pallas as pl
from jax.experimental.pallas import tpu as pltpu
from jax.sharding import PartitionSpec as P

D = 1024
DH = 64
FF = 4096
BLOCK = 64
STEP = 10
LISTED = 8

eps_norm = 1e-05
masked_score = -1e30
beta_one = 0.9
beta_two = 0.999
eps_adam = 1e-08
decay_rate = 0.01
rate_qkv = 0.1
rate_proj = 1.0
rate_up = 0.1
rate_down = 0.05
rate_vector = 2.0

bf16 = jnp.bfloat16
f32 = jnp.float32


def lookup(index_table, index_rows):
    matches = index_rows[..., None] == jnp.arange(index_table.shape[0], dtype=jnp.int32)
    return jnp.sum(jnp.where(matches, index_table, 0), axis=-1)


def owning_doc(doc_end, block_ids):
    return jnp.sum((block_ids[..., None] >= doc_end).astype(jnp.int32), axis=-1)


def dot(lhs, rhs, lhs_dim, rhs_dim):
    return lax.dot_general(
        lhs, rhs, (((lhs_dim,), (rhs_dim,)), ((), ())), preferred_element_type=f32
    )


def norm_rows(token_rows, gain_row, bias_row):
    row_mean = jnp.mean(token_rows, axis=-1, keepdims=True)
    centred = token_rows - row_mean
    row_var = jnp.mean(centred * centred, axis=-1, keepdims=True)
    inv_scale = lax.rsqrt(row_var + eps_norm)
    unit_rows = centred * inv_scale
    return (unit_rows * gain_row + bias_row, unit_rows, inv_scale)


def norm_back(grad_in, unit_rows, inv_scale, gain_row):
    scaled = grad_in * gain_row
    first_mean = jnp.mean(scaled, axis=-1, keepdims=True)
    second_mean = jnp.mean(scaled * unit_rows, axis=-1, keepdims=True)
    return inv_scale * (scaled - first_mean - unit_rows * second_mean)


def gelu_tanh(values):
    return jax.nn.gelu(values, approximate=True)


def adam_step(param_old, gradient, first_old, second_old, step_rate):
    first_new = beta_one * first_old + (1.0 - beta_one) * gradient
    second_new = beta_two * second_old + (1.0 - beta_two) * gradient * gradient
    first_hat = first_new / (1.0 - beta_one**STEP)
    second_hat = second_new / (1.0 - beta_two**STEP)
    updated = param_old - step_rate * (
        first_hat / (jnp.sqrt(second_hat) + eps_adam) + decay_rate * param_old
    )
    return (updated, first_new, second_new)


def xor_permute(value, axis, mask):
    count = lax.axis_size(axis)
    return lax.ppermute(value, axis, [(i, i ^ mask) for i in range(count)])


def head_other(partial_low):
    return xor_permute(partial_low, "head", 1)


def head_total(partial_low, other):
    total = partial_low.astype(f32) + other.astype(f32)
    step = 2
    while step < lax.axis_size("head"):
        total = total + xor_permute(total, "head", step)
        step *= 2
    return total


def axis_sum(value, axis):
    step = 1
    while step < lax.axis_size(axis):
        value = value + xor_permute(value, axis, step)
        step *= 2
    return value


def lane_cuts(lanes):
    chips = lanes // 2
    ys = 1 << ((chips.bit_length() - 1) // 2)
    return 2, ys, chips // ys


def relative_lanes(lanes):
    cores, ys, zs = lane_cuts(lanes)
    return [(kz * ys + ky) * cores + kc for kc in range(cores) for ky in range(ys) for kz in range(zs)]


def relative_gather(mine):
    cores, ys, zs = lane_cuts(lax.axis_size("seq"))
    column = [mine] + [xor_permute(mine, "seq", kz * ys * cores) for kz in range(1, zs)]
    pieces = list(column)
    for ky in range(1, ys):
        pieces += [xor_permute(piece, "seq", ky * cores) for piece in column]
    near = jnp.concatenate(pieces, axis=0)
    return near, xor_permute(near, "seq", 1)


GROUP = 4


def fill_rows(source_refs, kv_ref):
    start = 0
    for source_ref in source_refs:
        count = source_ref.shape[0]
        size = kv_ref.shape[0] // (count * len(source_refs))

        def copy(i, carry, start=start, size=size, source_ref=source_ref):
            at = pl.ds(pl.multiple_of(start + i * size, size), size)
            kv_ref[at, :] = source_ref[i, :size, :]
            return carry

        lax.fori_loop(0, count, copy, 0)
        start += count * size


def attend_kernel(off_ref, record_ref, *refs):
    *source_refs, bias_ref, ctx_ref, prob_ref, kv_ref = refs
    lanes, rows = ctx_ref.shape[0], ctx_ref.shape[1]
    first = record_ref.shape[1] - rows
    left = lax.broadcasted_iota(jnp.int32, (rows, 2 * DH), 1) < DH
    scale = DH**-0.5
    fill_rows(source_refs, kv_ref)

    def step(t, carry):
        units = [(t * GROUP + g, half) for g in range(GROUP) for half in range(2)]
        listed, scores = [], []
        for i, half in units:
            q_pair = record_ref[i, first:, :].astype(f32) * scale
            q_one = q_pair if half == 0 else pltpu.roll(q_pair, DH, 1)
            q_one = jnp.where(left, q_one, 0.0).astype(bf16)
            rows_here = jnp.concatenate(
                [
                    kv_ref[pl.ds(pl.multiple_of(off_ref[2 * i + half, j], BLOCK), BLOCK), :]
                    for j in range(LISTED)
                ],
                axis=0,
            )
            listed.append(rows_here)
            scores.append(dot(q_one, rows_here, 1, 1) + bias_ref[i, half : half + 1, :])
        tops = [jnp.max(score, axis=1, keepdims=True) for score in scores]
        grown = [jnp.exp(score - top) for score, top in zip(scores, tops)]
        totals = [jnp.sum(part, axis=1, keepdims=True) for part in grown]
        probs = [(part * (1.0 / total)).astype(bf16) for part, total in zip(grown, totals)]
        outs = []
        for (i, half), prob, rows_here in zip(units, probs, listed):
            prob_ref[i, half] = prob
            outs.append(dot(prob, rows_here, 1, 0))
        for g in range(GROUP):
            ctx_ref[t * GROUP + g] = jnp.where(
                left, pltpu.roll(outs[2 * g], DH, 1), outs[2 * g + 1]
            ).astype(bf16)
        return carry

    lax.fori_loop(0, lanes // GROUP, step, 0)


def attend_back_kernel(off_ref, record_ref, *refs):
    *source_refs, prob_ref, dctx_ref, dq_ref, own_ref, away_ref, kv_ref, dkv_ref = refs
    lanes, rows = dq_ref.shape[0], dq_ref.shape[1]
    first = record_ref.shape[1] - rows
    left = lax.broadcasted_iota(jnp.int32, (rows, 2 * DH), 1) < DH
    scale = DH**-0.5
    fill_rows(source_refs, kv_ref)
    dkv_ref[...] = jnp.zeros_like(dkv_ref)

    def step(t, carry):
        units = [(t * GROUP + g, half) for g in range(GROUP) for half in range(2)]
        queries, grads, offs, listed, prob_grads = [], [], [], [], []
        for i, half in units:
            q_pair = record_ref[i, first:, :].astype(f32) * scale
            d_pair = dctx_ref[i].astype(f32)
            q_one = q_pair if half == 0 else pltpu.roll(q_pair, DH, 1)
            queries.append(jnp.where(left, q_one, 0.0).astype(bf16))
            d_one = pltpu.roll(d_pair, DH, 1) if half == 0 else d_pair
            grads.append(jnp.where(left, 0.0, d_one).astype(bf16))
            offs.append(
                [pl.multiple_of(off_ref[2 * i + half, j], BLOCK) for j in range(LISTED)]
            )
            listed.append(
                jnp.concatenate([kv_ref[pl.ds(o, BLOCK), :] for o in offs[-1]], axis=0)
            )
            prob_grads.append(dot(grads[-1], listed[-1], 1, 1))
        probs_low = [prob_ref[i, half] for i, half in units]
        probs = [prob.astype(f32) for prob in probs_low]
        weighted = [prob * grad for prob, grad in zip(probs, prob_grads)]
        row_dots = [jnp.sum(part, axis=1, keepdims=True) for part in weighted]
        scores_low = [
            (part - prob * row_dot).astype(bf16)
            for part, prob, row_dot in zip(weighted, probs, row_dots)
        ]
        outs = [dot(score, rows_here, 1, 0) * scale for score, rows_here in zip(scores_low, listed)]
        for n in range(len(units)):
            both = jnp.concatenate([scores_low[n], probs_low[n]], axis=0)
            mates = jnp.concatenate([queries[n], grads[n]], axis=0)
            kv_grad = dot(both, mates, 0, 0)
            for j in range(LISTED):
                at = pl.ds(offs[n][j], BLOCK)
                dkv_ref[at, :] += kv_grad[j * BLOCK : (j + 1) * BLOCK]
        for g in range(GROUP):
            dq_ref[t * GROUP + g] = jnp.where(
                left, outs[2 * g], pltpu.roll(outs[2 * g + 1], DH, 1)
            ).astype(bf16)
        return carry

    lax.fori_loop(0, lanes // GROUP, step, 0)
    held = own_ref.shape[0]
    own_ref[...] = dkv_ref[:held, :]
    away_ref[...] = dkv_ref[held:, :].astype(bf16)


def message_kernel(own_ref, other_ref, dq_ref, mixed_ref, msg_ref):
    lanes, record = msg_ref.shape[0], msg_ref.shape[1]
    part_rows = 2 * record // 3
    pair_rows = part_rows // 2
    left = lax.broadcasted_iota(jnp.int32, (pair_rows, 2 * DH), 1) < DH

    def step(i, carry):
        row = pl.multiple_of(i * part_rows, part_rows)
        at = pl.ds(row, part_rows)
        total = own_ref[at, :]
        for k in range(other_ref.shape[0]):
            total += other_ref[k, at, :].astype(f32)
        low = total.astype(bf16)
        mixed_ref[at, : 2 * DH] = low
        msg_ref[i, :part_rows, :] = low
        dq = dq_ref[i]
        msg_ref[i, part_rows:, :] = dq
        dq = dq.astype(f32)
        second = pltpu.roll(dq, DH, 1)
        mixed_ref[pl.ds(row, pair_rows), 2 * DH :] = jnp.where(left, dq, 0.0).astype(bf16)
        mixed_ref[
            pl.ds(pl.multiple_of(row + pair_rows, pair_rows), pair_rows), 2 * DH :
        ] = jnp.where(left, second, 0.0).astype(bf16)
        return carry

    lax.fori_loop(0, lanes, step, 0)


def head_grad_kernel(head_ref, mixed_ref, *refs):
    *part_refs, out_ref = refs
    count = len(part_refs) // 2
    cut, size = part_refs[0].shape
    for k in range(count):
        row = pl.multiple_of((head_ref[0] ^ k) * size, size)
        total = dot(part_refs[k][...], mixed_ref[:cut, :], 0, 0)
        total += dot(part_refs[count + k][...], mixed_ref[cut:, :], 0, 0)
        out_ref[pl.ds(row, size), :] = total.astype(bf16)


def pack_kernel(share, low_ref, near_ref, far_ref, msg_ref, rows_ref):
    lanes, record = msg_ref.shape[0], msg_ref.shape[1]
    heads = lanes // share
    feat = heads * DH
    part_rows = 2 * record // 3
    pair_rows = part_rows // 2
    half = D // 2
    for c in range(3):
        cols = slice(c * feat, (c + 1) * feat)
        rows_ref[:, cols] = dot(low_ref[:, :half], near_ref[:, cols], 1, 0) + dot(
            low_ref[:, half:], far_ref[:, cols], 1, 0
        )
    left = lax.broadcasted_iota(jnp.int32, (part_rows, 2 * DH), 1) < DH
    for h in range(0, heads, 2):
        for r in range(share):
            at = slice(r * part_rows, (r + 1) * part_rows)
            query, keys, vals = (
                rows_ref[at, c * feat + h * DH : c * feat + (h + 2) * DH] for c in range(3)
            )
            even, odd = h * share + r, (h + 1) * share + r
            msg_ref[even, :part_rows, :] = jnp.where(left, keys, pltpu.roll(vals, DH, 1)).astype(
                bf16
            )
            msg_ref[odd, :part_rows, :] = jnp.where(left, pltpu.roll(keys, DH, 1), vals).astype(
                bf16
            )
            first, second = query[:pair_rows], query[pair_rows:]
            over = left[:pair_rows]
            msg_ref[even, part_rows:, :] = jnp.where(over, first, pltpu.roll(second, DH, 1)).astype(
                bf16
            )
            msg_ref[odd, part_rows:, :] = jnp.where(over, pltpu.roll(first, DH, 1), second).astype(
                bf16
            )


def unpack_pairs(read, heads, share, pair_rows, write):
    left = lax.broadcasted_iota(jnp.int32, (pair_rows, 2 * DH), 1) < DH
    for h in range(0, heads, 2):
        cols = slice(h * DH, (h + 2) * DH)
        for r in range(share):
            even, odd = read(h * share + r), read((h + 1) * share + r)
            base = 2 * r * pair_rows
            first = jnp.where(left, even, pltpu.roll(odd, DH, 1))
            second = jnp.where(left, pltpu.roll(even, DH, 1), odd)
            write(slice(base, base + pair_rows), cols, first)
            write(slice(base + pair_rows, base + 2 * pair_rows), cols, second)


def project_kernel(share, pairs_ref, proj_ref, ctx_ref, out_ref):
    heads, pair_rows = pairs_ref.shape[0] // share, pairs_ref.shape[1]

    def write(rows, cols, value):
        ctx_ref[rows, cols] = value.astype(bf16)

    unpack_pairs(lambda n: pairs_ref[n].astype(f32), heads, share, pair_rows, write)
    out_ref[...] = dot(ctx_ref[...], proj_ref[...], 1, 1).astype(bf16)


def dctx_kernel(share, low_ref, proj_ref, pairs_ref):
    heads, pair_rows = pairs_ref.shape[0] // share, pairs_ref.shape[1]
    left = lax.broadcasted_iota(jnp.int32, (pair_rows, 2 * DH), 1) < DH
    grad = dot(low_ref[...], proj_ref[...], 1, 0)
    for h in range(0, heads, 2):
        cols = slice(h * DH, (h + 2) * DH)
        for r in range(share):
            base = 2 * r * pair_rows
            first = grad[base : base + pair_rows, cols]
            second = grad[base + pair_rows : base + 2 * pair_rows, cols]
            pairs_ref[h * share + r] = jnp.where(left, first, pltpu.roll(second, DH, 1)).astype(
                bf16
            )
            pairs_ref[(h + 1) * share + r] = jnp.where(
                left, pltpu.roll(first, DH, 1), second
            ).astype(bf16)


def one_grad_kernel(share, msg_ref, near_ref, far_ref, unit_ref, place_ref, out_ref, late_ref, rows_ref):
    lanes, record = msg_ref.shape[0], msg_ref.shape[1]
    heads = lanes // share
    feat = heads * DH
    part_rows = 2 * record // 3
    pair_rows = part_rows // 2

    def write(rows, cols, value):
        rows_ref[rows, cols] = value.astype(bf16)

    unpack_pairs(
        lambda n: msg_ref[n, part_rows:, :].astype(f32), heads, share, pair_rows, write
    )
    left = lax.broadcasted_iota(jnp.int32, (part_rows, 2 * DH), 1) < DH
    for h in range(0, heads, 2):
        for r in range(share):
            even = msg_ref[h * share + r, :part_rows, :].astype(f32)
            odd = msg_ref[(h + 1) * share + r, :part_rows, :].astype(f32)
            at = slice(r * part_rows, (r + 1) * part_rows)
            keys = jnp.where(left, even, pltpu.roll(odd, DH, 1))
            vals = jnp.where(left, pltpu.roll(even, DH, 1), odd)
            rows_ref[at, feat + h * DH : feat + (h + 2) * DH] = keys.astype(bf16)
            rows_ref[at, 2 * feat + h * DH : 2 * feat + (h + 2) * DH] = vals.astype(bf16)
    half = D // 2
    out_ref[:, :half] = dot(rows_ref[...], near_ref[...], 1, 1).astype(bf16)
    out_ref[:, half:] = dot(rows_ref[...], far_ref[...], 1, 1).astype(bf16)
    grad = out_ref[...].astype(f32)
    gain = jnp.sum(grad * unit_ref[...], axis=0, keepdims=True)
    shift = jnp.sum(grad, axis=0, keepdims=True)
    sums = jnp.concatenate([gain, shift, jnp.zeros((14, D), f32)], axis=0).astype(bf16)
    late_ref[...] = dot(sums, place_ref[...], 1, 1).astype(bf16)


def weight_grad_kernel(lhs_a, rhs_a, lhs_b, rhs_b, out_ref, *, first):
    at = pl.program_id(0)

    @pl.when(at < first)
    def _():
        out_ref[...] = dot(lhs_a[...], rhs_a[...], 0, 0).astype(bf16)

    @pl.when(at >= first)
    def _():
        out_ref[...] = dot(lhs_b[...], rhs_b[...], 0, 0).astype(bf16)


def last_grad_kernel(lhs, rhs, whole_ref, out_ref):
    out_ref[...] = dot(lhs[...], rhs[...], 0, 0).astype(bf16)


VMEM_LIMIT = 48 * 1024 * 1024


def in_smem():
    return pl.BlockSpec(memory_space=pltpu.SMEM)


def call(kernel, outs, specs, scratch=(), out_specs=None):
    return pl.pallas_call(
        kernel,
        grid=(1,),
        out_shape=outs,
        in_specs=specs,
        out_specs=jax.tree.map(lambda o: whole(o.shape), outs) if out_specs is None else out_specs,
        scratch_shapes=list(scratch),
        compiler_params=pltpu.CompilerParams(vmem_limit_bytes=VMEM_LIMIT),
    )


def whole(shape):
    return pl.BlockSpec(tuple(shape), lambda i: (0,) * len(shape))


def array(shape, dtype=bf16):
    return jax.ShapeDtypeStruct(shape, dtype)


def ffn_weight_grads(first, second, width):
    units = first[1].shape[1]
    block = min(512, units)
    count = units // block
    specs = []
    for start, (lhs, rhs) in enumerate((first, second)):
        specs.append(whole(lhs.shape))
        specs.append(
            pl.BlockSpec(
                (rhs.shape[0], block),
                lambda i, start=start: (0, jnp.clip(i - start * count, 0, count - 1)),
            )
        )
    return pl.pallas_call(
        functools.partial(weight_grad_kernel, first=count),
        grid=(2 * count,),
        out_shape=array((D, width)),
        in_specs=specs,
        out_specs=pl.BlockSpec((D, block), lambda i: (0, i)),
        compiler_params=pltpu.CompilerParams(vmem_limit_bytes=VMEM_LIMIT),
        cost_estimate=pl.CostEstimate(
            flops=8 * D * units * first[1].shape[0], bytes_accessed=4 * D * width, transcendentals=0
        ),
    )(*first, *second)


def last_weight_grad(lhs, rhs, into):
    block = rhs.shape[1]
    return pl.pallas_call(
        last_grad_kernel,
        grid=(1,),
        out_shape=array(into.shape),
        in_specs=[whole(lhs.shape), whole(rhs.shape), pl.BlockSpec(memory_space=pl.ANY)],
        out_specs=pl.BlockSpec((D, block), lambda i: (0, into.shape[1] // block - 1)),
        input_output_aliases={2: 0},
        compiler_params=pltpu.CompilerParams(vmem_limit_bytes=VMEM_LIMIT),
    )(lhs, rhs, into)


def body(
    layer_input,
    output_grad,
    random_pick,
    doc_blocks,
    last_fill,
    shard_owner,
    qkv_weight,
    qkv_first,
    qkv_second,
    proj_weight,
    proj_first,
    proj_second,
    up_weight,
    up_first,
    up_second,
    down_weight,
    down_first,
    down_second,
    vec_params,
    vec_first,
    vec_second,
):
    lanes = lax.axis_size("seq")
    lane_index = lax.axis_index("seq")
    head_groups = lax.axis_size("head")
    head_index = lax.axis_index("head")
    slots = layer_input.shape[0]
    heads = random_pick.shape[2]
    feat = heads * DH
    units = up_weight.shape[1]
    rows = slots * BLOCK
    block_total = slots * lanes
    share = lanes // heads
    part_rows = rows // share
    pair_rows = part_rows // 2
    my_part = lane_index % share
    width = D // lanes

    picks = random_pick[:, 0].transpose(1, 0, 2).reshape(heads, slots * 3)
    picks = jnp.broadcast_to(picks[:, None], (heads, share, slots * 3)).reshape(lanes, slots * 3)
    picks = lax.all_to_all(picks, "seq", 0, 0, tiled=True).reshape(lanes, slots, 3)

    qkv_mine = qkv_weight.astype(bf16).transpose(1, 0, 2).reshape(width, 3 * feat)
    qkv_near, qkv_far = relative_gather(qkv_mine)
    rest_mine = jnp.concatenate(
        [up_weight.astype(bf16), down_weight.astype(bf16).T, proj_weight.astype(bf16).T], axis=1
    )
    rest_full = lax.all_gather(rest_mine, "seq", axis=0, tiled=True)
    up_full = rest_full[:, :units]
    down_full = rest_full[:, units : 2 * units]
    proj_block = pl.BlockSpec((D, feat), lambda i: (0, 2 * units // feat))

    column = jnp.arange(D, dtype=jnp.int32)
    owner = lookup(shard_owner, column // width)
    masks = jnp.array(relative_lanes(lanes), jnp.int32)
    position = jnp.sum(
        jnp.where(
            masks[None, :] == (owner ^ lane_index)[:, None], jnp.arange(lanes, dtype=jnp.int32), 0
        ),
        axis=1,
    )
    place = (owner * width + column % width)[:, None] == column[None, :]
    place_near = (position * width + column % width)[:, None] == column[None, :]
    place, place_near = place.astype(bf16), place_near.astype(bf16)
    rows_in = layer_input.reshape(rows, D)
    token_rows = dot(rows_in, place, 1, 0)
    grad_low = dot(output_grad.reshape(rows, D), place, 1, 0).astype(bf16)
    grad_rows = grad_low.astype(f32)
    exact = functools.partial(
        lax.dot_general, precision=lax.Precision.HIGHEST, preferred_element_type=f32
    )
    ahead = (((1,), (0,)), ((), ()))
    back = (((1,), (1,)), ((), ()))
    vec_rows = exact(vec_params[:5], place.astype(f32), ahead)
    vec_near = exact(vec_params[:2], place_near.astype(f32), ahead)
    up_bias = lax.dynamic_slice_in_dim(vec_params[5:].reshape(FF), head_index * units, units)

    normed_one, unit_one, scale_one = norm_rows(
        dot(rows_in, place_near, 1, 0), vec_near[0], vec_near[1]
    )
    low_one = normed_one.astype(bf16)
    lane_one = norm_rows(token_rows, vec_rows[0], vec_rows[1])[0].astype(bf16)
    own_cols = D // head_groups
    lane_one = lax.dynamic_slice_in_dim(lane_one, head_index * own_cols, own_cols, axis=1)
    low_one, lane_one = lax.optimization_barrier((low_one, lane_one))
    half = D // 2
    record = part_rows + pair_rows
    message = call(
        functools.partial(pack_kernel, share),
        array((lanes, record, 2 * DH)),
        [whole((rows, D)), whole((half, 3 * feat)), whole((half, 3 * feat))],
        [pltpu.VMEM((rows, 3 * feat), f32)],
    )(low_one, qkv_near, qkv_far)
    message, picks = lax.optimization_barrier((message, picks))
    received = lax.all_to_all(message, "seq", 0, 0, tiled=True)

    doc_end = jnp.cumsum(doc_blocks)
    doc_start = doc_end - doc_blocks
    doc_length = (doc_blocks - 1) * BLOCK + last_fill
    half_slot = (my_part * part_rows + jnp.arange(2, dtype=jnp.int32) * pair_rows) // BLOCK
    query_ids = half_slot[None, :] * lanes + jnp.arange(lanes, dtype=jnp.int32)[:, None]
    pick_half = jnp.sum(
        jnp.where(
            (half_slot[:, None] == jnp.arange(slots, dtype=jnp.int32)[None, :])[None, :, :, None],
            picks[:, None],
            0,
        ),
        axis=2,
    )
    query_doc = owning_doc(doc_end, query_ids)
    doc_first = lookup(doc_start, query_doc)
    doc_count = lookup(doc_blocks, query_doc)
    query_length = lookup(doc_length, query_doc)
    key_ids = jnp.concatenate(
        [
            jnp.stack(
                [
                    (query_ids - 1) % block_total,
                    query_ids,
                    (query_ids + 1) % block_total,
                    doc_first,
                    (doc_first + 1) % block_total,
                ],
                axis=-1,
            ),
            doc_first[..., None] + pick_half % doc_count[..., None],
        ],
        axis=-1,
    )
    same_doc = owning_doc(doc_end, key_ids) == query_doc[..., None]
    live_count = jnp.where(
        same_doc, query_length[..., None] - (key_ids - doc_first[..., None]) * BLOCK, 0
    )
    token = jnp.arange(BLOCK, dtype=jnp.int32)
    bias = jnp.where(token < live_count[..., None], 0.0, masked_score).astype(f32)
    bias = bias.reshape(lanes, 2, LISTED * BLOCK)
    key_lane = key_ids % lanes
    key_slot = key_ids // lanes
    if part_rows >= BLOCK:
        part_slots = part_rows // BLOCK
        offsets = (((key_slot // part_slots) ^ my_part) * lanes + key_lane) * part_rows
        offsets += (key_slot % part_slots) * BLOCK
    else:
        offsets = (key_lane * slots + key_slot) * BLOCK
    offsets = offsets.reshape(lanes * 2, LISTED)
    received, offsets, bias = lax.optimization_barrier((received, offsets, bias))

    parts = jnp.arange(share, dtype=jnp.int32)
    sources = [received] + [xor_permute(received, "seq", k) for k in range(1, share)]
    if part_rows < BLOCK:
        kv_parts = jnp.stack([part[:, :part_rows] for part in sources])
        kv_parts = kv_parts[parts ^ my_part].transpose(1, 0, 2, 3)
        sources = [kv_parts.reshape(lanes, slots * BLOCK, 2 * DH)]
    kv_shape = (block_total * BLOCK, 2 * DH)
    pairs_shape = (lanes, pair_rows, 2 * DH)
    probs_shape = (lanes, 2, pair_rows, LISTED * BLOCK)

    lane_one, sources = lax.optimization_barrier((lane_one, sources))
    all_one = lax.all_gather(lane_one.reshape(share, part_rows, own_cols), "seq", axis=0, tiled=False)
    all_one = lax.dynamic_index_in_dim(all_one, my_part, 1, keepdims=False)
    all_one = all_one.reshape(lanes * part_rows, own_cols)

    attend_specs = [in_smem(), whole(received.shape)] + [whole(part.shape) for part in sources]
    ctx_pairs, probs = call(
        attend_kernel,
        (array(pairs_shape), array(probs_shape)),
        attend_specs + [whole(bias.shape)],
        [pltpu.VMEM(kv_shape, bf16)],
    )(offsets, received, *sources, bias)
    ctx_pairs = lax.all_to_all(ctx_pairs, "seq", 0, 0, tiled=True)

    context, attn_part = call(
        functools.partial(project_kernel, share),
        (array((rows, feat)), array((rows, D))),
        [whole(pairs_shape), proj_block],
    )(ctx_pairs, rest_full)
    attn_sum = head_total(attn_part, head_other(attn_part))
    mid_rows = token_rows + attn_sum
    normed_two, unit_two, scale_two = norm_rows(mid_rows, vec_rows[2], vec_rows[3])
    low_two = normed_two.astype(bf16)
    hidden = dot(low_two, up_full, 1, 0) + up_bias
    active = gelu_tanh(hidden).astype(bf16)
    act_grad = dot(grad_low, down_full, 1, 0)
    hidden_grad = jax.vjp(gelu_tanh, hidden)[1](act_grad)[0]
    hidden_low = hidden_grad.astype(bf16)
    two_part = dot(hidden_low, up_full, 1, 1).astype(bf16)
    two_other = head_other(two_part)
    rest_grads = ffn_weight_grads(
        (low_two, hidden_low), (grad_low, active), rest_full.shape[1]
    )
    two_other, rest_grads = lax.optimization_barrier((two_other, rest_grads))
    two_grad = head_total(two_part, two_other)
    cut = all_one.shape[0] // 8
    first_part = [all_one[:cut]] + [
        xor_permute(all_one[:cut], "head", k) for k in range(1, head_groups)
    ]
    up_bias_grad = jnp.sum(hidden_grad, axis=0)

    mid_grad = grad_rows + norm_back(two_grad, unit_two, scale_two, vec_rows[2])
    attn_low = mid_grad.astype(bf16)
    dctx_pairs = call(
        functools.partial(dctx_kernel, share),
        array(pairs_shape),
        [whole((rows, D)), proj_block],
    )(attn_low, rest_full)
    rest_grads = last_weight_grad(attn_low, context, rest_grads)
    rest_owned = lax.psum_scatter(rest_grads, "seq", scatter_dimension=0, tiled=True).astype(f32)
    dctx_pairs = lax.all_to_all(dctx_pairs, "seq", 0, 0, tiled=True)
    dctx_pairs, rest_grads, first_part = lax.optimization_barrier(
        (dctx_pairs, rest_grads, first_part)
    )
    later_one, _ = lax.optimization_barrier((all_one[cut:], first_part))
    second_part = [later_one] + [
        xor_permute(later_one, "head", k) for k in range(1, head_groups)
    ]
    held_rows = lanes * part_rows
    away_rows = kv_shape[0] - held_rows
    if part_rows < BLOCK:
        back_shapes = (kv_shape[0] // 2,) * 2
    else:
        back_shapes = (held_rows, away_rows)
    dq_pairs, dkv_own, dkv_away = call(
        attend_back_kernel,
        (
            array(pairs_shape),
            array((back_shapes[0], 2 * DH), f32),
            array((back_shapes[1], 2 * DH)),
        ),
        attend_specs + [whole(probs_shape), whole(pairs_shape)],
        [pltpu.VMEM(kv_shape, bf16), pltpu.VMEM(kv_shape, f32)],
    )(offsets, received, *sources, probs, dctx_pairs)
    if part_rows < BLOCK:
        dkv_parts = jnp.concatenate([dkv_own, dkv_away.astype(f32)], axis=0)
        dkv_parts = dkv_parts.reshape(lanes, share, part_rows, 2 * DH)
        dkv_parts = dkv_parts[:, parts ^ my_part].transpose(1, 0, 2, 3)
        dkv_own = dkv_parts[0].reshape(held_rows, 2 * DH)
        dkv_away = dkv_parts[1:].astype(bf16)
    dkv_away = dkv_away.reshape(share - 1, held_rows, 2 * DH)
    others = jnp.stack([xor_permute(dkv_away[k - 1], "seq", k) for k in range(1, share)])
    others, active = lax.optimization_barrier((others, active))
    mixed, message = call(
        message_kernel,
        (array((held_rows, 4 * DH)), array((lanes, record, 2 * DH))),
        [whole((held_rows, 2 * DH)), whole(others.shape), whole(pairs_shape)],
    )(dkv_own, others, dq_pairs)
    returned = lax.all_to_all(message, "seq", 0, 0, tiled=True)
    head_grads = call(
        head_grad_kernel,
        array((D, 4 * DH)),
        [in_smem(), whole(mixed.shape)] + [whole(part.shape) for part in first_part + second_part],
    )(head_index.reshape(1).astype(jnp.int32), mixed, *first_part, *second_part)
    ffn_part = dot(active, down_full, 1, 1).astype(bf16)
    ffn_other = head_other(ffn_part)
    early_rows = jnp.stack(
        [jnp.sum(two_grad * unit_two, axis=0), jnp.sum(two_grad, axis=0), jnp.sum(grad_rows, axis=0)]
    )
    early_rows = exact(early_rows, place.astype(f32), back)
    early_rows = jnp.concatenate([early_rows, up_bias_grad.reshape(units // D, D)], axis=0)
    returned, head_grads, ffn_other, early_rows = lax.optimization_barrier(
        (returned, head_grads, ffn_other, early_rows)
    )
    result = (mid_rows + head_total(ffn_part, ffn_other) + vec_rows[4]).astype(bf16)
    head_grads = head_grads.reshape(lanes, width, 4 * DH)
    grad_q = head_grads[:, :, 2 * DH : 3 * DH]
    head_grads = jnp.concatenate(
        [
            head_grads[:, :, : 2 * DH],
            jnp.concatenate([grad_q[:, : width // 2], grad_q[:, width // 2 :]], axis=2),
        ],
        axis=1,
    )
    one_part, late_rows = call(
        functools.partial(one_grad_kernel, share),
        (array((rows, D)), array((16, D))),
        [whole(message.shape), whole((half, 3 * feat)), whole((half, 3 * feat))]
        + [whole((rows, D)), whole((D, D))],
        [pltpu.VMEM((rows, 3 * feat), bf16)],
    )(returned, qkv_near, qkv_far, unit_one, place_near)
    one_other = head_other(one_part)
    early_rows, one_part = lax.optimization_barrier((early_rows, one_part))
    early_rows = axis_sum(early_rows, "seq")
    late_rows = late_rows[:2].reshape(2 * D // (2 * DH), 2 * DH)
    late_rows = jnp.broadcast_to(late_rows[None], (lanes,) + late_rows.shape)
    head_grads = lax.all_to_all(
        jnp.concatenate([head_grads, late_rows], axis=1), "seq", 0, 0, tiled=True
    ).astype(f32)
    head_grads, one_other = lax.optimization_barrier((head_grads, one_other))
    one_grad = head_total(one_part, one_other)
    late_rows = axis_sum(jnp.sum(head_grads[:, width + width // 2 :], axis=0).reshape(2, D), "head")
    head_grads = head_grads[:, : width + width // 2]
    head_grads = jnp.sum(
        head_grads.reshape(heads, share, width + width // 2, 2 * DH), axis=1
    )
    kv_owned = head_grads[:, :width].reshape(heads, width, 2, DH).transpose(2, 1, 0, 3)
    q_owned = jnp.concatenate([head_grads[:, width:, :DH], head_grads[:, width:, DH:]], axis=1)
    qkv_grad = jnp.concatenate(
        [q_owned.transpose(1, 0, 2).reshape(1, width, feat), kv_owned.reshape(2, width, feat)], axis=0
    )

    layer_output = lax.dot_general(result, place, back, preferred_element_type=f32).astype(bf16)
    input_grad = exact(mid_grad, place.astype(f32), back) + exact(
        norm_back(one_grad, unit_one, scale_one, vec_near[0]), place_near.astype(f32), back
    )
    bias_rows = early_rows[3:]
    step = 1
    while step < head_groups:
        other = xor_permute(bias_rows, "head", step)
        high = (head_index & step) != 0
        bias_rows = jnp.where(
            high,
            jnp.concatenate([other, bias_rows], axis=0),
            jnp.concatenate([bias_rows, other], axis=0),
        )
        step *= 2
    vec_grad = jnp.concatenate([late_rows, early_rows[:3], bias_rows], axis=0)
    up_grad = rest_owned[:, :units]
    down_grad = rest_owned[:, units : 2 * units].T
    proj_grad = rest_owned[:, 2 * units :].T
    qkv_new, qkv_first_new, qkv_second_new = adam_step(
        qkv_weight, qkv_grad, qkv_first, qkv_second, rate_qkv
    )
    proj_new, proj_first_new, proj_second_new = adam_step(
        proj_weight, proj_grad, proj_first, proj_second, rate_proj
    )
    up_new, up_first_new, up_second_new = adam_step(up_weight, up_grad, up_first, up_second, rate_up)
    down_new, down_first_new, down_second_new = adam_step(
        down_weight, down_grad, down_first, down_second, rate_down
    )
    vec_new, vec_first_new, vec_second_new = adam_step(
        vec_params, vec_grad, vec_first, vec_second, rate_vector
    )
    return (
        layer_output.reshape(slots, BLOCK, D),
        input_grad.reshape(slots, BLOCK, D),
        qkv_new,
        qkv_first_new,
        qkv_second_new,
        qkv_new.astype(bf16),
        proj_new,
        proj_first_new,
        proj_second_new,
        proj_new.astype(bf16),
        up_new,
        up_first_new,
        up_second_new,
        up_new.astype(bf16),
        down_new,
        down_first_new,
        down_second_new,
        down_new.astype(bf16),
        vec_new,
        vec_first_new,
        vec_second_new,
    )


def solution(mesh):
    rows_by_seq = P(None, "seq", None)
    cols = P("head", "seq")
    ups = P("seq", "head")
    qkvs = P(None, "seq", "head")
    placed = (
        (rows_by_seq, rows_by_seq, P(None, "seq", "head", None), P(), P(), P())
        + (qkvs,) * 3
        + (cols,) * 3
        + (ups,) * 3
        + (cols,) * 3
        + (P(),) * 3
    )
    return jax.shard_map(
        body,
        mesh=mesh,
        in_specs=placed,
        out_specs=(rows_by_seq, rows_by_seq)
        + (qkvs,) * 4
        + (cols,) * 4
        + (ups,) * 4
        + (cols,) * 4
        + (P(),) * 3,
        check_vma=False,
    )
```

```python
import functools

import jax
import jax.numpy as jnp
from jax import lax
from jax.experimental import pallas as pl
from jax.experimental.pallas import tpu as pltpu
from jax.sharding import PartitionSpec as P

D = 1024
DH = 64
FF = 4096
BLOCK = 64
STEP = 10
LISTED = 8

eps_norm = 1e-05
masked_score = -1e30
beta_one = 0.9
beta_two = 0.999
eps_adam = 1e-08
decay_rate = 0.01
rate_qkv = 0.1
rate_proj = 1.0
rate_up = 0.1
rate_down = 0.05
rate_vector = 2.0

bf16 = jnp.bfloat16
f32 = jnp.float32


def lookup(index_table, index_rows):
    matches = index_rows[..., None] == jnp.arange(index_table.shape[0], dtype=jnp.int32)
    return jnp.sum(jnp.where(matches, index_table, 0), axis=-1)


def owning_doc(doc_end, block_ids):
    return jnp.sum((block_ids[..., None] >= doc_end).astype(jnp.int32), axis=-1)


def dot(lhs, rhs, lhs_dim, rhs_dim):
    return lax.dot_general(
        lhs, rhs, (((lhs_dim,), (rhs_dim,)), ((), ())), preferred_element_type=f32
    )


def norm_rows(token_rows, gain_row, bias_row):
    row_mean = jnp.mean(token_rows, axis=-1, keepdims=True)
    centred = token_rows - row_mean
    row_var = jnp.mean(centred * centred, axis=-1, keepdims=True)
    inv_scale = lax.rsqrt(row_var + eps_norm)
    unit_rows = centred * inv_scale
    return (unit_rows * gain_row + bias_row, unit_rows, inv_scale)


def norm_back(grad_in, unit_rows, inv_scale, gain_row):
    scaled = grad_in * gain_row
    first_mean = jnp.mean(scaled, axis=-1, keepdims=True)
    second_mean = jnp.mean(scaled * unit_rows, axis=-1, keepdims=True)
    return inv_scale * (scaled - first_mean - unit_rows * second_mean)


def gelu_tanh(values):
    return jax.nn.gelu(values, approximate=True)


def adam_step(param_old, gradient, first_old, second_old, step_rate):
    first_new = beta_one * first_old + (1.0 - beta_one) * gradient
    second_new = beta_two * second_old + (1.0 - beta_two) * gradient * gradient
    first_hat = first_new / (1.0 - beta_one**STEP)
    second_hat = second_new / (1.0 - beta_two**STEP)
    updated = param_old - step_rate * (
        first_hat / (jnp.sqrt(second_hat) + eps_adam) + decay_rate * param_old
    )
    return (updated, first_new, second_new)


def xor_permute(value, axis, mask):
    count = lax.axis_size(axis)
    return lax.ppermute(value, axis, [(i, i ^ mask) for i in range(count)])


def head_other(partial_low):
    return xor_permute(partial_low, "head", 1)


def head_total(partial_low, other):
    total = partial_low.astype(f32) + other.astype(f32)
    step = 2
    while step < lax.axis_size("head"):
        total = total + xor_permute(total, "head", step)
        step *= 2
    return total


def axis_sum(value, axis):
    step = 1
    while step < lax.axis_size(axis):
        value = value + xor_permute(value, axis, step)
        step *= 2
    return value


def lane_cuts(lanes):
    chips = lanes // 2
    ys = 1 << ((chips.bit_length() - 1) // 2)
    return 2, ys, chips // ys


def z_order(zs):
    return list(range(zs))


def relative_lanes(lanes):
    cores, ys, zs = lane_cuts(lanes)
    return [
        (kz * ys + ky) * cores + kc
        for kc in range(cores)
        for ky in range(ys)
        for kz in z_order(zs)
    ]


def relative_gather(mine, ready):
    cores, ys, zs = lane_cuts(lax.axis_size("seq"))
    column = [xor_permute(mine, "seq", kz * ys * cores) if kz else mine for kz in z_order(zs)]
    pieces = list(column)
    for ky in range(1, ys):
        pieces += [xor_permute(piece, "seq", ky * cores) for piece in column]
    near = jnp.concatenate(pieces, axis=0)
    near, ready = lax.optimization_barrier((near, ready))
    return near, xor_permute(near, "seq", 1), ready


def y_parts(total):
    _, ys, _ = lane_cuts(lax.axis_size("seq"))
    size = total.shape[0] // ys
    return total[:size], [total[k * size : (k + 1) * size].astype(bf16) for k in range(1, ys)]


def y_others(sent):
    cores, _, _ = lane_cuts(lax.axis_size("seq"))
    return [xor_permute(part, "seq", (k + 1) * cores) for k, part in enumerate(sent)]


def z_parts(total):
    _, _, zs = lane_cuts(lax.axis_size("seq"))
    size = total.shape[0] // zs
    at = {kz: total[i * size : (i + 1) * size] for i, kz in enumerate(z_order(zs))}
    return at[0], [at[kz].astype(bf16) for kz in range(1, zs)]


def z_others(sent):
    cores, ys, _ = lane_cuts(lax.axis_size("seq"))
    return [xor_permute(part, "seq", (k + 1) * ys * cores) for k, part in enumerate(sent)]


def added(kept, others):
    for other in others:
        kept = kept + other.astype(f32)
    return kept


GROUP = 8
CHUNKS = 2


def fill_rows(source_refs, kv_ref):
    start = 0
    for source_ref in source_refs:
        count = source_ref.shape[0]
        size = kv_ref.shape[0] // (count * len(source_refs))

        def copy(i, carry, start=start, size=size, source_ref=source_ref):
            at = pl.ds(pl.multiple_of(start + i * size, size), size)
            kv_ref[at, :] = source_ref[i, :size, :]
            return carry

        lax.fori_loop(0, count, copy, 0)
        start += count * size


def attend_kernel(off_ref, record_ref, *refs):
    *source_refs, bias_ref, ctx_ref, prob_ref, kv_ref = refs
    lanes, rows = ctx_ref.shape[0], ctx_ref.shape[1]
    first = record_ref.shape[1] - rows
    left = lax.broadcasted_iota(jnp.int32, (rows, 2 * DH), 1) < DH
    scale = DH**-0.5
    fill_rows(source_refs, kv_ref)

    def step(t, carry):
        units = [(t * GROUP + g, half) for g in range(GROUP) for half in range(2)]
        listed, scores = [], []
        for i, half in units:
            q_pair = record_ref[i, first:, :].astype(f32) * scale
            q_one = q_pair if half == 0 else pltpu.roll(q_pair, DH, 1)
            q_one = jnp.where(left, q_one, 0.0).astype(bf16)
            rows_here = jnp.concatenate(
                [
                    kv_ref[pl.ds(pl.multiple_of(off_ref[2 * i + half, j], BLOCK), BLOCK), :]
                    for j in range(LISTED)
                ],
                axis=0,
            )
            listed.append(rows_here)
            scores.append(dot(q_one, rows_here, 1, 1) + bias_ref[i, half : half + 1, :])
        tops = [jnp.max(score, axis=1, keepdims=True) for score in scores]
        grown = [jnp.exp(score - top) for score, top in zip(scores, tops)]
        totals = [jnp.sum(part, axis=1, keepdims=True) for part in grown]
        probs = [(part * (1.0 / total)).astype(bf16) for part, total in zip(grown, totals)]
        outs = []
        for (i, half), prob, rows_here in zip(units, probs, listed):
            prob_ref[i, half] = prob
            outs.append(dot(prob, rows_here, 1, 0))
        for g in range(GROUP):
            ctx_ref[t * GROUP + g] = jnp.where(
                left, pltpu.roll(outs[2 * g], DH, 1), outs[2 * g + 1]
            ).astype(bf16)
        return carry

    lax.fori_loop(0, lanes // GROUP, step, 0)


def attend_back_kernel(off_ref, record_ref, *refs):
    *source_refs, prob_ref, dctx_ref, dq_ref, own_ref, away_ref, kv_ref, dkv_ref = refs
    lanes, rows = dq_ref.shape[0], dq_ref.shape[1]
    first = record_ref.shape[1] - rows
    left = lax.broadcasted_iota(jnp.int32, (rows, 2 * DH), 1) < DH
    scale = DH**-0.5
    fill_rows(source_refs, kv_ref)
    dkv_ref[...] = jnp.zeros_like(dkv_ref)

    def step(t, carry):
        units = [(t * GROUP + g, half) for g in range(GROUP) for half in range(2)]
        queries, grads, offs, listed, prob_grads = [], [], [], [], []
        for i, half in units:
            q_pair = record_ref[i, first:, :].astype(f32) * scale
            d_pair = dctx_ref[i].astype(f32)
            q_one = q_pair if half == 0 else pltpu.roll(q_pair, DH, 1)
            queries.append(jnp.where(left, q_one, 0.0).astype(bf16))
            d_one = pltpu.roll(d_pair, DH, 1) if half == 0 else d_pair
            grads.append(jnp.where(left, 0.0, d_one).astype(bf16))
            offs.append(
                [pl.multiple_of(off_ref[2 * i + half, j], BLOCK) for j in range(LISTED)]
            )
            listed.append(
                jnp.concatenate([kv_ref[pl.ds(o, BLOCK), :] for o in offs[-1]], axis=0)
            )
            prob_grads.append(dot(grads[-1], listed[-1], 1, 1))
        probs_low = [prob_ref[i, half] for i, half in units]
        probs = [prob.astype(f32) for prob in probs_low]
        weighted = [prob * grad for prob, grad in zip(probs, prob_grads)]
        row_dots = [jnp.sum(part, axis=1, keepdims=True) for part in weighted]
        scores_low = [
            (part - prob * row_dot).astype(bf16)
            for part, prob, row_dot in zip(weighted, probs, row_dots)
        ]
        outs = [dot(score, rows_here, 1, 0) * scale for score, rows_here in zip(scores_low, listed)]
        for n in range(len(units)):
            both = jnp.concatenate([scores_low[n], probs_low[n]], axis=0)
            mates = jnp.concatenate([queries[n], grads[n]], axis=0)
            kv_grad = dot(both, mates, 0, 0)
            for j in range(LISTED):
                at = pl.ds(offs[n][j], BLOCK)
                dkv_ref[at, :] += kv_grad[j * BLOCK : (j + 1) * BLOCK]
        for g in range(GROUP):
            dq_ref[t * GROUP + g] = jnp.where(
                left, outs[2 * g], pltpu.roll(outs[2 * g + 1], DH, 1)
            ).astype(bf16)
        return carry

    lax.fori_loop(0, lanes // GROUP, step, 0)
    held = own_ref.shape[0]
    own_ref[...] = dkv_ref[:held, :]
    away_ref[...] = dkv_ref[held:, :].astype(bf16)


def message_kernel(own_ref, other_ref, dq_ref, msg_ref):
    lanes, record = msg_ref.shape[0], msg_ref.shape[1]
    part_rows = 2 * record // 3

    def step(i, carry):
        at = pl.ds(pl.multiple_of(i * part_rows, part_rows), part_rows)
        total = own_ref[at, :]
        for k in range(other_ref.shape[0]):
            total += other_ref[k, at, :].astype(f32)
        msg_ref[i, :part_rows, :] = total.astype(bf16)
        msg_ref[i, part_rows:, :] = dq_ref[i]
        return carry

    lax.fori_loop(0, lanes, step, 0)


def pack_kernel(share, low_ref, near_ref, far_ref, msg_ref, rows_ref):
    lanes, record = msg_ref.shape[0], msg_ref.shape[1]
    heads = lanes // share
    feat = heads * DH
    part_rows = 2 * record // 3
    pair_rows = part_rows // 2
    half = D // 2
    for c in range(3):
        cols = slice(c * feat, (c + 1) * feat)
        rows_ref[:, cols] = dot(low_ref[:, :half], near_ref[:, cols], 1, 0) + dot(
            low_ref[:, half:], far_ref[:, cols], 1, 0
        )
    left = lax.broadcasted_iota(jnp.int32, (part_rows, 2 * DH), 1) < DH
    for h in range(0, heads, 2):
        for r in range(share):
            at = slice(r * part_rows, (r + 1) * part_rows)
            query, keys, vals = (
                rows_ref[at, c * feat + h * DH : c * feat + (h + 2) * DH] for c in range(3)
            )
            even, odd = h * share + r, (h + 1) * share + r
            msg_ref[even, :part_rows, :] = jnp.where(left, keys, pltpu.roll(vals, DH, 1)).astype(
                bf16
            )
            msg_ref[odd, :part_rows, :] = jnp.where(left, pltpu.roll(keys, DH, 1), vals).astype(
                bf16
            )
            first, second = query[:pair_rows], query[pair_rows:]
            over = left[:pair_rows]
            msg_ref[even, part_rows:, :] = jnp.where(over, first, pltpu.roll(second, DH, 1)).astype(
                bf16
            )
            msg_ref[odd, part_rows:, :] = jnp.where(over, pltpu.roll(first, DH, 1), second).astype(
                bf16
            )


def unpack_pairs(read, heads, share, pair_rows, write):
    left = lax.broadcasted_iota(jnp.int32, (pair_rows, 2 * DH), 1) < DH
    for h in range(0, heads, 2):
        cols = slice(h * DH, (h + 2) * DH)
        for r in range(share):
            even, odd = read(h * share + r), read((h + 1) * share + r)
            base = 2 * r * pair_rows
            first = jnp.where(left, even, pltpu.roll(odd, DH, 1))
            second = jnp.where(left, pltpu.roll(even, DH, 1), odd)
            write(slice(base, base + pair_rows), cols, first)
            write(slice(base + pair_rows, base + 2 * pair_rows), cols, second)


def project_kernel(share, pairs_ref, proj_ref, ctx_ref, out_ref):
    heads, pair_rows = pairs_ref.shape[0] // share, pairs_ref.shape[1]

    def write(rows, cols, value):
        ctx_ref[rows, cols] = value.astype(bf16)

    unpack_pairs(lambda n: pairs_ref[n].astype(f32), heads, share, pair_rows, write)
    out_ref[...] = dot(ctx_ref[...], proj_ref[...], 1, 1).astype(bf16)


def dctx_kernel(share, low_ref, proj_ref, pairs_ref):
    heads, pair_rows = pairs_ref.shape[0] // share, pairs_ref.shape[1]
    left = lax.broadcasted_iota(jnp.int32, (pair_rows, 2 * DH), 1) < DH
    grad = dot(low_ref[...], proj_ref[...], 1, 0)
    for h in range(0, heads, 2):
        cols = slice(h * DH, (h + 2) * DH)
        for r in range(share):
            base = 2 * r * pair_rows
            first = grad[base : base + pair_rows, cols]
            second = grad[base + pair_rows : base + 2 * pair_rows, cols]
            pairs_ref[h * share + r] = jnp.where(left, first, pltpu.roll(second, DH, 1)).astype(
                bf16
            )
            pairs_ref[(h + 1) * share + r] = jnp.where(
                left, pltpu.roll(first, DH, 1), second
            ).astype(bf16)


def one_grad_kernel(share, msg_ref, near_ref, far_ref, unit_ref, place_ref, out_ref, late_ref, rows_ref):
    lanes, record = msg_ref.shape[0], msg_ref.shape[1]
    heads = lanes // share
    feat = heads * DH
    part_rows = 2 * record // 3
    pair_rows = part_rows // 2

    def write(rows, cols, value):
        rows_ref[rows, cols] = value.astype(bf16)

    unpack_pairs(
        lambda n: msg_ref[n, part_rows:, :].astype(f32), heads, share, pair_rows, write
    )
    left = lax.broadcasted_iota(jnp.int32, (part_rows, 2 * DH), 1) < DH
    for h in range(0, heads, 2):
        for r in range(share):
            even = msg_ref[h * share + r, :part_rows, :].astype(f32)
            odd = msg_ref[(h + 1) * share + r, :part_rows, :].astype(f32)
            at = slice(r * part_rows, (r + 1) * part_rows)
            keys = jnp.where(left, even, pltpu.roll(odd, DH, 1))
            vals = jnp.where(left, pltpu.roll(even, DH, 1), odd)
            rows_ref[at, feat + h * DH : feat + (h + 2) * DH] = keys.astype(bf16)
            rows_ref[at, 2 * feat + h * DH : 2 * feat + (h + 2) * DH] = vals.astype(bf16)
    half = D // 2
    out_ref[:, :half] = dot(rows_ref[...], near_ref[...], 1, 1).astype(bf16)
    out_ref[:, half:] = dot(rows_ref[...], far_ref[...], 1, 1).astype(bf16)
    grad = out_ref[...].astype(f32)
    gain = jnp.sum(grad * unit_ref[...], axis=0, keepdims=True)
    shift = jnp.sum(grad, axis=0, keepdims=True)
    sums = jnp.concatenate([gain, shift, jnp.zeros((14, D), f32)], axis=0)
    total = 0.0
    for _ in range(3):
        low = sums.astype(bf16)
        total += dot(low, place_ref[...], 1, 1)
        sums = sums - low.astype(f32)
    late_ref[...] = total


def weight_grad_kernel(lhs_a, rhs_a, lhs_b, rhs_b, out_ref, *, first):
    at = pl.program_id(0)

    @pl.when(at < first)
    def _():
        out_ref[...] = dot(lhs_a[...], rhs_a[...], 0, 0).astype(bf16)

    @pl.when(at >= first)
    def _():
        out_ref[...] = dot(lhs_b[...], rhs_b[...], 0, 0).astype(bf16)


def last_grad_kernel(lhs, rhs, whole_ref, out_ref):
    out_ref[...] = dot(lhs[...], rhs[...], 0, 0).astype(bf16)


VMEM_LIMIT = 48 * 1024 * 1024


def in_smem():
    return pl.BlockSpec(memory_space=pltpu.SMEM)


def call(kernel, outs, specs, scratch=(), out_specs=None):
    return pl.pallas_call(
        kernel,
        grid=(1,),
        out_shape=outs,
        in_specs=specs,
        out_specs=jax.tree.map(lambda o: whole(o.shape), outs) if out_specs is None else out_specs,
        scratch_shapes=list(scratch),
        compiler_params=pltpu.CompilerParams(vmem_limit_bytes=VMEM_LIMIT),
    )


def whole(shape):
    return pl.BlockSpec(tuple(shape), lambda i: (0,) * len(shape))


def array(shape, dtype=bf16):
    return jax.ShapeDtypeStruct(shape, dtype)


def ffn_weight_grads(first, second, aside, more):
    units = first[1].shape[1]
    block = min(512, units)
    counts = (units // block, (units - aside) // block)
    specs = []
    for start, skip, count, (lhs, rhs) in (
        (0, 0, counts[0], first),
        (counts[0], aside // block, counts[1], second),
    ):
        specs.append(whole(lhs.shape))
        specs.append(
            pl.BlockSpec(
                (rhs.shape[0], block),
                lambda i, start=start, skip=skip, count=count: (
                    0,
                    jnp.clip(i - start, 0, count - 1) + skip,
                ),
            )
        )
    width = 2 * units - aside
    return pl.pallas_call(
        functools.partial(weight_grad_kernel, first=counts[0]),
        grid=(sum(counts),),
        out_shape=array((D, width + more)),
        in_specs=specs,
        out_specs=pl.BlockSpec((D, block), lambda i: (0, i)),
        compiler_params=pltpu.CompilerParams(vmem_limit_bytes=VMEM_LIMIT),
        cost_estimate=pl.CostEstimate(
            flops=2 * D * width * first[1].shape[0], bytes_accessed=2 * D * width, transcendentals=0
        ),
    )(*first, *second)


def last_weight_grad(lhs, rhs, into):
    block = rhs.shape[1]
    return pl.pallas_call(
        last_grad_kernel,
        grid=(1,),
        out_shape=array(into.shape),
        in_specs=[whole(lhs.shape), whole(rhs.shape), pl.BlockSpec(memory_space=pl.ANY)],
        out_specs=pl.BlockSpec((D, block), lambda i: (0, into.shape[1] // block - 1)),
        input_output_aliases={2: 0},
        compiler_params=pltpu.CompilerParams(vmem_limit_bytes=VMEM_LIMIT),
    )(lhs, rhs, into)


def body(
    layer_input,
    output_grad,
    random_pick,
    doc_blocks,
    last_fill,
    shard_owner,
    qkv_weight,
    qkv_first,
    qkv_second,
    proj_weight,
    proj_first,
    proj_second,
    up_weight,
    up_first,
    up_second,
    down_weight,
    down_first,
    down_second,
    vec_params,
    vec_first,
    vec_second,
):
    lanes = lax.axis_size("seq")
    lane_index = lax.axis_index("seq")
    head_groups = lax.axis_size("head")
    head_index = lax.axis_index("head")
    slots = layer_input.shape[0]
    heads = random_pick.shape[2]
    feat = heads * DH
    units = up_weight.shape[1]
    rows = slots * BLOCK
    block_total = slots * lanes
    share = lanes // heads
    part_rows = rows // share
    pair_rows = part_rows // 2
    my_part = lane_index % share
    width = D // lanes

    picks = random_pick[:, 0].transpose(1, 0, 2).reshape(heads, slots * 3)
    picks = jnp.broadcast_to(picks[:, None], (heads, share, slots * 3)).reshape(lanes, slots * 3)
    picks = lax.all_to_all(picks, "seq", 0, 0, tiled=True).reshape(lanes, slots, 3)

    qkv_mine = qkv_weight.astype(bf16).transpose(1, 0, 2).reshape(width, 3 * feat)
    first_mine = jnp.concatenate([up_weight.astype(bf16), proj_weight.astype(bf16).T], axis=1)
    first_full = lax.all_gather(first_mine, "seq", axis=0, tiled=True)
    up_full = first_full[:, :units]
    proj_block = pl.BlockSpec((D, feat), lambda i: (0, units // feat))

    column = jnp.arange(D, dtype=jnp.int32)
    owner = lookup(shard_owner, column // width)
    masks = jnp.array(relative_lanes(lanes), jnp.int32)
    position = jnp.sum(
        jnp.where(
            masks[None, :] == (owner ^ lane_index)[:, None], jnp.arange(lanes, dtype=jnp.int32), 0
        ),
        axis=1,
    )
    place = (owner * width + column % width)[:, None] == column[None, :]
    place_near = (position * width + column % width)[:, None] == column[None, :]
    place, place_near = place.astype(bf16), place_near.astype(bf16)
    rows_in = layer_input.reshape(rows, D)
    token_rows = dot(rows_in, place, 1, 0)
    grad_low = dot(output_grad.reshape(rows, D), place, 1, 0).astype(bf16)
    grad_rows = grad_low.astype(f32)
    exact = functools.partial(
        lax.dot_general, precision=lax.Precision.HIGHEST, preferred_element_type=f32
    )
    ahead = (((1,), (0,)), ((), ()))
    back = (((1,), (1,)), ((), ()))
    vec_rows = exact(vec_params[:5], place.astype(f32), ahead)
    vec_near = exact(vec_params[:2], place_near.astype(f32), ahead)
    up_bias = lax.dynamic_slice_in_dim(vec_params[5:].reshape(FF), head_index * units, units)

    normed_one, unit_one, scale_one = norm_rows(
        dot(rows_in, place_near, 1, 0), vec_near[0], vec_near[1]
    )
    low_one = normed_one.astype(bf16)
    qkv_near, qkv_far, low_one = relative_gather(qkv_mine, low_one)
    half = D // 2
    record = part_rows + pair_rows
    message = call(
        functools.partial(pack_kernel, share),
        array((lanes, record, 2 * DH)),
        [whole((rows, D)), whole((half, 3 * feat)), whole((half, 3 * feat))],
        [pltpu.VMEM((rows, 3 * feat), f32)],
    )(low_one, qkv_near, qkv_far)
    message, picks = lax.optimization_barrier((message, picks))
    received = lax.all_to_all(message, "seq", 0, 0, tiled=True)

    doc_end = jnp.cumsum(doc_blocks)
    doc_start = doc_end - doc_blocks
    doc_length = (doc_blocks - 1) * BLOCK + last_fill
    half_slot = (my_part * part_rows + jnp.arange(2, dtype=jnp.int32) * pair_rows) // BLOCK
    query_ids = half_slot[None, :] * lanes + jnp.arange(lanes, dtype=jnp.int32)[:, None]
    pick_half = jnp.sum(
        jnp.where(
            (half_slot[:, None] == jnp.arange(slots, dtype=jnp.int32)[None, :])[None, :, :, None],
            picks[:, None],
            0,
        ),
        axis=2,
    )
    query_doc = owning_doc(doc_end, query_ids)
    doc_first = lookup(doc_start, query_doc)
    doc_count = lookup(doc_blocks, query_doc)
    query_length = lookup(doc_length, query_doc)
    key_ids = jnp.concatenate(
        [
            jnp.stack(
                [
                    (query_ids - 1) % block_total,
                    query_ids,
                    (query_ids + 1) % block_total,
                    doc_first,
                    (doc_first + 1) % block_total,
                ],
                axis=-1,
            ),
            doc_first[..., None] + pick_half % doc_count[..., None],
        ],
        axis=-1,
    )
    same_doc = owning_doc(doc_end, key_ids) == query_doc[..., None]
    live_count = jnp.where(
        same_doc, query_length[..., None] - (key_ids - doc_first[..., None]) * BLOCK, 0
    )
    token = jnp.arange(BLOCK, dtype=jnp.int32)
    bias = jnp.where(token < live_count[..., None], 0.0, masked_score).astype(f32)
    bias = bias.reshape(lanes, 2, LISTED * BLOCK)
    key_lane = key_ids % lanes
    key_slot = key_ids // lanes
    if part_rows >= BLOCK:
        part_slots = part_rows // BLOCK
        offsets = (((key_slot // part_slots) ^ my_part) * lanes + key_lane) * part_rows
        offsets += (key_slot % part_slots) * BLOCK
    else:
        offsets = (key_lane * slots + key_slot) * BLOCK
    offsets = offsets.reshape(lanes * 2, LISTED)
    down_mine = down_weight.astype(bf16).T
    received, offsets, bias, down_mine = lax.optimization_barrier(
        (received, offsets, bias, down_mine)
    )
    down_full = lax.all_gather(down_mine, "seq", axis=0, tiled=True)

    parts = jnp.arange(share, dtype=jnp.int32)
    sources = [received] + [xor_permute(received, "seq", k) for k in range(1, share)]
    if part_rows < BLOCK:
        kv_parts = jnp.stack([part[:, :part_rows] for part in sources])
        kv_parts = kv_parts[parts ^ my_part].transpose(1, 0, 2, 3)
        sources = [kv_parts.reshape(lanes, slots * BLOCK, 2 * DH)]
    kv_shape = (block_total * BLOCK, 2 * DH)
    pairs_shape = (lanes, pair_rows, 2 * DH)
    probs_shape = (lanes, 2, pair_rows, LISTED * BLOCK)

    attend_specs = [in_smem(), whole(received.shape)] + [whole(part.shape) for part in sources]
    ctx_pairs, probs = call(
        attend_kernel,
        (array(pairs_shape), array(probs_shape)),
        attend_specs + [whole(bias.shape)],
        [pltpu.VMEM(kv_shape, bf16)],
    )(offsets, received, *sources, bias)
    ctx_pairs = lax.all_to_all(ctx_pairs, "seq", 0, 0, tiled=True)

    context, attn_part = call(
        functools.partial(project_kernel, share),
        (array((rows, feat)), array((rows, D))),
        [whole(pairs_shape), proj_block],
    )(ctx_pairs, first_full)
    attn_sum = head_total(attn_part, head_other(attn_part))
    mid_rows = token_rows + attn_sum
    normed_two, unit_two, scale_two = norm_rows(mid_rows, vec_rows[2], vec_rows[3])
    low_two = normed_two.astype(bf16)
    hidden = dot(low_two, up_full, 1, 0) + up_bias
    active = gelu_tanh(hidden).astype(bf16)
    act_grad = dot(grad_low, down_full, 1, 0)
    hidden_grad = jax.vjp(gelu_tanh, hidden)[1](act_grad)[0]
    hidden_low = hidden_grad.astype(bf16)
    two_part = dot(hidden_low, up_full, 1, 1).astype(bf16)
    two_other = head_other(two_part)
    rest_grads = ffn_weight_grads((low_two, hidden_low), (grad_low, active), 0, feat)
    two_other, rest_grads = lax.optimization_barrier((two_other, rest_grads))
    two_grad = head_total(two_part, two_other)
    up_bias_grad = jnp.sum(hidden_grad, axis=0)

    mid_grad = grad_rows + norm_back(two_grad, unit_two, scale_two, vec_rows[2])
    attn_low = mid_grad.astype(bf16)
    dctx_pairs = call(
        functools.partial(dctx_kernel, share),
        array(pairs_shape),
        [whole((rows, D)), proj_block],
    )(attn_low, first_full)
    rest_grads = last_weight_grad(attn_low, context, rest_grads)
    rest_owned = lax.psum_scatter(rest_grads, "seq", scatter_dimension=0, tiled=True).astype(f32)
    dctx_pairs = lax.all_to_all(dctx_pairs, "seq", 0, 0, tiled=True)
    dctx_pairs, rest_grads = lax.optimization_barrier((dctx_pairs, rest_grads))
    held_rows = lanes * part_rows
    away_rows = kv_shape[0] - held_rows
    if part_rows < BLOCK:
        back_shapes = (kv_shape[0] // 2,) * 2
    else:
        back_shapes = (held_rows, away_rows)
    dq_pairs, dkv_own, dkv_away = call(
        attend_back_kernel,
        (
            array(pairs_shape),
            array((back_shapes[0], 2 * DH), f32),
            array((back_shapes[1], 2 * DH)),
        ),
        attend_specs + [whole(probs_shape), whole(pairs_shape)],
        [pltpu.VMEM(kv_shape, bf16), pltpu.VMEM(kv_shape, f32)],
    )(offsets, received, *sources, probs, dctx_pairs)
    if part_rows < BLOCK:
        dkv_parts = jnp.concatenate([dkv_own, dkv_away.astype(f32)], axis=0)
        dkv_parts = dkv_parts.reshape(lanes, share, part_rows, 2 * DH)
        dkv_parts = dkv_parts[:, parts ^ my_part].transpose(1, 0, 2, 3)
        dkv_own = dkv_parts[0].reshape(held_rows, 2 * DH)
        dkv_away = dkv_parts[1:].astype(bf16)
    dkv_away = dkv_away.reshape(share - 1, held_rows, 2 * DH)
    others = jnp.stack([xor_permute(dkv_away[k - 1], "seq", k) for k in range(1, share)])
    others, active = lax.optimization_barrier((others, active))
    message = call(
        message_kernel,
        array((lanes, record, 2 * DH)),
        [whole((held_rows, 2 * DH)), whole(others.shape), whole(pairs_shape)],
    )(dkv_own, others, dq_pairs)
    returned = lax.all_to_all(message, "seq", 0, 0, tiled=True)
    ffn_part = dot(active, down_full, 1, 1).astype(bf16)
    ffn_other = head_other(ffn_part)
    early_rows = jnp.stack(
        [jnp.sum(two_grad * unit_two, axis=0), jnp.sum(two_grad, axis=0), jnp.sum(grad_rows, axis=0)]
    )
    early_rows = exact(early_rows, place.astype(f32), back)
    early_rows = jnp.concatenate([early_rows, up_bias_grad.reshape(units // D, D)], axis=0)
    returned, ffn_other, early_rows = lax.optimization_barrier((returned, ffn_other, early_rows))
    result = (mid_rows + head_total(ffn_part, ffn_other) + vec_rows[4]).astype(bf16)
    one_part, late_rows, dqkv = call(
        functools.partial(one_grad_kernel, share),
        (array((rows, D)), array((16, D), f32), array((rows, 3 * feat))),
        [whole(message.shape), whole((half, 3 * feat)), whole((half, 3 * feat))]
        + [whole((rows, D)), whole((D, D))],
    )(returned, qkv_near, qkv_far, unit_one, place_near)
    one_other = head_other(one_part)
    vec_sums = axis_sum(jnp.concatenate([late_rows[:2], early_rows], axis=0), "seq")
    late_rows = axis_sum(vec_sums[:2], "head")
    early_rows = vec_sums[2:]

    chunk = 3 * feat // CHUNKS
    far_sums, near_sums = [], []
    for c in range(CHUNKS):
        cols = dqkv[:, c * chunk : (c + 1) * chunk]
        far_sums.append(xor_permute(dot(low_one[:, half:], cols, 0, 0).astype(bf16), "seq", 1))
        near_sums.append(dot(low_one[:, :half], cols, 0, 0))
    qkv_owned = []
    for near_sum, far_sum in zip(near_sums, far_sums):
        kept, sent = y_parts(added(near_sum, [far_sum]))
        kept, sent = z_parts(added(kept, y_others(sent)))
        qkv_owned.append((kept, z_others(sent)))
    qkv_last = qkv_owned.pop()
    qkv_owned = [added(*pair) for pair in qkv_owned]
    one_grad = head_total(one_part, one_other)

    layer_output = lax.dot_general(result, place, back, preferred_element_type=f32).astype(bf16)
    input_grad = exact(mid_grad, place.astype(f32), back) + exact(
        norm_back(one_grad, unit_one, scale_one, vec_near[0]), place_near.astype(f32), back
    )
    bias_rows = early_rows[3:]
    step = 1
    while step < head_groups:
        other = xor_permute(bias_rows, "head", step)
        high = (head_index & step) != 0
        bias_rows = jnp.where(
            high,
            jnp.concatenate([other, bias_rows], axis=0),
            jnp.concatenate([bias_rows, other], axis=0),
        )
        step *= 2
    vec_grad = jnp.concatenate([late_rows, early_rows[:3], bias_rows], axis=0)
    up_grad = rest_owned[:, :units]
    down_grad = rest_owned[:, units : 2 * units].T
    proj_grad = rest_owned[:, 2 * units :].T
    proj_new, proj_first_new, proj_second_new = adam_step(
        proj_weight, proj_grad, proj_first, proj_second, rate_proj
    )
    up_new, up_first_new, up_second_new = adam_step(up_weight, up_grad, up_first, up_second, rate_up)
    down_new, down_first_new, down_second_new = adam_step(
        down_weight, down_grad, down_first, down_second, rate_down
    )
    qkv_last, up_new, down_new, proj_new = lax.optimization_barrier(
        (qkv_last, up_new, down_new, proj_new)
    )
    qkv_owned.append(added(*qkv_last))
    qkv_grad = jnp.concatenate(qkv_owned, axis=1).reshape(width, 3, feat).transpose(1, 0, 2)
    qkv_new, qkv_first_new, qkv_second_new = adam_step(
        qkv_weight, qkv_grad, qkv_first, qkv_second, rate_qkv
    )
    vec_new, vec_first_new, vec_second_new = adam_step(
        vec_params, vec_grad, vec_first, vec_second, rate_vector
    )
    return (
        layer_output.reshape(slots, BLOCK, D),
        input_grad.reshape(slots, BLOCK, D),
        qkv_new,
        qkv_first_new,
        qkv_second_new,
        qkv_new.astype(bf16),
        proj_new,
        proj_first_new,
        proj_second_new,
        proj_new.astype(bf16),
        up_new,
        up_first_new,
        up_second_new,
        up_new.astype(bf16),
        down_new,
        down_first_new,
        down_second_new,
        down_new.astype(bf16),
        vec_new,
        vec_first_new,
        vec_second_new,
    )


def solution(mesh):
    rows_by_seq = P(None, "seq", None)
    cols = P("head", "seq")
    ups = P("seq", "head")
    qkvs = P(None, "seq", "head")
    placed = (
        (rows_by_seq, rows_by_seq, P(None, "seq", "head", None), P(), P(), P())
        + (qkvs,) * 3
        + (cols,) * 3
        + (ups,) * 3
        + (cols,) * 3
        + (P(),) * 3
    )
    return jax.shard_map(
        body,
        mesh=mesh,
        in_specs=placed,
        out_specs=(rows_by_seq, rows_by_seq)
        + (qkvs,) * 4
        + (cols,) * 4
        + (ups,) * 4
        + (cols,) * 4
        + (P(),) * 3,
        check_vma=False,
    )
```

```python
import functools

import jax
import jax.numpy as jnp
from jax import lax
from jax.experimental import pallas as pl
from jax.experimental.pallas import tpu as pltpu
from jax.sharding import PartitionSpec as P

D = 1024
DH = 64
FF = 4096
BLOCK = 64
STEP = 10
LISTED = 8

eps_norm = 1e-05
masked_score = -1e30
beta_one = 0.9
beta_two = 0.999
eps_adam = 1e-08
decay_rate = 0.01
rate_qkv = 0.1
rate_proj = 1.0
rate_up = 0.1
rate_down = 0.05
rate_vector = 2.0

bf16 = jnp.bfloat16
f32 = jnp.float32


def lookup(index_table, index_rows):
    matches = index_rows[..., None] == jnp.arange(index_table.shape[0], dtype=jnp.int32)
    return jnp.sum(jnp.where(matches, index_table, 0), axis=-1)


def owning_doc(doc_end, block_ids):
    return jnp.sum((block_ids[..., None] >= doc_end).astype(jnp.int32), axis=-1)


def dot(lhs, rhs, lhs_dim, rhs_dim):
    return lax.dot_general(
        lhs, rhs, (((lhs_dim,), (rhs_dim,)), ((), ())), preferred_element_type=f32
    )


def norm_rows(token_rows, gain_row, bias_row):
    row_mean = jnp.mean(token_rows, axis=-1, keepdims=True)
    centred = token_rows - row_mean
    row_var = jnp.mean(centred * centred, axis=-1, keepdims=True)
    inv_scale = lax.rsqrt(row_var + eps_norm)
    unit_rows = centred * inv_scale
    return (unit_rows * gain_row + bias_row, unit_rows, inv_scale)


def norm_back(grad_in, unit_rows, inv_scale, gain_row):
    scaled = grad_in * gain_row
    first_mean = jnp.mean(scaled, axis=-1, keepdims=True)
    second_mean = jnp.mean(scaled * unit_rows, axis=-1, keepdims=True)
    return inv_scale * (scaled - first_mean - unit_rows * second_mean)


def gelu_tanh(values):
    return jax.nn.gelu(values, approximate=True)


def adam_step(param_old, gradient, first_old, second_old, step_rate):
    first_new = beta_one * first_old + (1.0 - beta_one) * gradient
    second_new = beta_two * second_old + (1.0 - beta_two) * gradient * gradient
    first_hat = first_new / (1.0 - beta_one**STEP)
    second_hat = second_new / (1.0 - beta_two**STEP)
    updated = param_old - step_rate * (
        first_hat / (jnp.sqrt(second_hat) + eps_adam) + decay_rate * param_old
    )
    return (updated, first_new, second_new)


def xor_permute(value, axis, mask):
    count = lax.axis_size(axis)
    return lax.ppermute(value, axis, [(i, i ^ mask) for i in range(count)])


def head_other(partial_low):
    return xor_permute(partial_low, "head", 1)


def head_total(partial_low, other):
    total = partial_low.astype(f32) + other.astype(f32)
    step = 2
    while step < lax.axis_size("head"):
        total = total + xor_permute(total, "head", step)
        step *= 2
    return total


def axis_sum(value, axis):
    step = 1
    while step < lax.axis_size(axis):
        value = value + xor_permute(value, axis, step)
        step *= 2
    return value


def lane_cuts(lanes):
    chips = lanes // 2
    ys = 1 << ((chips.bit_length() - 1) // 2)
    return 2, ys, chips // ys


def z_order(zs):
    return list(range(zs))


def relative_lanes(lanes):
    cores, ys, zs = lane_cuts(lanes)
    return [
        (kz * ys + ky) * cores + kc
        for kc in range(cores)
        for ky in range(ys)
        for kz in z_order(zs)
    ]


def relative_gather(mine, ready):
    cores, ys, zs = lane_cuts(lax.axis_size("seq"))
    column = [xor_permute(mine, "seq", kz * ys * cores) if kz else mine for kz in z_order(zs)]
    pieces = list(column)
    for ky in range(1, ys):
        pieces += [xor_permute(piece, "seq", ky * cores) for piece in column]
    near = jnp.concatenate(pieces, axis=0)
    near, ready = lax.optimization_barrier((near, ready))
    return near, xor_permute(near, "seq", 1), ready


def y_parts(total):
    _, ys, _ = lane_cuts(lax.axis_size("seq"))
    size = total.shape[0] // ys
    return total[:size], [total[k * size : (k + 1) * size].astype(bf16) for k in range(1, ys)]


def y_others(sent):
    cores, _, _ = lane_cuts(lax.axis_size("seq"))
    return [xor_permute(part, "seq", (k + 1) * cores) for k, part in enumerate(sent)]


def z_parts(total):
    _, _, zs = lane_cuts(lax.axis_size("seq"))
    size = total.shape[0] // zs
    at = {kz: total[i * size : (i + 1) * size] for i, kz in enumerate(z_order(zs))}
    return at[0], [at[kz].astype(bf16) for kz in range(1, zs)]


def z_others(sent):
    cores, ys, _ = lane_cuts(lax.axis_size("seq"))
    return [xor_permute(part, "seq", (k + 1) * ys * cores) for k, part in enumerate(sent)]


def added(kept, others):
    for other in others:
        kept = kept + other.astype(f32)
    return kept


GROUP = 8
CHUNKS = 2


def fill_rows(source_refs, kv_ref):
    start = 0
    for source_ref in source_refs:
        count = source_ref.shape[0]
        size = kv_ref.shape[0] // (count * len(source_refs))

        def copy(i, carry, start=start, size=size, source_ref=source_ref):
            at = pl.ds(pl.multiple_of(start + i * size, size), size)
            kv_ref[at, :] = source_ref[i, :size, :]
            return carry

        lax.fori_loop(0, count, copy, 0)
        start += count * size


def attend_kernel(off_ref, record_ref, *refs):
    *source_refs, bias_ref, ctx_ref, prob_ref, kv_ref = refs
    lanes, rows = ctx_ref.shape[0], ctx_ref.shape[1]
    first = record_ref.shape[1] - rows
    left = lax.broadcasted_iota(jnp.int32, (rows, 2 * DH), 1) < DH
    scale = DH**-0.5
    fill_rows(source_refs, kv_ref)

    def step(t, carry):
        units = [(t * GROUP + g, half) for g in range(GROUP) for half in range(2)]
        listed, scores = [], []
        for i, half in units:
            q_pair = record_ref[i, first:, :].astype(f32) * scale
            q_one = q_pair if half == 0 else pltpu.roll(q_pair, DH, 1)
            q_one = jnp.where(left, q_one, 0.0).astype(bf16)
            rows_here = jnp.concatenate(
                [
                    kv_ref[pl.ds(pl.multiple_of(off_ref[2 * i + half, j], BLOCK), BLOCK), :]
                    for j in range(LISTED)
                ],
                axis=0,
            )
            listed.append(rows_here)
            scores.append(dot(q_one, rows_here, 1, 1) + bias_ref[i, half : half + 1, :])
        tops = [jnp.max(score, axis=1, keepdims=True) for score in scores]
        grown = [jnp.exp(score - top) for score, top in zip(scores, tops)]
        totals = [jnp.sum(part, axis=1, keepdims=True) for part in grown]
        probs = [(part * (1.0 / total)).astype(bf16) for part, total in zip(grown, totals)]
        outs = []
        for (i, half), prob, rows_here in zip(units, probs, listed):
            prob_ref[i, half] = prob
            outs.append(dot(prob, rows_here, 1, 0))
        for g in range(GROUP):
            ctx_ref[t * GROUP + g] = jnp.where(
                left, pltpu.roll(outs[2 * g], DH, 1), outs[2 * g + 1]
            ).astype(bf16)
        return carry

    lax.fori_loop(0, lanes // GROUP, step, 0)


def attend_back_kernel(off_ref, record_ref, *refs):
    *source_refs, prob_ref, dctx_ref, dq_ref, own_ref, away_ref, kv_ref, dkv_ref = refs
    lanes, rows = dq_ref.shape[0], dq_ref.shape[1]
    first = record_ref.shape[1] - rows
    left = lax.broadcasted_iota(jnp.int32, (rows, 2 * DH), 1) < DH
    scale = DH**-0.5
    fill_rows(source_refs, kv_ref)
    dkv_ref[...] = jnp.zeros_like(dkv_ref)

    def step(t, carry):
        units = [(t * GROUP + g, half) for g in range(GROUP) for half in range(2)]
        queries, grads, offs, listed, prob_grads = [], [], [], [], []
        for i, half in units:
            q_pair = record_ref[i, first:, :].astype(f32) * scale
            d_pair = dctx_ref[i].astype(f32)
            q_one = q_pair if half == 0 else pltpu.roll(q_pair, DH, 1)
            queries.append(jnp.where(left, q_one, 0.0).astype(bf16))
            d_one = pltpu.roll(d_pair, DH, 1) if half == 0 else d_pair
            grads.append(jnp.where(left, 0.0, d_one).astype(bf16))
            offs.append(
                [pl.multiple_of(off_ref[2 * i + half, j], BLOCK) for j in range(LISTED)]
            )
            listed.append(
                jnp.concatenate([kv_ref[pl.ds(o, BLOCK), :] for o in offs[-1]], axis=0)
            )
            prob_grads.append(dot(grads[-1], listed[-1], 1, 1))
        probs_low = [prob_ref[i, half] for i, half in units]
        probs = [prob.astype(f32) for prob in probs_low]
        weighted = [prob * grad for prob, grad in zip(probs, prob_grads)]
        row_dots = [jnp.sum(part, axis=1, keepdims=True) for part in weighted]
        scores_low = [
            (part - prob * row_dot).astype(bf16)
            for part, prob, row_dot in zip(weighted, probs, row_dots)
        ]
        outs = [dot(score, rows_here, 1, 0) * scale for score, rows_here in zip(scores_low, listed)]
        for n in range(len(units)):
            both = jnp.concatenate([scores_low[n], probs_low[n]], axis=0)
            mates = jnp.concatenate([queries[n], grads[n]], axis=0)
            kv_grad = dot(both, mates, 0, 0)
            for j in range(LISTED):
                at = pl.ds(offs[n][j], BLOCK)
                dkv_ref[at, :] += kv_grad[j * BLOCK : (j + 1) * BLOCK]
        for g in range(GROUP):
            dq_ref[t * GROUP + g] = jnp.where(
                left, outs[2 * g], pltpu.roll(outs[2 * g + 1], DH, 1)
            ).astype(bf16)
        return carry

    lax.fori_loop(0, lanes // GROUP, step, 0)
    held = own_ref.shape[0]
    own_ref[...] = dkv_ref[:held, :]
    away_ref[...] = dkv_ref[held:, :].astype(bf16)


def message_kernel(own_ref, other_ref, dq_ref, msg_ref):
    lanes, record = msg_ref.shape[0], msg_ref.shape[1]
    part_rows = 2 * record // 3

    def step(i, carry):
        at = pl.ds(pl.multiple_of(i * part_rows, part_rows), part_rows)
        total = own_ref[at, :]
        for k in range(other_ref.shape[0]):
            total += other_ref[k, at, :].astype(f32)
        msg_ref[i, :part_rows, :] = total.astype(bf16)
        msg_ref[i, part_rows:, :] = dq_ref[i]
        return carry

    lax.fori_loop(0, lanes, step, 0)


def pack_kernel(share, low_ref, near_ref, far_ref, msg_ref, rows_ref):
    lanes, record = msg_ref.shape[0], msg_ref.shape[1]
    heads = lanes // share
    feat = heads * DH
    part_rows = 2 * record // 3
    pair_rows = part_rows // 2
    half = D // 2
    for c in range(3):
        cols = slice(c * feat, (c + 1) * feat)
        rows_ref[:, cols] = dot(low_ref[:, :half], near_ref[:, cols], 1, 0) + dot(
            low_ref[:, half:], far_ref[:, cols], 1, 0
        )
    left = lax.broadcasted_iota(jnp.int32, (part_rows, 2 * DH), 1) < DH
    for h in range(0, heads, 2):
        for r in range(share):
            at = slice(r * part_rows, (r + 1) * part_rows)
            query, keys, vals = (
                rows_ref[at, c * feat + h * DH : c * feat + (h + 2) * DH] for c in range(3)
            )
            even, odd = h * share + r, (h + 1) * share + r
            msg_ref[even, :part_rows, :] = jnp.where(left, keys, pltpu.roll(vals, DH, 1)).astype(
                bf16
            )
            msg_ref[odd, :part_rows, :] = jnp.where(left, pltpu.roll(keys, DH, 1), vals).astype(
                bf16
            )
            first, second = query[:pair_rows], query[pair_rows:]
            over = left[:pair_rows]
            msg_ref[even, part_rows:, :] = jnp.where(over, first, pltpu.roll(second, DH, 1)).astype(
                bf16
            )
            msg_ref[odd, part_rows:, :] = jnp.where(over, pltpu.roll(first, DH, 1), second).astype(
                bf16
            )


def unpack_pairs(read, heads, share, pair_rows, write):
    left = lax.broadcasted_iota(jnp.int32, (pair_rows, 2 * DH), 1) < DH
    for h in range(0, heads, 2):
        cols = slice(h * DH, (h + 2) * DH)
        for r in range(share):
            even, odd = read(h * share + r), read((h + 1) * share + r)
            base = 2 * r * pair_rows
            first = jnp.where(left, even, pltpu.roll(odd, DH, 1))
            second = jnp.where(left, pltpu.roll(even, DH, 1), odd)
            write(slice(base, base + pair_rows), cols, first)
            write(slice(base + pair_rows, base + 2 * pair_rows), cols, second)


def project_kernel(share, pairs_ref, proj_ref, ctx_ref, out_ref):
    heads, pair_rows = pairs_ref.shape[0] // share, pairs_ref.shape[1]

    def write(rows, cols, value):
        ctx_ref[rows, cols] = value.astype(bf16)

    unpack_pairs(lambda n: pairs_ref[n].astype(f32), heads, share, pair_rows, write)
    out_ref[...] = dot(ctx_ref[...], proj_ref[...], 1, 1).astype(bf16)


def dctx_kernel(share, low_ref, proj_ref, pairs_ref):
    heads, pair_rows = pairs_ref.shape[0] // share, pairs_ref.shape[1]
    left = lax.broadcasted_iota(jnp.int32, (pair_rows, 2 * DH), 1) < DH
    grad = dot(low_ref[...], proj_ref[...], 1, 0)
    for h in range(0, heads, 2):
        cols = slice(h * DH, (h + 2) * DH)
        for r in range(share):
            base = 2 * r * pair_rows
            first = grad[base : base + pair_rows, cols]
            second = grad[base + pair_rows : base + 2 * pair_rows, cols]
            pairs_ref[h * share + r] = jnp.where(left, first, pltpu.roll(second, DH, 1)).astype(
                bf16
            )
            pairs_ref[(h + 1) * share + r] = jnp.where(
                left, pltpu.roll(first, DH, 1), second
            ).astype(bf16)


def one_grad_kernel(share, msg_ref, near_ref, far_ref, unit_ref, place_ref, out_ref, late_ref, rows_ref):
    lanes, record = msg_ref.shape[0], msg_ref.shape[1]
    heads = lanes // share
    feat = heads * DH
    part_rows = 2 * record // 3
    pair_rows = part_rows // 2

    def write(rows, cols, value):
        rows_ref[rows, cols] = value.astype(bf16)

    unpack_pairs(
        lambda n: msg_ref[n, part_rows:, :].astype(f32), heads, share, pair_rows, write
    )
    left = lax.broadcasted_iota(jnp.int32, (part_rows, 2 * DH), 1) < DH
    for h in range(0, heads, 2):
        for r in range(share):
            even = msg_ref[h * share + r, :part_rows, :].astype(f32)
            odd = msg_ref[(h + 1) * share + r, :part_rows, :].astype(f32)
            at = slice(r * part_rows, (r + 1) * part_rows)
            keys = jnp.where(left, even, pltpu.roll(odd, DH, 1))
            vals = jnp.where(left, pltpu.roll(even, DH, 1), odd)
            rows_ref[at, feat + h * DH : feat + (h + 2) * DH] = keys.astype(bf16)
            rows_ref[at, 2 * feat + h * DH : 2 * feat + (h + 2) * DH] = vals.astype(bf16)
    half = D // 2
    cols = slice(0, rows_ref.shape[1])
    out_ref[:, :half] = dot(rows_ref[...], near_ref[:, cols], 1, 1).astype(bf16)
    out_ref[:, half:] = dot(rows_ref[...], far_ref[:, cols], 1, 1).astype(bf16)
    grad = out_ref[...].astype(f32)
    gain = jnp.sum(grad * unit_ref[...], axis=0, keepdims=True)
    shift = jnp.sum(grad, axis=0, keepdims=True)
    sums = jnp.concatenate([gain, shift, jnp.zeros((14, D), f32)], axis=0)
    total = 0.0
    for _ in range(3):
        low = sums.astype(bf16)
        total += dot(low, place_ref[...], 1, 1)
        sums = sums - low.astype(f32)
    late_ref[...] = total


def weight_grad_kernel(lhs_a, rhs_a, lhs_b, rhs_b, out_ref, *, first):
    at = pl.program_id(0)

    @pl.when(at < first)
    def _():
        out_ref[...] = dot(lhs_a[...], rhs_a[...], 0, 0).astype(bf16)

    @pl.when(at >= first)
    def _():
        out_ref[...] = dot(lhs_b[...], rhs_b[...], 0, 0).astype(bf16)


def last_grad_kernel(lhs, rhs, whole_ref, out_ref):
    out_ref[...] = dot(lhs[...], rhs[...], 0, 0).astype(bf16)


VMEM_LIMIT = 48 * 1024 * 1024


def in_smem():
    return pl.BlockSpec(memory_space=pltpu.SMEM)


def call(kernel, outs, specs, scratch=(), out_specs=None):
    return pl.pallas_call(
        kernel,
        grid=(1,),
        out_shape=outs,
        in_specs=specs,
        out_specs=jax.tree.map(lambda o: whole(o.shape), outs) if out_specs is None else out_specs,
        scratch_shapes=list(scratch),
        compiler_params=pltpu.CompilerParams(vmem_limit_bytes=VMEM_LIMIT),
    )


def whole(shape):
    return pl.BlockSpec(tuple(shape), lambda i: (0,) * len(shape))


def array(shape, dtype=bf16):
    return jax.ShapeDtypeStruct(shape, dtype)


def ffn_weight_grads(first, second, aside, more):
    units = first[1].shape[1]
    block = min(512, units)
    counts = (units // block, (units - aside) // block)
    specs = []
    for start, skip, count, (lhs, rhs) in (
        (0, 0, counts[0], first),
        (counts[0], aside // block, counts[1], second),
    ):
        specs.append(whole(lhs.shape))
        specs.append(
            pl.BlockSpec(
                (rhs.shape[0], block),
                lambda i, start=start, skip=skip, count=count: (
                    0,
                    jnp.clip(i - start, 0, count - 1) + skip,
                ),
            )
        )
    width = 2 * units - aside
    return pl.pallas_call(
        functools.partial(weight_grad_kernel, first=counts[0]),
        grid=(sum(counts),),
        out_shape=array((D, width + more)),
        in_specs=specs,
        out_specs=pl.BlockSpec((D, block), lambda i: (0, i)),
        compiler_params=pltpu.CompilerParams(vmem_limit_bytes=VMEM_LIMIT),
        cost_estimate=pl.CostEstimate(
            flops=2 * D * width * first[1].shape[0], bytes_accessed=2 * D * width, transcendentals=0
        ),
    )(*first, *second)


def last_weight_grad(lhs, rhs, into):
    block = rhs.shape[1]
    return pl.pallas_call(
        last_grad_kernel,
        grid=(1,),
        out_shape=array(into.shape),
        in_specs=[whole(lhs.shape), whole(rhs.shape), pl.BlockSpec(memory_space=pl.ANY)],
        out_specs=pl.BlockSpec((D, block), lambda i: (0, into.shape[1] // block - 1)),
        input_output_aliases={2: 0},
        compiler_params=pltpu.CompilerParams(vmem_limit_bytes=VMEM_LIMIT),
    )(lhs, rhs, into)


def body(
    layer_input,
    output_grad,
    random_pick,
    doc_blocks,
    last_fill,
    shard_owner,
    qkv_weight,
    qkv_first,
    qkv_second,
    proj_weight,
    proj_first,
    proj_second,
    up_weight,
    up_first,
    up_second,
    down_weight,
    down_first,
    down_second,
    vec_params,
    vec_first,
    vec_second,
):
    lanes = lax.axis_size("seq")
    lane_index = lax.axis_index("seq")
    head_groups = lax.axis_size("head")
    head_index = lax.axis_index("head")
    slots = layer_input.shape[0]
    heads = random_pick.shape[2]
    feat = heads * DH
    units = up_weight.shape[1]
    rows = slots * BLOCK
    block_total = slots * lanes
    share = lanes // heads
    part_rows = rows // share
    pair_rows = part_rows // 2
    my_part = lane_index % share
    my_head = lane_index // share
    width = D // lanes

    qkv_mine = qkv_weight.astype(bf16).transpose(1, 0, 2).reshape(width, 3 * feat)
    pick_count = slots * heads * 3
    pick_rows = random_pick[:, 0].reshape(1, pick_count)
    pick_rows = jnp.concatenate([pick_rows // 256, pick_rows % 256], axis=0)
    pick_rows = jnp.pad(pick_rows, ((0, width - 2), (0, 2 * DH - pick_count)))
    qkv_mine = jnp.concatenate([qkv_mine, pick_rows.astype(bf16)], axis=1)
    first_mine = jnp.concatenate([up_weight.astype(bf16), proj_weight.astype(bf16).T], axis=1)
    first_full = lax.all_gather(first_mine, "seq", axis=0, tiled=True)
    up_full = first_full[:, :units]
    proj_block = pl.BlockSpec((D, feat), lambda i: (0, units // feat))

    column = jnp.arange(D, dtype=jnp.int32)
    owner = lookup(shard_owner, column // width)
    masks = jnp.array(relative_lanes(lanes), jnp.int32)
    position = jnp.sum(
        jnp.where(
            masks[None, :] == (owner ^ lane_index)[:, None], jnp.arange(lanes, dtype=jnp.int32), 0
        ),
        axis=1,
    )
    place = (owner * width + column % width)[:, None] == column[None, :]
    place_near = (position * width + column % width)[:, None] == column[None, :]
    place, place_near = place.astype(bf16), place_near.astype(bf16)
    rows_in = layer_input.reshape(rows, D)
    token_rows = dot(rows_in, place, 1, 0)
    grad_low = dot(output_grad.reshape(rows, D), place, 1, 0).astype(bf16)
    grad_rows = grad_low.astype(f32)
    exact = functools.partial(
        lax.dot_general, precision=lax.Precision.HIGHEST, preferred_element_type=f32
    )
    ahead = (((1,), (0,)), ((), ()))
    back = (((1,), (1,)), ((), ()))
    vec_rows = exact(vec_params[:5], place.astype(f32), ahead)
    vec_near = exact(vec_params[:2], place_near.astype(f32), ahead)
    up_bias = lax.dynamic_slice_in_dim(vec_params[5:].reshape(FF), head_index * units, units)

    normed_one, unit_one, scale_one = norm_rows(
        dot(rows_in, place_near, 1, 0), vec_near[0], vec_near[1]
    )
    low_one = normed_one.astype(bf16)
    qkv_near, qkv_far, low_one = relative_gather(qkv_mine, low_one)
    half = D // 2
    record = part_rows + pair_rows
    message = call(
        functools.partial(pack_kernel, share),
        array((lanes, record, 2 * DH)),
        [whole((rows, D)), whole(qkv_near.shape), whole(qkv_far.shape)],
        [pltpu.VMEM((rows, 3 * feat), f32)],
    )(low_one, qkv_near, qkv_far)
    down_mine = down_weight.astype(bf16).T
    pick_bytes = [
        part.reshape(-1, width, 3 * feat + 2 * DH)[:, :2, 3 * feat : 3 * feat + pick_count]
        for part in (qkv_near, qkv_far)
    ]
    message, pick_bytes, down_mine = lax.optimization_barrier((message, pick_bytes, down_mine))
    down_full = lax.all_gather(down_mine, "seq", axis=0, tiled=True)
    received = lax.all_to_all(message, "seq", 0, 0, tiled=True)

    pick_bytes = jnp.concatenate(pick_bytes, axis=0).astype(f32).astype(jnp.int32)
    picks = (pick_bytes[:, 0] * 256 + pick_bytes[:, 1]).reshape(lanes, slots, heads, 3)
    picks = lax.dynamic_index_in_dim(picks, my_head, 2, keepdims=False)
    from_lane = jnp.arange(lanes, dtype=jnp.int32) ^ lane_index
    picks = jnp.sum(
        jnp.where((masks[None, :] == from_lane[:, None])[..., None, None], picks[None], 0), axis=1
    )

    doc_end = jnp.cumsum(doc_blocks)
    doc_start = doc_end - doc_blocks
    doc_length = (doc_blocks - 1) * BLOCK + last_fill
    half_slot = (my_part * part_rows + jnp.arange(2, dtype=jnp.int32) * pair_rows) // BLOCK
    query_ids = half_slot[None, :] * lanes + jnp.arange(lanes, dtype=jnp.int32)[:, None]
    pick_half = jnp.sum(
        jnp.where(
            (half_slot[:, None] == jnp.arange(slots, dtype=jnp.int32)[None, :])[None, :, :, None],
            picks[:, None],
            0,
        ),
        axis=2,
    )
    query_doc = owning_doc(doc_end, query_ids)
    doc_first = lookup(doc_start, query_doc)
    doc_count = lookup(doc_blocks, query_doc)
    query_length = lookup(doc_length, query_doc)
    key_ids = jnp.concatenate(
        [
            jnp.stack(
                [
                    (query_ids - 1) % block_total,
                    query_ids,
                    (query_ids + 1) % block_total,
                    doc_first,
                    (doc_first + 1) % block_total,
                ],
                axis=-1,
            ),
            doc_first[..., None] + pick_half % doc_count[..., None],
        ],
        axis=-1,
    )
    same_doc = owning_doc(doc_end, key_ids) == query_doc[..., None]
    live_count = jnp.where(
        same_doc, query_length[..., None] - (key_ids - doc_first[..., None]) * BLOCK, 0
    )
    token = jnp.arange(BLOCK, dtype=jnp.int32)
    bias = jnp.where(token < live_count[..., None], 0.0, masked_score).astype(f32)
    bias = bias.reshape(lanes, 2, LISTED * BLOCK)
    key_lane = key_ids % lanes
    key_slot = key_ids // lanes
    if part_rows >= BLOCK:
        part_slots = part_rows // BLOCK
        offsets = (((key_slot // part_slots) ^ my_part) * lanes + key_lane) * part_rows
        offsets += (key_slot % part_slots) * BLOCK
    else:
        offsets = (key_lane * slots + key_slot) * BLOCK
    offsets = offsets.reshape(lanes * 2, LISTED)
    received, offsets, bias = lax.optimization_barrier((received, offsets, bias))

    parts = jnp.arange(share, dtype=jnp.int32)
    sources = [received] + [xor_permute(received, "seq", k) for k in range(1, share)]
    if part_rows < BLOCK:
        kv_parts = jnp.stack([part[:, :part_rows] for part in sources])
        kv_parts = kv_parts[parts ^ my_part].transpose(1, 0, 2, 3)
        sources = [kv_parts.reshape(lanes, slots * BLOCK, 2 * DH)]
    kv_shape = (block_total * BLOCK, 2 * DH)
    pairs_shape = (lanes, pair_rows, 2 * DH)
    probs_shape = (lanes, 2, pair_rows, LISTED * BLOCK)

    attend_specs = [in_smem(), whole(received.shape)] + [whole(part.shape) for part in sources]
    ctx_pairs, probs = call(
        attend_kernel,
        (array(pairs_shape), array(probs_shape)),
        attend_specs + [whole(bias.shape)],
        [pltpu.VMEM(kv_shape, bf16)],
    )(offsets, received, *sources, bias)
    ctx_pairs = lax.all_to_all(ctx_pairs, "seq", 0, 0, tiled=True)

    context, attn_part = call(
        functools.partial(project_kernel, share),
        (array((rows, feat)), array((rows, D))),
        [whole(pairs_shape), proj_block],
    )(ctx_pairs, first_full)
    attn_sum = head_total(attn_part, head_other(attn_part))
    mid_rows = token_rows + attn_sum
    normed_two, unit_two, scale_two = norm_rows(mid_rows, vec_rows[2], vec_rows[3])
    low_two = normed_two.astype(bf16)
    hidden = dot(low_two, up_full, 1, 0) + up_bias
    active = gelu_tanh(hidden).astype(bf16)
    act_grad = dot(grad_low, down_full, 1, 0)
    hidden_grad = jax.vjp(gelu_tanh, hidden)[1](act_grad)[0]
    hidden_low = hidden_grad.astype(bf16)
    two_part = dot(hidden_low, up_full, 1, 1).astype(bf16)
    two_other = head_other(two_part)
    rest_grads = ffn_weight_grads((low_two, hidden_low), (grad_low, active), 0, feat)
    two_other, rest_grads = lax.optimization_barrier((two_other, rest_grads))
    two_grad = head_total(two_part, two_other)
    up_bias_grad = jnp.sum(hidden_grad, axis=0)

    mid_grad = grad_rows + norm_back(two_grad, unit_two, scale_two, vec_rows[2])
    attn_low = mid_grad.astype(bf16)
    dctx_pairs = call(
        functools.partial(dctx_kernel, share),
        array(pairs_shape),
        [whole((rows, D)), proj_block],
    )(attn_low, first_full)
    rest_grads = last_weight_grad(attn_low, context, rest_grads)
    rest_owned = lax.psum_scatter(rest_grads, "seq", scatter_dimension=0, tiled=True).astype(f32)
    dctx_pairs = lax.all_to_all(dctx_pairs, "seq", 0, 0, tiled=True)
    dctx_pairs, rest_grads = lax.optimization_barrier((dctx_pairs, rest_grads))
    held_rows = lanes * part_rows
    away_rows = kv_shape[0] - held_rows
    if part_rows < BLOCK:
        back_shapes = (kv_shape[0] // 2,) * 2
    else:
        back_shapes = (held_rows, away_rows)
    dq_pairs, dkv_own, dkv_away = call(
        attend_back_kernel,
        (
            array(pairs_shape),
            array((back_shapes[0], 2 * DH), f32),
            array((back_shapes[1], 2 * DH)),
        ),
        attend_specs + [whole(probs_shape), whole(pairs_shape)],
        [pltpu.VMEM(kv_shape, bf16), pltpu.VMEM(kv_shape, f32)],
    )(offsets, received, *sources, probs, dctx_pairs)
    if part_rows < BLOCK:
        dkv_parts = jnp.concatenate([dkv_own, dkv_away.astype(f32)], axis=0)
        dkv_parts = dkv_parts.reshape(lanes, share, part_rows, 2 * DH)
        dkv_parts = dkv_parts[:, parts ^ my_part].transpose(1, 0, 2, 3)
        dkv_own = dkv_parts[0].reshape(held_rows, 2 * DH)
        dkv_away = dkv_parts[1:].astype(bf16)
    dkv_away = dkv_away.reshape(share - 1, held_rows, 2 * DH)
    others = jnp.stack([xor_permute(dkv_away[k - 1], "seq", k) for k in range(1, share)])
    others, active = lax.optimization_barrier((others, active))
    message = call(
        message_kernel,
        array((lanes, record, 2 * DH)),
        [whole((held_rows, 2 * DH)), whole(others.shape), whole(pairs_shape)],
    )(dkv_own, others, dq_pairs)
    returned = lax.all_to_all(message, "seq", 0, 0, tiled=True)
    ffn_part = dot(active, down_full, 1, 1).astype(bf16)
    ffn_other = head_other(ffn_part)
    early_rows = jnp.stack(
        [jnp.sum(two_grad * unit_two, axis=0), jnp.sum(two_grad, axis=0), jnp.sum(grad_rows, axis=0)]
    )
    early_rows = exact(early_rows, place.astype(f32), back)
    early_rows = jnp.concatenate([early_rows, up_bias_grad.reshape(units // D, D)], axis=0)
    returned, ffn_other, early_rows = lax.optimization_barrier((returned, ffn_other, early_rows))
    result = (mid_rows + head_total(ffn_part, ffn_other) + vec_rows[4]).astype(bf16)
    one_part, late_rows, dqkv = call(
        functools.partial(one_grad_kernel, share),
        (array((rows, D)), array((16, D), f32), array((rows, 3 * feat))),
        [whole(message.shape), whole(qkv_near.shape), whole(qkv_far.shape)]
        + [whole((rows, D)), whole((D, D))],
    )(returned, qkv_near, qkv_far, unit_one, place_near)
    one_other = head_other(one_part)
    vec_sums = axis_sum(jnp.concatenate([late_rows[:2], early_rows], axis=0), "seq")
    late_rows = axis_sum(vec_sums[:2], "head")
    early_rows = vec_sums[2:]

    chunk = 3 * feat // CHUNKS
    far_sums, near_sums = [], []
    for c in range(CHUNKS):
        cols = dqkv[:, c * chunk : (c + 1) * chunk]
        far_sums.append(xor_permute(dot(low_one[:, half:], cols, 0, 0).astype(bf16), "seq", 1))
        near_sums.append(dot(low_one[:, :half], cols, 0, 0))
    qkv_owned = []
    for near_sum, far_sum in zip(near_sums, far_sums):
        kept, sent = y_parts(added(near_sum, [far_sum]))
        kept, sent = z_parts(added(kept, y_others(sent)))
        qkv_owned.append((kept, z_others(sent)))
    qkv_last = qkv_owned.pop()
    qkv_owned = [added(*pair) for pair in qkv_owned]
    one_grad = head_total(one_part, one_other)

    layer_output = lax.dot_general(result, place, back, preferred_element_type=f32).astype(bf16)
    input_grad = exact(mid_grad, place.astype(f32), back) + exact(
        norm_back(one_grad, unit_one, scale_one, vec_near[0]), place_near.astype(f32), back
    )
    bias_rows = early_rows[3:]
    step = 1
    while step < head_groups:
        other = xor_permute(bias_rows, "head", step)
        high = (head_index & step) != 0
        bias_rows = jnp.where(
            high,
            jnp.concatenate([other, bias_rows], axis=0),
            jnp.concatenate([bias_rows, other], axis=0),
        )
        step *= 2
    vec_grad = jnp.concatenate([late_rows, early_rows[:3], bias_rows], axis=0)
    up_grad = rest_owned[:, :units]
    down_grad = rest_owned[:, units : 2 * units].T
    proj_grad = rest_owned[:, 2 * units :].T
    proj_new, proj_first_new, proj_second_new = adam_step(
        proj_weight, proj_grad, proj_first, proj_second, rate_proj
    )
    up_new, up_first_new, up_second_new = adam_step(up_weight, up_grad, up_first, up_second, rate_up)
    down_new, down_first_new, down_second_new = adam_step(
        down_weight, down_grad, down_first, down_second, rate_down
    )
    qkv_last, up_new, down_new, proj_new = lax.optimization_barrier(
        (qkv_last, up_new, down_new, proj_new)
    )
    qkv_owned.append(added(*qkv_last))
    qkv_grad = jnp.concatenate(qkv_owned, axis=1).reshape(width, 3, feat).transpose(1, 0, 2)
    qkv_new, qkv_first_new, qkv_second_new = adam_step(
        qkv_weight, qkv_grad, qkv_first, qkv_second, rate_qkv
    )
    vec_new, vec_first_new, vec_second_new = adam_step(
        vec_params, vec_grad, vec_first, vec_second, rate_vector
    )
    return (
        layer_output.reshape(slots, BLOCK, D),
        input_grad.reshape(slots, BLOCK, D),
        qkv_new,
        qkv_first_new,
        qkv_second_new,
        qkv_new.astype(bf16),
        proj_new,
        proj_first_new,
        proj_second_new,
        proj_new.astype(bf16),
        up_new,
        up_first_new,
        up_second_new,
        up_new.astype(bf16),
        down_new,
        down_first_new,
        down_second_new,
        down_new.astype(bf16),
        vec_new,
        vec_first_new,
        vec_second_new,
    )


def solution(mesh):
    rows_by_seq = P(None, "seq", None)
    cols = P("head", "seq")
    ups = P("seq", "head")
    qkvs = P(None, "seq", "head")
    placed = (
        (rows_by_seq, rows_by_seq, P(None, "seq", "head", None), P(), P(), P())
        + (qkvs,) * 3
        + (cols,) * 3
        + (ups,) * 3
        + (cols,) * 3
        + (P(),) * 3
    )
    return jax.shard_map(
        body,
        mesh=mesh,
        in_specs=placed,
        out_specs=(rows_by_seq, rows_by_seq)
        + (qkvs,) * 4
        + (cols,) * 4
        + (ups,) * 4
        + (cols,) * 4
        + (P(),) * 3,
        check_vma=False,
    )
```

```python
import functools

import jax
import jax.numpy as jnp
from jax import lax
from jax.experimental import pallas as pl
from jax.experimental.pallas import tpu as pltpu
from jax.sharding import PartitionSpec as P

D = 1024
DH = 64
FF = 4096
BLOCK = 64
STEP = 10
LISTED = 8

eps_norm = 1e-05
masked_score = -1e30
beta_one = 0.9
beta_two = 0.999
eps_adam = 1e-08
decay_rate = 0.01
rate_qkv = 0.1
rate_proj = 1.0
rate_up = 0.1
rate_down = 0.05
rate_vector = 2.0

bf16 = jnp.bfloat16
f32 = jnp.float32


def lookup(index_table, index_rows):
    matches = index_rows[..., None] == jnp.arange(index_table.shape[0], dtype=jnp.int32)
    return jnp.sum(jnp.where(matches, index_table, 0), axis=-1)


def owning_doc(doc_end, block_ids):
    return jnp.sum((block_ids[..., None] >= doc_end).astype(jnp.int32), axis=-1)


def dot(lhs, rhs, lhs_dim, rhs_dim):
    return lax.dot_general(
        lhs, rhs, (((lhs_dim,), (rhs_dim,)), ((), ())), preferred_element_type=f32
    )


def norm_rows(token_rows, gain_row, bias_row):
    row_mean = jnp.mean(token_rows, axis=-1, keepdims=True)
    centred = token_rows - row_mean
    row_var = jnp.mean(centred * centred, axis=-1, keepdims=True)
    inv_scale = lax.rsqrt(row_var + eps_norm)
    unit_rows = centred * inv_scale
    return (unit_rows * gain_row + bias_row, unit_rows, inv_scale)


def norm_back(grad_in, unit_rows, inv_scale, gain_row):
    scaled = grad_in * gain_row
    first_mean = jnp.mean(scaled, axis=-1, keepdims=True)
    second_mean = jnp.mean(scaled * unit_rows, axis=-1, keepdims=True)
    return inv_scale * (scaled - first_mean - unit_rows * second_mean)


def gelu_tanh(values):
    return jax.nn.gelu(values, approximate=True)


def adam_step(param_old, gradient, first_old, second_old, step_rate):
    first_new = beta_one * first_old + (1.0 - beta_one) * gradient
    second_new = beta_two * second_old + (1.0 - beta_two) * gradient * gradient
    first_hat = first_new / (1.0 - beta_one**STEP)
    second_hat = second_new / (1.0 - beta_two**STEP)
    updated = param_old - step_rate * (
        first_hat / (jnp.sqrt(second_hat) + eps_adam) + decay_rate * param_old
    )
    return (updated, first_new, second_new)


def xor_permute(value, axis, mask):
    count = lax.axis_size(axis)
    return lax.ppermute(value, axis, [(i, i ^ mask) for i in range(count)])


def head_other(partial_low):
    return xor_permute(partial_low, "head", 1)


def head_total(partial_low, other):
    total = partial_low.astype(f32) + other.astype(f32)
    step = 2
    while step < lax.axis_size("head"):
        total = total + xor_permute(total, "head", step)
        step *= 2
    return total


def axis_sum(value, axis):
    step = 1
    while step < lax.axis_size(axis):
        value = value + xor_permute(value, axis, step)
        step *= 2
    return value


def lane_cuts(lanes):
    chips = lanes // 2
    ys = 1 << ((chips.bit_length() - 1) // 2)
    return 2, ys, chips // ys


def z_order(zs):
    return list(range(zs))


def relative_lanes(lanes):
    cores, ys, zs = lane_cuts(lanes)
    return [
        (kz * ys + ky) * cores + kc
        for kc in range(cores)
        for ky in range(ys)
        for kz in z_order(zs)
    ]


def relative_gather(mine, ready):
    cores, ys, zs = lane_cuts(lax.axis_size("seq"))
    column = [xor_permute(mine, "seq", kz * ys * cores) if kz else mine for kz in z_order(zs)]
    pieces = list(column)
    for ky in range(1, ys):
        pieces += [xor_permute(piece, "seq", ky * cores) for piece in column]
    near = jnp.concatenate(pieces, axis=0)
    near, ready = lax.optimization_barrier((near, ready))
    return near, xor_permute(near, "seq", 1), ready


def y_parts(total):
    _, ys, _ = lane_cuts(lax.axis_size("seq"))
    size = total.shape[0] // ys
    return total[:size], [total[k * size : (k + 1) * size].astype(bf16) for k in range(1, ys)]


def y_others(sent):
    cores, _, _ = lane_cuts(lax.axis_size("seq"))
    return [xor_permute(part, "seq", (k + 1) * cores) for k, part in enumerate(sent)]


def z_parts(total):
    _, _, zs = lane_cuts(lax.axis_size("seq"))
    size = total.shape[0] // zs
    at = {kz: total[i * size : (i + 1) * size] for i, kz in enumerate(z_order(zs))}
    return at[0], [at[kz].astype(bf16) for kz in range(1, zs)]


def z_others(sent):
    cores, ys, _ = lane_cuts(lax.axis_size("seq"))
    return [xor_permute(part, "seq", (k + 1) * ys * cores) for k, part in enumerate(sent)]


def added(kept, others):
    for other in others:
        kept = kept + other.astype(f32)
    return kept


GROUP = 8
CHUNKS = 2


def fill_rows(source_refs, kv_ref):
    start = 0
    for source_ref in source_refs:
        count = source_ref.shape[0]
        size = kv_ref.shape[0] // (count * len(source_refs))

        def copy(i, carry, start=start, size=size, source_ref=source_ref):
            at = pl.ds(pl.multiple_of(start + i * size, size), size)
            kv_ref[at, :] = source_ref[i, :size, :]
            return carry

        lax.fori_loop(0, count, copy, 0)
        start += count * size


def attend_kernel(off_ref, record_ref, *refs):
    *source_refs, bias_ref, ctx_ref, prob_ref, kv_ref = refs
    lanes, rows = ctx_ref.shape[0], ctx_ref.shape[1]
    first = record_ref.shape[1] - rows
    left = lax.broadcasted_iota(jnp.int32, (rows, 2 * DH), 1) < DH
    scale = DH**-0.5
    fill_rows(source_refs, kv_ref)

    def step(t, carry):
        units = [(t * GROUP + g, half) for g in range(GROUP) for half in range(2)]
        listed, scores = [], []
        for i, half in units:
            q_pair = record_ref[i, first:, :].astype(f32) * scale
            q_one = q_pair if half == 0 else pltpu.roll(q_pair, DH, 1)
            q_one = jnp.where(left, q_one, 0.0).astype(bf16)
            rows_here = jnp.concatenate(
                [
                    kv_ref[pl.ds(pl.multiple_of(off_ref[2 * i + half, j], BLOCK), BLOCK), :]
                    for j in range(LISTED)
                ],
                axis=0,
            )
            listed.append(rows_here)
            scores.append(dot(q_one, rows_here, 1, 1) + bias_ref[i, half : half + 1, :])
        tops = [jnp.max(score, axis=1, keepdims=True) for score in scores]
        grown = [jnp.exp(score - top) for score, top in zip(scores, tops)]
        totals = [jnp.sum(part, axis=1, keepdims=True) for part in grown]
        probs = [(part * (1.0 / total)).astype(bf16) for part, total in zip(grown, totals)]
        outs = []
        for (i, half), prob, rows_here in zip(units, probs, listed):
            prob_ref[i, half] = prob
            outs.append(dot(prob, rows_here, 1, 0))
        for g in range(GROUP):
            ctx_ref[t * GROUP + g] = jnp.where(
                left, pltpu.roll(outs[2 * g], DH, 1), outs[2 * g + 1]
            ).astype(bf16)
        return carry

    lax.fori_loop(0, lanes // GROUP, step, 0)


def attend_back_kernel(off_ref, record_ref, *refs):
    *source_refs, prob_ref, dctx_ref, dq_ref, own_ref, away_ref, kv_ref, dkv_ref = refs
    lanes, rows = dq_ref.shape[0], dq_ref.shape[1]
    first = record_ref.shape[1] - rows
    left = lax.broadcasted_iota(jnp.int32, (rows, 2 * DH), 1) < DH
    scale = DH**-0.5
    fill_rows(source_refs, kv_ref)
    dkv_ref[...] = jnp.zeros_like(dkv_ref)

    def step(t, carry):
        units = [(t * GROUP + g, half) for g in range(GROUP) for half in range(2)]
        queries, grads, offs, listed, prob_grads = [], [], [], [], []
        for i, half in units:
            q_pair = record_ref[i, first:, :].astype(f32) * scale
            d_pair = dctx_ref[i].astype(f32)
            q_one = q_pair if half == 0 else pltpu.roll(q_pair, DH, 1)
            queries.append(jnp.where(left, q_one, 0.0).astype(bf16))
            d_one = pltpu.roll(d_pair, DH, 1) if half == 0 else d_pair
            grads.append(jnp.where(left, 0.0, d_one).astype(bf16))
            offs.append(
                [pl.multiple_of(off_ref[2 * i + half, j], BLOCK) for j in range(LISTED)]
            )
            listed.append(
                jnp.concatenate([kv_ref[pl.ds(o, BLOCK), :] for o in offs[-1]], axis=0)
            )
            prob_grads.append(dot(grads[-1], listed[-1], 1, 1))
        probs_low = [prob_ref[i, half] for i, half in units]
        probs = [prob.astype(f32) for prob in probs_low]
        weighted = [prob * grad for prob, grad in zip(probs, prob_grads)]
        row_dots = [jnp.sum(part, axis=1, keepdims=True) for part in weighted]
        scores_low = [
            (part - prob * row_dot).astype(bf16)
            for part, prob, row_dot in zip(weighted, probs, row_dots)
        ]
        outs = [dot(score, rows_here, 1, 0) * scale for score, rows_here in zip(scores_low, listed)]
        for n in range(len(units)):
            both = jnp.concatenate([scores_low[n], probs_low[n]], axis=0)
            mates = jnp.concatenate([queries[n], grads[n]], axis=0)
            kv_grad = dot(both, mates, 0, 0)
            for j in range(LISTED):
                at = pl.ds(offs[n][j], BLOCK)
                dkv_ref[at, :] += kv_grad[j * BLOCK : (j + 1) * BLOCK]
        for g in range(GROUP):
            dq_ref[t * GROUP + g] = jnp.where(
                left, outs[2 * g], pltpu.roll(outs[2 * g + 1], DH, 1)
            ).astype(bf16)
        return carry

    lax.fori_loop(0, lanes // GROUP, step, 0)
    held = own_ref.shape[0]
    own_ref[...] = dkv_ref[:held, :]
    away_ref[...] = dkv_ref[held:, :].astype(bf16)


def message_kernel(own_ref, other_ref, dq_ref, msg_ref):
    lanes, record = msg_ref.shape[0], msg_ref.shape[1]
    part_rows = 2 * record // 3

    def step(i, carry):
        at = pl.ds(pl.multiple_of(i * part_rows, part_rows), part_rows)
        total = own_ref[at, :]
        for k in range(other_ref.shape[0]):
            total += other_ref[k, at, :].astype(f32)
        msg_ref[i, :part_rows, :] = total.astype(bf16)
        msg_ref[i, part_rows:, :] = dq_ref[i]
        return carry

    lax.fori_loop(0, lanes, step, 0)


def pack_kernel(share, low_ref, near_ref, far_ref, msg_ref, rows_ref):
    lanes, record = msg_ref.shape[0], msg_ref.shape[1]
    heads = lanes // share
    feat = heads * DH
    part_rows = 2 * record // 3
    pair_rows = part_rows // 2
    half = D // 2
    for c in range(3):
        cols = slice(c * feat, (c + 1) * feat)
        rows_ref[:, cols] = dot(low_ref[:, :half], near_ref[:, cols], 1, 0) + dot(
            low_ref[:, half:], far_ref[:, cols], 1, 0
        )
    left = lax.broadcasted_iota(jnp.int32, (part_rows, 2 * DH), 1) < DH
    for h in range(0, heads, 2):
        for r in range(share):
            at = slice(r * part_rows, (r + 1) * part_rows)
            query, keys, vals = (
                rows_ref[at, c * feat + h * DH : c * feat + (h + 2) * DH] for c in range(3)
            )
            even, odd = h * share + r, (h + 1) * share + r
            msg_ref[even, :part_rows, :] = jnp.where(left, keys, pltpu.roll(vals, DH, 1)).astype(
                bf16
            )
            msg_ref[odd, :part_rows, :] = jnp.where(left, pltpu.roll(keys, DH, 1), vals).astype(
                bf16
            )
            first, second = query[:pair_rows], query[pair_rows:]
            over = left[:pair_rows]
            msg_ref[even, part_rows:, :] = jnp.where(over, first, pltpu.roll(second, DH, 1)).astype(
                bf16
            )
            msg_ref[odd, part_rows:, :] = jnp.where(over, pltpu.roll(first, DH, 1), second).astype(
                bf16
            )


def unpack_pairs(read, heads, share, pair_rows, write):
    left = lax.broadcasted_iota(jnp.int32, (pair_rows, 2 * DH), 1) < DH
    for h in range(0, heads, 2):
        cols = slice(h * DH, (h + 2) * DH)
        for r in range(share):
            even, odd = read(h * share + r), read((h + 1) * share + r)
            base = 2 * r * pair_rows
            first = jnp.where(left, even, pltpu.roll(odd, DH, 1))
            second = jnp.where(left, pltpu.roll(even, DH, 1), odd)
            write(slice(base, base + pair_rows), cols, first)
            write(slice(base + pair_rows, base + 2 * pair_rows), cols, second)


def project_kernel(share, pairs_ref, proj_ref, ctx_ref, out_ref):
    heads, pair_rows = pairs_ref.shape[0] // share, pairs_ref.shape[1]

    def write(rows, cols, value):
        ctx_ref[rows, cols] = value.astype(bf16)

    unpack_pairs(lambda n: pairs_ref[n].astype(f32), heads, share, pair_rows, write)
    out_ref[...] = dot(ctx_ref[...], proj_ref[...], 1, 1).astype(bf16)


def dctx_kernel(share, low_ref, proj_ref, pairs_ref):
    heads, pair_rows = pairs_ref.shape[0] // share, pairs_ref.shape[1]
    left = lax.broadcasted_iota(jnp.int32, (pair_rows, 2 * DH), 1) < DH
    grad = dot(low_ref[...], proj_ref[...], 1, 0)
    for h in range(0, heads, 2):
        cols = slice(h * DH, (h + 2) * DH)
        for r in range(share):
            base = 2 * r * pair_rows
            first = grad[base : base + pair_rows, cols]
            second = grad[base + pair_rows : base + 2 * pair_rows, cols]
            pairs_ref[h * share + r] = jnp.where(left, first, pltpu.roll(second, DH, 1)).astype(
                bf16
            )
            pairs_ref[(h + 1) * share + r] = jnp.where(
                left, pltpu.roll(first, DH, 1), second
            ).astype(bf16)


def one_grad_kernel(share, msg_ref, near_ref, far_ref, unit_ref, place_ref, out_ref, late_ref, rows_ref):
    lanes, record = msg_ref.shape[0], msg_ref.shape[1]
    heads = lanes // share
    feat = heads * DH
    part_rows = 2 * record // 3
    pair_rows = part_rows // 2

    def write(rows, cols, value):
        rows_ref[rows, cols] = value.astype(bf16)

    unpack_pairs(
        lambda n: msg_ref[n, part_rows:, :].astype(f32), heads, share, pair_rows, write
    )
    left = lax.broadcasted_iota(jnp.int32, (part_rows, 2 * DH), 1) < DH
    for h in range(0, heads, 2):
        for r in range(share):
            even = msg_ref[h * share + r, :part_rows, :].astype(f32)
            odd = msg_ref[(h + 1) * share + r, :part_rows, :].astype(f32)
            at = slice(r * part_rows, (r + 1) * part_rows)
            keys = jnp.where(left, even, pltpu.roll(odd, DH, 1))
            vals = jnp.where(left, pltpu.roll(even, DH, 1), odd)
            rows_ref[at, feat + h * DH : feat + (h + 2) * DH] = keys.astype(bf16)
            rows_ref[at, 2 * feat + h * DH : 2 * feat + (h + 2) * DH] = vals.astype(bf16)
    half = D // 2
    cols = slice(0, rows_ref.shape[1])
    out_ref[:, :half] = dot(rows_ref[...], near_ref[:, cols], 1, 1).astype(bf16)
    out_ref[:, half:] = dot(rows_ref[...], far_ref[:, cols], 1, 1).astype(bf16)
    grad = out_ref[...].astype(f32)
    gain = jnp.sum(grad * unit_ref[...], axis=0, keepdims=True)
    shift = jnp.sum(grad, axis=0, keepdims=True)
    sums = jnp.concatenate([gain, shift, jnp.zeros((14, D), f32)], axis=0)
    total = 0.0
    for _ in range(3):
        low = sums.astype(bf16)
        total += dot(low, place_ref[...], 1, 1)
        sums = sums - low.astype(f32)
    late_ref[...] = total


def weight_grad_kernel(lhs_a, rhs_a, lhs_b, rhs_b, out_ref, *, first):
    at = pl.program_id(0)

    @pl.when(at < first)
    def _():
        out_ref[...] = dot(lhs_a[...], rhs_a[...], 0, 0).astype(bf16)

    @pl.when(at >= first)
    def _():
        out_ref[...] = dot(lhs_b[...], rhs_b[...], 0, 0).astype(bf16)


VMEM_LIMIT = 48 * 1024 * 1024


def in_smem():
    return pl.BlockSpec(memory_space=pltpu.SMEM)


def call(kernel, outs, specs, scratch=(), out_specs=None):
    return pl.pallas_call(
        kernel,
        grid=(1,),
        out_shape=outs,
        in_specs=specs,
        out_specs=jax.tree.map(lambda o: whole(o.shape), outs) if out_specs is None else out_specs,
        scratch_shapes=list(scratch),
        compiler_params=pltpu.CompilerParams(vmem_limit_bytes=VMEM_LIMIT),
    )


def whole(shape):
    return pl.BlockSpec(tuple(shape), lambda i: (0,) * len(shape))


def array(shape, dtype=bf16):
    return jax.ShapeDtypeStruct(shape, dtype)


def ffn_weight_grads(first, second, aside, more):
    units = first[1].shape[1]
    block = min(512, units)
    counts = (units // block, (units - aside) // block)
    specs = []
    for start, skip, count, (lhs, rhs) in (
        (0, 0, counts[0], first),
        (counts[0], aside // block, counts[1], second),
    ):
        specs.append(whole(lhs.shape))
        specs.append(
            pl.BlockSpec(
                (rhs.shape[0], block),
                lambda i, start=start, skip=skip, count=count: (
                    0,
                    jnp.clip(i - start, 0, count - 1) + skip,
                ),
            )
        )
    width = 2 * units - aside
    return pl.pallas_call(
        functools.partial(weight_grad_kernel, first=counts[0]),
        grid=(sum(counts),),
        out_shape=array((D, width + more)),
        in_specs=specs,
        out_specs=pl.BlockSpec((D, block), lambda i: (0, i)),
        compiler_params=pltpu.CompilerParams(vmem_limit_bytes=VMEM_LIMIT),
        cost_estimate=pl.CostEstimate(
            flops=2 * D * width * first[1].shape[0], bytes_accessed=2 * D * width, transcendentals=0
        ),
    )(*first, *second)


def body(
    layer_input,
    output_grad,
    random_pick,
    doc_blocks,
    last_fill,
    shard_owner,
    qkv_weight,
    qkv_first,
    qkv_second,
    proj_weight,
    proj_first,
    proj_second,
    up_weight,
    up_first,
    up_second,
    down_weight,
    down_first,
    down_second,
    vec_params,
    vec_first,
    vec_second,
):
    lanes = lax.axis_size("seq")
    lane_index = lax.axis_index("seq")
    head_groups = lax.axis_size("head")
    head_index = lax.axis_index("head")
    slots = layer_input.shape[0]
    heads = random_pick.shape[2]
    feat = heads * DH
    units = up_weight.shape[1]
    rows = slots * BLOCK
    block_total = slots * lanes
    share = lanes // heads
    part_rows = rows // share
    pair_rows = part_rows // 2
    my_part = lane_index % share
    my_head = lane_index // share
    width = D // lanes

    qkv_mine = qkv_weight.astype(bf16).transpose(1, 0, 2).reshape(width, 3 * feat)
    pick_count = slots * heads * 3
    pick_rows = random_pick[:, 0].reshape(1, pick_count)
    pick_rows = jnp.concatenate([pick_rows // 256, pick_rows % 256], axis=0)
    pick_rows = jnp.pad(pick_rows, ((0, width - 2), (0, 2 * DH - pick_count)))
    qkv_mine = jnp.concatenate([qkv_mine, pick_rows.astype(bf16)], axis=1)
    first_mine = jnp.concatenate([up_weight.astype(bf16), proj_weight.astype(bf16).T], axis=1)
    first_full = lax.all_gather(first_mine, "seq", axis=0, tiled=True)
    up_full = first_full[:, :units]
    proj_block = pl.BlockSpec((D, feat), lambda i: (0, units // feat))

    column = jnp.arange(D, dtype=jnp.int32)
    owner = lookup(shard_owner, column // width)
    masks = jnp.array(relative_lanes(lanes), jnp.int32)
    position = jnp.sum(
        jnp.where(
            masks[None, :] == (owner ^ lane_index)[:, None], jnp.arange(lanes, dtype=jnp.int32), 0
        ),
        axis=1,
    )
    place = (owner * width + column % width)[:, None] == column[None, :]
    place_near = (position * width + column % width)[:, None] == column[None, :]
    place, place_near = place.astype(bf16), place_near.astype(bf16)
    rows_in = layer_input.reshape(rows, D)
    token_rows = dot(rows_in, place, 1, 0)
    grad_low = dot(output_grad.reshape(rows, D), place, 1, 0).astype(bf16)
    grad_rows = grad_low.astype(f32)
    exact = functools.partial(
        lax.dot_general, precision=lax.Precision.HIGHEST, preferred_element_type=f32
    )
    ahead = (((1,), (0,)), ((), ()))
    back = (((1,), (1,)), ((), ()))
    vec_rows = exact(vec_params[:5], place.astype(f32), ahead)
    vec_near = exact(vec_params[:2], place_near.astype(f32), ahead)
    up_bias = lax.dynamic_slice_in_dim(vec_params[5:].reshape(FF), head_index * units, units)

    normed_one, unit_one, scale_one = norm_rows(
        dot(rows_in, place_near, 1, 0), vec_near[0], vec_near[1]
    )
    low_one = normed_one.astype(bf16)
    qkv_near, qkv_far, low_one = relative_gather(qkv_mine, low_one)
    half = D // 2
    record = part_rows + pair_rows
    message = call(
        functools.partial(pack_kernel, share),
        array((lanes, record, 2 * DH)),
        [whole((rows, D)), whole(qkv_near.shape), whole(qkv_far.shape)],
        [pltpu.VMEM((rows, 3 * feat), f32)],
    )(low_one, qkv_near, qkv_far)
    down_mine = down_weight.astype(bf16).T
    pick_bytes = [
        part.reshape(-1, width, 3 * feat + 2 * DH)[:, :2, 3 * feat : 3 * feat + pick_count]
        for part in (qkv_near, qkv_far)
    ]
    message, pick_bytes, down_mine = lax.optimization_barrier((message, pick_bytes, down_mine))
    down_full = lax.all_gather(down_mine, "seq", axis=0, tiled=True)
    received = lax.all_to_all(message, "seq", 0, 0, tiled=True)

    pick_bytes = jnp.concatenate(pick_bytes, axis=0).astype(f32).astype(jnp.int32)
    picks = (pick_bytes[:, 0] * 256 + pick_bytes[:, 1]).reshape(lanes, slots, heads, 3)
    picks = lax.dynamic_index_in_dim(picks, my_head, 2, keepdims=False)
    from_lane = jnp.arange(lanes, dtype=jnp.int32) ^ lane_index
    picks = jnp.sum(
        jnp.where((masks[None, :] == from_lane[:, None])[..., None, None], picks[None], 0), axis=1
    )

    doc_end = jnp.cumsum(doc_blocks)
    doc_start = doc_end - doc_blocks
    doc_length = (doc_blocks - 1) * BLOCK + last_fill
    half_slot = (my_part * part_rows + jnp.arange(2, dtype=jnp.int32) * pair_rows) // BLOCK
    query_ids = half_slot[None, :] * lanes + jnp.arange(lanes, dtype=jnp.int32)[:, None]
    pick_half = jnp.sum(
        jnp.where(
            (half_slot[:, None] == jnp.arange(slots, dtype=jnp.int32)[None, :])[None, :, :, None],
            picks[:, None],
            0,
        ),
        axis=2,
    )
    query_doc = owning_doc(doc_end, query_ids)
    doc_first = lookup(doc_start, query_doc)
    doc_count = lookup(doc_blocks, query_doc)
    query_length = lookup(doc_length, query_doc)
    key_ids = jnp.concatenate(
        [
            jnp.stack(
                [
                    (query_ids - 1) % block_total,
                    query_ids,
                    (query_ids + 1) % block_total,
                    doc_first,
                    (doc_first + 1) % block_total,
                ],
                axis=-1,
            ),
            doc_first[..., None] + pick_half % doc_count[..., None],
        ],
        axis=-1,
    )
    same_doc = owning_doc(doc_end, key_ids) == query_doc[..., None]
    live_count = jnp.where(
        same_doc, query_length[..., None] - (key_ids - doc_first[..., None]) * BLOCK, 0
    )
    token = jnp.arange(BLOCK, dtype=jnp.int32)
    bias = jnp.where(token < live_count[..., None], 0.0, masked_score).astype(f32)
    bias = bias.reshape(lanes, 2, LISTED * BLOCK)
    key_lane = key_ids % lanes
    key_slot = key_ids // lanes
    if part_rows >= BLOCK:
        part_slots = part_rows // BLOCK
        offsets = (((key_slot // part_slots) ^ my_part) * lanes + key_lane) * part_rows
        offsets += (key_slot % part_slots) * BLOCK
    else:
        offsets = (key_lane * slots + key_slot) * BLOCK
    offsets = offsets.reshape(lanes * 2, LISTED)
    received, offsets, bias = lax.optimization_barrier((received, offsets, bias))

    parts = jnp.arange(share, dtype=jnp.int32)
    sources = [received] + [xor_permute(received, "seq", k) for k in range(1, share)]
    if part_rows < BLOCK:
        kv_parts = jnp.stack([part[:, :part_rows] for part in sources])
        kv_parts = kv_parts[parts ^ my_part].transpose(1, 0, 2, 3)
        sources = [kv_parts.reshape(lanes, slots * BLOCK, 2 * DH)]
    kv_shape = (block_total * BLOCK, 2 * DH)
    pairs_shape = (lanes, pair_rows, 2 * DH)
    probs_shape = (lanes, 2, pair_rows, LISTED * BLOCK)

    attend_specs = [in_smem(), whole(received.shape)] + [whole(part.shape) for part in sources]
    ctx_pairs, probs = call(
        attend_kernel,
        (array(pairs_shape), array(probs_shape)),
        attend_specs + [whole(bias.shape)],
        [pltpu.VMEM(kv_shape, bf16)],
    )(offsets, received, *sources, bias)
    ctx_pairs = lax.all_to_all(ctx_pairs, "seq", 0, 0, tiled=True)

    context, attn_part = call(
        functools.partial(project_kernel, share),
        (array((rows, feat)), array((rows, D))),
        [whole(pairs_shape), proj_block],
    )(ctx_pairs, first_full)
    attn_sum = head_total(attn_part, head_other(attn_part))
    mid_rows = token_rows + attn_sum
    normed_two, unit_two, scale_two = norm_rows(mid_rows, vec_rows[2], vec_rows[3])
    low_two = normed_two.astype(bf16)
    hidden = dot(low_two, up_full, 1, 0) + up_bias
    active = gelu_tanh(hidden).astype(bf16)
    act_grad = dot(grad_low, down_full, 1, 0)
    hidden_grad = jax.vjp(gelu_tanh, hidden)[1](act_grad)[0]
    hidden_low = hidden_grad.astype(bf16)
    two_part = dot(hidden_low, up_full, 1, 1).astype(bf16)
    two_other = head_other(two_part)
    ffn_grads = ffn_weight_grads((low_two, hidden_low), (grad_low, active), 0, 0)
    two_other, ffn_grads = lax.optimization_barrier((two_other, ffn_grads))
    ffn_owned = lax.psum_scatter(ffn_grads, "seq", scatter_dimension=0, tiled=True).astype(f32)
    two_grad = head_total(two_part, two_other)
    up_bias_grad = jnp.sum(hidden_grad, axis=0)

    mid_grad = grad_rows + norm_back(two_grad, unit_two, scale_two, vec_rows[2])
    attn_low = mid_grad.astype(bf16)
    dctx_pairs = call(
        functools.partial(dctx_kernel, share),
        array(pairs_shape),
        [whole((rows, D)), proj_block],
    )(attn_low, first_full)
    dctx_pairs = lax.all_to_all(dctx_pairs, "seq", 0, 0, tiled=True)
    dctx_pairs, ffn_grads = lax.optimization_barrier((dctx_pairs, ffn_grads))
    held_rows = lanes * part_rows
    away_rows = kv_shape[0] - held_rows
    if part_rows < BLOCK:
        back_shapes = (kv_shape[0] // 2,) * 2
    else:
        back_shapes = (held_rows, away_rows)
    dq_pairs, dkv_own, dkv_away = call(
        attend_back_kernel,
        (
            array(pairs_shape),
            array((back_shapes[0], 2 * DH), f32),
            array((back_shapes[1], 2 * DH)),
        ),
        attend_specs + [whole(probs_shape), whole(pairs_shape)],
        [pltpu.VMEM(kv_shape, bf16), pltpu.VMEM(kv_shape, f32)],
    )(offsets, received, *sources, probs, dctx_pairs)
    if part_rows < BLOCK:
        dkv_parts = jnp.concatenate([dkv_own, dkv_away.astype(f32)], axis=0)
        dkv_parts = dkv_parts.reshape(lanes, share, part_rows, 2 * DH)
        dkv_parts = dkv_parts[:, parts ^ my_part].transpose(1, 0, 2, 3)
        dkv_own = dkv_parts[0].reshape(held_rows, 2 * DH)
        dkv_away = dkv_parts[1:].astype(bf16)
    dkv_away = dkv_away.reshape(share - 1, held_rows, 2 * DH)
    others = jnp.stack([xor_permute(dkv_away[k - 1], "seq", k) for k in range(1, share)])
    others, active, attn_low = lax.optimization_barrier((others, active, attn_low))
    message = call(
        message_kernel,
        array((lanes, record, 2 * DH)),
        [whole((held_rows, 2 * DH)), whole(others.shape), whole(pairs_shape)],
    )(dkv_own, others, dq_pairs)
    returned = lax.all_to_all(message, "seq", 0, 0, tiled=True)
    attn_near = dot(attn_low, dot(place, place_near, 0, 0).astype(bf16), 1, 0).astype(bf16)
    proj_far = dot(attn_near[:, half:], context, 0, 0).astype(bf16)
    proj_sums = added(dot(attn_near[:, :half], context, 0, 0), [xor_permute(proj_far, "seq", 1)])
    proj_kept, proj_sent = y_parts(proj_sums)
    proj_other = y_others(proj_sent)
    ffn_part = dot(active, down_full, 1, 1).astype(bf16)
    ffn_other = head_other(ffn_part)
    early_rows = jnp.stack(
        [jnp.sum(two_grad * unit_two, axis=0), jnp.sum(two_grad, axis=0), jnp.sum(grad_rows, axis=0)]
    )
    early_rows = exact(early_rows, place.astype(f32), back)
    early_rows = jnp.concatenate([early_rows, up_bias_grad.reshape(units // D, D)], axis=0)
    returned, ffn_other, early_rows = lax.optimization_barrier((returned, ffn_other, early_rows))
    result = (mid_rows + head_total(ffn_part, ffn_other) + vec_rows[4]).astype(bf16)
    one_part, late_rows, dqkv = call(
        functools.partial(one_grad_kernel, share),
        (array((rows, D)), array((16, D), f32), array((rows, 3 * feat))),
        [whole(message.shape), whole(qkv_near.shape), whole(qkv_far.shape)]
        + [whole((rows, D)), whole((D, D))],
    )(returned, qkv_near, qkv_far, unit_one, place_near)
    one_other = head_other(one_part)
    vec_sums = jnp.concatenate([late_rows[:2], early_rows], axis=0)
    vec_sums, proj_other = lax.optimization_barrier((vec_sums, proj_other))
    proj_kept, proj_sent = z_parts(added(proj_kept, proj_other))
    proj_other = z_others(proj_sent)
    vec_sums = axis_sum(vec_sums, "seq")
    vec_sums, proj_other = lax.optimization_barrier((vec_sums, proj_other))
    proj_owned = added(proj_kept, proj_other)
    late_rows = axis_sum(vec_sums[:2], "head")
    early_rows = vec_sums[2:]

    chunk = 3 * feat // CHUNKS
    far_sums, near_sums = [], []
    for c in range(CHUNKS):
        cols = dqkv[:, c * chunk : (c + 1) * chunk]
        far_sums.append(xor_permute(dot(low_one[:, half:], cols, 0, 0).astype(bf16), "seq", 1))
        near_sums.append(dot(low_one[:, :half], cols, 0, 0))
    qkv_owned = []
    for near_sum, far_sum in zip(near_sums, far_sums):
        kept, sent = y_parts(added(near_sum, [far_sum]))
        kept, sent = z_parts(added(kept, y_others(sent)))
        qkv_owned.append((kept, z_others(sent)))
    qkv_last = qkv_owned.pop()
    qkv_owned = [added(*pair) for pair in qkv_owned]
    one_grad = head_total(one_part, one_other)

    layer_output = lax.dot_general(result, place, back, preferred_element_type=f32).astype(bf16)
    input_grad = exact(mid_grad, place.astype(f32), back) + exact(
        norm_back(one_grad, unit_one, scale_one, vec_near[0]), place_near.astype(f32), back
    )
    bias_rows = early_rows[3:]
    step = 1
    while step < head_groups:
        other = xor_permute(bias_rows, "head", step)
        high = (head_index & step) != 0
        bias_rows = jnp.where(
            high,
            jnp.concatenate([other, bias_rows], axis=0),
            jnp.concatenate([bias_rows, other], axis=0),
        )
        step *= 2
    vec_grad = jnp.concatenate([late_rows, early_rows[:3], bias_rows], axis=0)
    up_grad = ffn_owned[:, :units]
    down_grad = ffn_owned[:, units:].T
    proj_grad = proj_owned.T
    proj_new, proj_first_new, proj_second_new = adam_step(
        proj_weight, proj_grad, proj_first, proj_second, rate_proj
    )
    up_new, up_first_new, up_second_new = adam_step(up_weight, up_grad, up_first, up_second, rate_up)
    down_new, down_first_new, down_second_new = adam_step(
        down_weight, down_grad, down_first, down_second, rate_down
    )
    qkv_last, up_new, down_new, proj_new = lax.optimization_barrier(
        (qkv_last, up_new, down_new, proj_new)
    )
    qkv_owned.append(added(*qkv_last))
    qkv_grad = jnp.concatenate(qkv_owned, axis=1).reshape(width, 3, feat).transpose(1, 0, 2)
    qkv_new, qkv_first_new, qkv_second_new = adam_step(
        qkv_weight, qkv_grad, qkv_first, qkv_second, rate_qkv
    )
    vec_new, vec_first_new, vec_second_new = adam_step(
        vec_params, vec_grad, vec_first, vec_second, rate_vector
    )
    return (
        layer_output.reshape(slots, BLOCK, D),
        input_grad.reshape(slots, BLOCK, D),
        qkv_new,
        qkv_first_new,
        qkv_second_new,
        qkv_new.astype(bf16),
        proj_new,
        proj_first_new,
        proj_second_new,
        proj_new.astype(bf16),
        up_new,
        up_first_new,
        up_second_new,
        up_new.astype(bf16),
        down_new,
        down_first_new,
        down_second_new,
        down_new.astype(bf16),
        vec_new,
        vec_first_new,
        vec_second_new,
    )


def solution(mesh):
    rows_by_seq = P(None, "seq", None)
    cols = P("head", "seq")
    ups = P("seq", "head")
    qkvs = P(None, "seq", "head")
    placed = (
        (rows_by_seq, rows_by_seq, P(None, "seq", "head", None), P(), P(), P())
        + (qkvs,) * 3
        + (cols,) * 3
        + (ups,) * 3
        + (cols,) * 3
        + (P(),) * 3
    )
    return jax.shard_map(
        body,
        mesh=mesh,
        in_specs=placed,
        out_specs=(rows_by_seq, rows_by_seq)
        + (qkvs,) * 4
        + (cols,) * 4
        + (ups,) * 4
        + (cols,) * 4
        + (P(),) * 3,
        check_vma=False,
    )
```

```python
import functools

import jax
import jax.numpy as jnp
from jax import lax
from jax.experimental import pallas as pl
from jax.experimental.pallas import tpu as pltpu
from jax.sharding import PartitionSpec as P

D = 1024
DH = 64
FF = 4096
BLOCK = 64
STEP = 10
LISTED = 8

eps_norm = 1e-05
masked_score = -1e30
beta_one = 0.9
beta_two = 0.999
eps_adam = 1e-08
decay_rate = 0.01
rate_qkv = 0.1
rate_proj = 1.0
rate_up = 0.1
rate_down = 0.05
rate_vector = 2.0

bf16 = jnp.bfloat16
f32 = jnp.float32


def lookup(index_table, index_rows):
    matches = index_rows[..., None] == jnp.arange(index_table.shape[0], dtype=jnp.int32)
    return jnp.sum(jnp.where(matches, index_table, 0), axis=-1)


def owning_doc(doc_end, block_ids):
    return jnp.sum((block_ids[..., None] >= doc_end).astype(jnp.int32), axis=-1)


def dot(lhs, rhs, lhs_dim, rhs_dim):
    return lax.dot_general(
        lhs, rhs, (((lhs_dim,), (rhs_dim,)), ((), ())), preferred_element_type=f32
    )


def norm_rows(token_rows, gain_row, bias_row):
    row_mean = jnp.mean(token_rows, axis=-1, keepdims=True)
    centred = token_rows - row_mean
    row_var = jnp.mean(centred * centred, axis=-1, keepdims=True)
    inv_scale = lax.rsqrt(row_var + eps_norm)
    unit_rows = centred * inv_scale
    return (unit_rows * gain_row + bias_row, unit_rows, inv_scale)


def norm_back(grad_in, unit_rows, inv_scale, gain_row):
    scaled = grad_in * gain_row
    first_mean = jnp.mean(scaled, axis=-1, keepdims=True)
    second_mean = jnp.mean(scaled * unit_rows, axis=-1, keepdims=True)
    return inv_scale * (scaled - first_mean - unit_rows * second_mean)


def gelu_tanh(values):
    return jax.nn.gelu(values, approximate=True)


def adam_step(param_old, gradient, first_old, second_old, step_rate):
    first_new = beta_one * first_old + (1.0 - beta_one) * gradient
    second_new = beta_two * second_old + (1.0 - beta_two) * gradient * gradient
    first_hat = first_new / (1.0 - beta_one**STEP)
    second_hat = second_new / (1.0 - beta_two**STEP)
    updated = param_old - step_rate * (
        first_hat / (jnp.sqrt(second_hat) + eps_adam) + decay_rate * param_old
    )
    return (updated, first_new, second_new)


def xor_permute(value, axis, mask):
    count = lax.axis_size(axis)
    return lax.ppermute(value, axis, [(i, i ^ mask) for i in range(count)])


def head_other(partial_low):
    return xor_permute(partial_low, "head", 1)


def head_total(partial_low, other):
    total = partial_low.astype(f32) + other.astype(f32)
    step = 2
    while step < lax.axis_size("head"):
        total = total + xor_permute(total, "head", step)
        step *= 2
    return total


def axis_sum(value, axis):
    step = 1
    while step < lax.axis_size(axis):
        value = value + xor_permute(value, axis, step)
        step *= 2
    return value


def lane_cuts(lanes):
    chips = lanes // 2
    ys = 1 << ((chips.bit_length() - 1) // 2)
    return 2, ys, chips // ys


def z_order(zs):
    return list(range(zs))


def relative_lanes(lanes):
    cores, ys, zs = lane_cuts(lanes)
    return [
        (kz * ys + ky) * cores + kc
        for kc in range(cores)
        for ky in range(ys)
        for kz in z_order(zs)
    ]


def relative_gather(mine, ready):
    cores, ys, zs = lane_cuts(lax.axis_size("seq"))
    column = [xor_permute(mine, "seq", kz * ys * cores) if kz else mine for kz in z_order(zs)]
    pieces = list(column)
    for ky in range(1, ys):
        pieces += [xor_permute(piece, "seq", ky * cores) for piece in column]
    near = jnp.concatenate(pieces, axis=0)
    near, ready = lax.optimization_barrier((near, ready))
    return near, xor_permute(near, "seq", 1), ready


def y_parts(total):
    _, ys, _ = lane_cuts(lax.axis_size("seq"))
    size = total.shape[0] // ys
    return total[:size], [total[k * size : (k + 1) * size].astype(bf16) for k in range(1, ys)]


def y_others(sent):
    cores, _, _ = lane_cuts(lax.axis_size("seq"))
    return [xor_permute(part, "seq", (k + 1) * cores) for k, part in enumerate(sent)]


def z_parts(total):
    _, _, zs = lane_cuts(lax.axis_size("seq"))
    size = total.shape[0] // zs
    at = {kz: total[i * size : (i + 1) * size] for i, kz in enumerate(z_order(zs))}
    return at[0], [at[kz].astype(bf16) for kz in range(1, zs)]


def z_others(sent):
    cores, ys, _ = lane_cuts(lax.axis_size("seq"))
    return [xor_permute(part, "seq", (k + 1) * ys * cores) for k, part in enumerate(sent)]


def added(kept, others):
    for other in others:
        kept = kept + other.astype(f32)
    return kept


GROUP = 8
CHUNKS = 2


def fill_rows(source_refs, kv_ref):
    start = 0
    for source_ref in source_refs:
        count = source_ref.shape[0]
        size = kv_ref.shape[0] // (count * len(source_refs))

        def copy(i, carry, start=start, size=size, source_ref=source_ref):
            at = pl.ds(pl.multiple_of(start + i * size, size), size)
            kv_ref[at, :] = source_ref[i, :size, :]
            return carry

        lax.fori_loop(0, count, copy, 0)
        start += count * size


def attend_kernel(off_ref, record_ref, *refs):
    *source_refs, bias_ref, ctx_ref, prob_ref, kv_ref = refs
    lanes, rows = ctx_ref.shape[0], ctx_ref.shape[1]
    first = record_ref.shape[1] - rows
    left = lax.broadcasted_iota(jnp.int32, (rows, 2 * DH), 1) < DH
    scale = DH**-0.5
    fill_rows(source_refs, kv_ref)

    def step(t, carry):
        units = [(t * GROUP + g, half) for g in range(GROUP) for half in range(2)]
        listed, scores = [], []
        for i, half in units:
            q_pair = record_ref[i, first:, :].astype(f32) * scale
            q_one = q_pair if half == 0 else pltpu.roll(q_pair, DH, 1)
            q_one = jnp.where(left, q_one, 0.0).astype(bf16)
            rows_here = jnp.concatenate(
                [
                    kv_ref[pl.ds(pl.multiple_of(off_ref[2 * i + half, j], BLOCK), BLOCK), :]
                    for j in range(LISTED)
                ],
                axis=0,
            )
            listed.append(rows_here)
            scores.append(dot(q_one, rows_here, 1, 1) + bias_ref[i, half : half + 1, :])
        tops = [jnp.max(score, axis=1, keepdims=True) for score in scores]
        grown = [jnp.exp(score - top) for score, top in zip(scores, tops)]
        totals = [jnp.sum(part, axis=1, keepdims=True) for part in grown]
        probs = [(part * (1.0 / total)).astype(bf16) for part, total in zip(grown, totals)]
        outs = []
        for (i, half), prob, rows_here in zip(units, probs, listed):
            prob_ref[i, half] = prob
            outs.append(dot(prob, rows_here, 1, 0))
        for g in range(GROUP):
            ctx_ref[t * GROUP + g] = jnp.where(
                left, pltpu.roll(outs[2 * g], DH, 1), outs[2 * g + 1]
            ).astype(bf16)
        return carry

    lax.fori_loop(0, lanes // GROUP, step, 0)


def attend_back_kernel(off_ref, record_ref, *refs):
    *source_refs, prob_ref, dctx_ref, dq_ref, own_ref, away_ref, kv_ref, dkv_ref = refs
    lanes, rows = dq_ref.shape[0], dq_ref.shape[1]
    first = record_ref.shape[1] - rows
    left = lax.broadcasted_iota(jnp.int32, (rows, 2 * DH), 1) < DH
    scale = DH**-0.5
    fill_rows(source_refs, kv_ref)
    dkv_ref[...] = jnp.zeros_like(dkv_ref)

    def step(t, carry):
        units = [(t * GROUP + g, half) for g in range(GROUP) for half in range(2)]
        queries, grads, offs, listed, prob_grads = [], [], [], [], []
        for i, half in units:
            q_pair = record_ref[i, first:, :].astype(f32) * scale
            d_pair = dctx_ref[i].astype(f32)
            q_one = q_pair if half == 0 else pltpu.roll(q_pair, DH, 1)
            queries.append(jnp.where(left, q_one, 0.0).astype(bf16))
            d_one = pltpu.roll(d_pair, DH, 1) if half == 0 else d_pair
            grads.append(jnp.where(left, 0.0, d_one).astype(bf16))
            offs.append(
                [pl.multiple_of(off_ref[2 * i + half, j], BLOCK) for j in range(LISTED)]
            )
            listed.append(
                jnp.concatenate([kv_ref[pl.ds(o, BLOCK), :] for o in offs[-1]], axis=0)
            )
            prob_grads.append(dot(grads[-1], listed[-1], 1, 1))
        probs_low = [prob_ref[i, half] for i, half in units]
        probs = [prob.astype(f32) for prob in probs_low]
        weighted = [prob * grad for prob, grad in zip(probs, prob_grads)]
        row_dots = [jnp.sum(part, axis=1, keepdims=True) for part in weighted]
        scores_low = [
            (part - prob * row_dot).astype(bf16)
            for part, prob, row_dot in zip(weighted, probs, row_dots)
        ]
        outs = [dot(score, rows_here, 1, 0) * scale for score, rows_here in zip(scores_low, listed)]
        for n in range(len(units)):
            both = jnp.concatenate([scores_low[n], probs_low[n]], axis=0)
            mates = jnp.concatenate([queries[n], grads[n]], axis=0)
            kv_grad = dot(both, mates, 0, 0)
            for j in range(LISTED):
                at = pl.ds(offs[n][j], BLOCK)
                dkv_ref[at, :] += kv_grad[j * BLOCK : (j + 1) * BLOCK]
        for g in range(GROUP):
            dq_ref[t * GROUP + g] = jnp.where(
                left, outs[2 * g], pltpu.roll(outs[2 * g + 1], DH, 1)
            ).astype(bf16)
        return carry

    lax.fori_loop(0, lanes // GROUP, step, 0)
    held = own_ref.shape[0]
    own_ref[...] = dkv_ref[:held, :]
    away_ref[...] = dkv_ref[held:, :].astype(bf16)


def message_kernel(own_ref, other_ref, dq_ref, msg_ref):
    lanes, record = msg_ref.shape[0], msg_ref.shape[1]
    part_rows = 2 * record // 3

    def step(i, carry):
        at = pl.ds(pl.multiple_of(i * part_rows, part_rows), part_rows)
        total = own_ref[at, :]
        for k in range(other_ref.shape[0]):
            total += other_ref[k, at, :].astype(f32)
        msg_ref[i, :part_rows, :] = total.astype(bf16)
        msg_ref[i, part_rows:, :] = dq_ref[i]
        return carry

    lax.fori_loop(0, lanes, step, 0)


def pack_kernel(share, low_ref, near_ref, far_ref, msg_ref, rows_ref):
    lanes, record = msg_ref.shape[0], msg_ref.shape[1]
    heads = lanes // share
    feat = heads * DH
    part_rows = 2 * record // 3
    pair_rows = part_rows // 2
    half = D // 2
    for c in range(3):
        cols = slice(c * feat, (c + 1) * feat)
        rows_ref[:, cols] = dot(low_ref[:, :half], near_ref[:, cols], 1, 0) + dot(
            low_ref[:, half:], far_ref[:, cols], 1, 0
        )
    left = lax.broadcasted_iota(jnp.int32, (part_rows, 2 * DH), 1) < DH
    for h in range(0, heads, 2):
        for r in range(share):
            at = slice(r * part_rows, (r + 1) * part_rows)
            query, keys, vals = (
                rows_ref[at, c * feat + h * DH : c * feat + (h + 2) * DH] for c in range(3)
            )
            even, odd = h * share + r, (h + 1) * share + r
            msg_ref[even, :part_rows, :] = jnp.where(left, keys, pltpu.roll(vals, DH, 1)).astype(
                bf16
            )
            msg_ref[odd, :part_rows, :] = jnp.where(left, pltpu.roll(keys, DH, 1), vals).astype(
                bf16
            )
            first, second = query[:pair_rows], query[pair_rows:]
            over = left[:pair_rows]
            msg_ref[even, part_rows:, :] = jnp.where(over, first, pltpu.roll(second, DH, 1)).astype(
                bf16
            )
            msg_ref[odd, part_rows:, :] = jnp.where(over, pltpu.roll(first, DH, 1), second).astype(
                bf16
            )


def unpack_pairs(read, heads, share, pair_rows, write):
    left = lax.broadcasted_iota(jnp.int32, (pair_rows, 2 * DH), 1) < DH
    for h in range(0, heads, 2):
        cols = slice(h * DH, (h + 2) * DH)
        for r in range(share):
            even, odd = read(h * share + r), read((h + 1) * share + r)
            base = 2 * r * pair_rows
            first = jnp.where(left, even, pltpu.roll(odd, DH, 1))
            second = jnp.where(left, pltpu.roll(even, DH, 1), odd)
            write(slice(base, base + pair_rows), cols, first)
            write(slice(base + pair_rows, base + 2 * pair_rows), cols, second)


def project_kernel(share, pairs_ref, proj_ref, ctx_ref, out_ref):
    heads, pair_rows = pairs_ref.shape[0] // share, pairs_ref.shape[1]

    def write(rows, cols, value):
        ctx_ref[rows, cols] = value.astype(bf16)

    unpack_pairs(lambda n: pairs_ref[n].astype(f32), heads, share, pair_rows, write)
    out_ref[...] = dot(ctx_ref[...], proj_ref[...], 1, 1).astype(bf16)


def dctx_kernel(share, low_ref, proj_ref, pairs_ref):
    heads, pair_rows = pairs_ref.shape[0] // share, pairs_ref.shape[1]
    left = lax.broadcasted_iota(jnp.int32, (pair_rows, 2 * DH), 1) < DH
    grad = dot(low_ref[...], proj_ref[...], 1, 0)
    for h in range(0, heads, 2):
        cols = slice(h * DH, (h + 2) * DH)
        for r in range(share):
            base = 2 * r * pair_rows
            first = grad[base : base + pair_rows, cols]
            second = grad[base + pair_rows : base + 2 * pair_rows, cols]
            pairs_ref[h * share + r] = jnp.where(left, first, pltpu.roll(second, DH, 1)).astype(
                bf16
            )
            pairs_ref[(h + 1) * share + r] = jnp.where(
                left, pltpu.roll(first, DH, 1), second
            ).astype(bf16)


def one_grad_kernel(share, msg_ref, near_ref, far_ref, unit_ref, place_ref, out_ref, late_ref, rows_ref):
    lanes, record = msg_ref.shape[0], msg_ref.shape[1]
    heads = lanes // share
    feat = heads * DH
    part_rows = 2 * record // 3
    pair_rows = part_rows // 2

    def write(rows, cols, value):
        rows_ref[rows, cols] = value.astype(bf16)

    unpack_pairs(
        lambda n: msg_ref[n, part_rows:, :].astype(f32), heads, share, pair_rows, write
    )
    left = lax.broadcasted_iota(jnp.int32, (part_rows, 2 * DH), 1) < DH
    for h in range(0, heads, 2):
        for r in range(share):
            even = msg_ref[h * share + r, :part_rows, :].astype(f32)
            odd = msg_ref[(h + 1) * share + r, :part_rows, :].astype(f32)
            at = slice(r * part_rows, (r + 1) * part_rows)
            keys = jnp.where(left, even, pltpu.roll(odd, DH, 1))
            vals = jnp.where(left, pltpu.roll(even, DH, 1), odd)
            rows_ref[at, feat + h * DH : feat + (h + 2) * DH] = keys.astype(bf16)
            rows_ref[at, 2 * feat + h * DH : 2 * feat + (h + 2) * DH] = vals.astype(bf16)
    half = D // 2
    cols = slice(0, rows_ref.shape[1])
    out_ref[:, :half] = dot(rows_ref[...], near_ref[:, cols], 1, 1).astype(bf16)
    out_ref[:, half:] = dot(rows_ref[...], far_ref[:, cols], 1, 1).astype(bf16)
    grad = out_ref[...].astype(f32)
    gain = jnp.sum(grad * unit_ref[...], axis=0, keepdims=True)
    shift = jnp.sum(grad, axis=0, keepdims=True)
    sums = jnp.concatenate([gain, shift, jnp.zeros((14, D), f32)], axis=0)
    total = 0.0
    for _ in range(3):
        low = sums.astype(bf16)
        total += dot(low, place_ref[...], 1, 1)
        sums = sums - low.astype(f32)
    late_ref[...] = total


def weight_grad_kernel(lhs_a, rhs_a, lhs_b, rhs_b, out_ref, *, first):
    at = pl.program_id(0)

    @pl.when(at < first)
    def _():
        out_ref[...] = dot(lhs_a[...], rhs_a[...], 0, 0).astype(bf16)

    @pl.when(at >= first)
    def _():
        out_ref[...] = dot(lhs_b[...], rhs_b[...], 0, 0).astype(bf16)


VMEM_LIMIT = 48 * 1024 * 1024


def in_smem():
    return pl.BlockSpec(memory_space=pltpu.SMEM)


def call(kernel, outs, specs, scratch=(), out_specs=None):
    return pl.pallas_call(
        kernel,
        grid=(1,),
        out_shape=outs,
        in_specs=specs,
        out_specs=jax.tree.map(lambda o: whole(o.shape), outs) if out_specs is None else out_specs,
        scratch_shapes=list(scratch),
        compiler_params=pltpu.CompilerParams(vmem_limit_bytes=VMEM_LIMIT),
    )


def whole(shape):
    return pl.BlockSpec(tuple(shape), lambda i: (0,) * len(shape))


def array(shape, dtype=bf16):
    return jax.ShapeDtypeStruct(shape, dtype)


def ffn_weight_grads(first, second, aside, more):
    units = first[1].shape[1]
    block = min(512, units)
    counts = (units // block, (units - aside) // block)
    specs = []
    for start, skip, count, (lhs, rhs) in (
        (0, 0, counts[0], first),
        (counts[0], aside // block, counts[1], second),
    ):
        specs.append(whole(lhs.shape))
        specs.append(
            pl.BlockSpec(
                (rhs.shape[0], block),
                lambda i, start=start, skip=skip, count=count: (
                    0,
                    jnp.clip(i - start, 0, count - 1) + skip,
                ),
            )
        )
    width = 2 * units - aside
    return pl.pallas_call(
        functools.partial(weight_grad_kernel, first=counts[0]),
        grid=(sum(counts),),
        out_shape=array((D, width + more)),
        in_specs=specs,
        out_specs=pl.BlockSpec((D, block), lambda i: (0, i)),
        compiler_params=pltpu.CompilerParams(vmem_limit_bytes=VMEM_LIMIT),
        cost_estimate=pl.CostEstimate(
            flops=2 * D * width * first[1].shape[0], bytes_accessed=2 * D * width, transcendentals=0
        ),
    )(*first, *second)


def body(
    layer_input,
    output_grad,
    random_pick,
    doc_blocks,
    last_fill,
    shard_owner,
    qkv_weight,
    qkv_first,
    qkv_second,
    proj_weight,
    proj_first,
    proj_second,
    up_weight,
    up_first,
    up_second,
    down_weight,
    down_first,
    down_second,
    vec_params,
    vec_first,
    vec_second,
):
    lanes = lax.axis_size("seq")
    lane_index = lax.axis_index("seq")
    head_groups = lax.axis_size("head")
    head_index = lax.axis_index("head")
    slots = layer_input.shape[0]
    heads = random_pick.shape[2]
    feat = heads * DH
    units = up_weight.shape[1]
    rows = slots * BLOCK
    block_total = slots * lanes
    share = lanes // heads
    part_rows = rows // share
    pair_rows = part_rows // 2
    my_part = lane_index % share
    my_head = lane_index // share
    width = D // lanes

    qkv_mine = qkv_weight.astype(bf16).transpose(1, 0, 2).reshape(width, 3 * feat)
    pick_count = slots * heads * 3
    pick_rows = random_pick[:, 0].reshape(1, pick_count)
    pick_rows = jnp.concatenate([pick_rows // 256, pick_rows % 256], axis=0)
    pick_rows = jnp.pad(pick_rows, ((0, width - 2), (0, 2 * DH - pick_count)))
    qkv_mine = jnp.concatenate([qkv_mine, pick_rows.astype(bf16)], axis=1)
    first_mine = jnp.concatenate([up_weight.astype(bf16), proj_weight.astype(bf16).T], axis=1)
    first_full = lax.all_gather(first_mine, "seq", axis=0, tiled=True)
    up_full = first_full[:, :units]
    proj_block = pl.BlockSpec((D, feat), lambda i: (0, units // feat))

    column = jnp.arange(D, dtype=jnp.int32)
    owner = lookup(shard_owner, column // width)
    masks = jnp.array(relative_lanes(lanes), jnp.int32)
    position = jnp.sum(
        jnp.where(
            masks[None, :] == (owner ^ lane_index)[:, None], jnp.arange(lanes, dtype=jnp.int32), 0
        ),
        axis=1,
    )
    place = (owner * width + column % width)[:, None] == column[None, :]
    place_near = (position * width + column % width)[:, None] == column[None, :]
    place, place_near = place.astype(bf16), place_near.astype(bf16)
    rows_in = layer_input.reshape(rows, D)
    token_rows = dot(rows_in, place, 1, 0)
    grad_low = dot(output_grad.reshape(rows, D), place, 1, 0).astype(bf16)
    grad_rows = grad_low.astype(f32)
    exact = functools.partial(
        lax.dot_general, precision=lax.Precision.HIGHEST, preferred_element_type=f32
    )
    ahead = (((1,), (0,)), ((), ()))
    back = (((1,), (1,)), ((), ()))
    vec_rows = exact(vec_params[:5], place.astype(f32), ahead)
    vec_near = exact(vec_params[:2], place_near.astype(f32), ahead)
    up_bias = lax.dynamic_slice_in_dim(vec_params[5:].reshape(FF), head_index * units, units)

    normed_one, unit_one, scale_one = norm_rows(
        dot(rows_in, place_near, 1, 0), vec_near[0], vec_near[1]
    )
    low_one = normed_one.astype(bf16)
    qkv_near, qkv_far, low_one = relative_gather(qkv_mine, low_one)
    half = D // 2
    record = part_rows + pair_rows
    message = call(
        functools.partial(pack_kernel, share),
        array((lanes, record, 2 * DH)),
        [whole((rows, D)), whole(qkv_near.shape), whole(qkv_far.shape)],
        [pltpu.VMEM((rows, 3 * feat), f32)],
    )(low_one, qkv_near, qkv_far)
    down_mine = down_weight.astype(bf16).T
    pick_bytes = [
        part.reshape(-1, width, 3 * feat + 2 * DH)[:, :2, 3 * feat : 3 * feat + pick_count]
        for part in (qkv_near, qkv_far)
    ]
    message, pick_bytes, down_mine = lax.optimization_barrier((message, pick_bytes, down_mine))
    down_full = lax.all_gather(down_mine, "seq", axis=0, tiled=True)
    received = lax.all_to_all(message, "seq", 0, 0, tiled=True)

    pick_bytes = jnp.concatenate(pick_bytes, axis=0).astype(f32).astype(jnp.int32)
    picks = (pick_bytes[:, 0] * 256 + pick_bytes[:, 1]).reshape(lanes, slots, heads, 3)
    picks = lax.dynamic_index_in_dim(picks, my_head, 2, keepdims=False)
    from_lane = jnp.arange(lanes, dtype=jnp.int32) ^ lane_index
    picks = jnp.sum(
        jnp.where((masks[None, :] == from_lane[:, None])[..., None, None], picks[None], 0), axis=1
    )

    doc_end = jnp.cumsum(doc_blocks)
    doc_start = doc_end - doc_blocks
    doc_length = (doc_blocks - 1) * BLOCK + last_fill
    half_slot = (my_part * part_rows + jnp.arange(2, dtype=jnp.int32) * pair_rows) // BLOCK
    query_ids = half_slot[None, :] * lanes + jnp.arange(lanes, dtype=jnp.int32)[:, None]
    pick_half = jnp.sum(
        jnp.where(
            (half_slot[:, None] == jnp.arange(slots, dtype=jnp.int32)[None, :])[None, :, :, None],
            picks[:, None],
            0,
        ),
        axis=2,
    )
    query_doc = owning_doc(doc_end, query_ids)
    doc_first = lookup(doc_start, query_doc)
    doc_count = lookup(doc_blocks, query_doc)
    query_length = lookup(doc_length, query_doc)
    key_ids = jnp.concatenate(
        [
            jnp.stack(
                [
                    (query_ids - 1) % block_total,
                    query_ids,
                    (query_ids + 1) % block_total,
                    doc_first,
                    (doc_first + 1) % block_total,
                ],
                axis=-1,
            ),
            doc_first[..., None] + pick_half % doc_count[..., None],
        ],
        axis=-1,
    )
    same_doc = owning_doc(doc_end, key_ids) == query_doc[..., None]
    live_count = jnp.where(
        same_doc, query_length[..., None] - (key_ids - doc_first[..., None]) * BLOCK, 0
    )
    token = jnp.arange(BLOCK, dtype=jnp.int32)
    bias = jnp.where(token < live_count[..., None], 0.0, masked_score).astype(f32)
    bias = bias.reshape(lanes, 2, LISTED * BLOCK)
    key_lane = key_ids % lanes
    key_slot = key_ids // lanes
    if part_rows >= BLOCK:
        part_slots = part_rows // BLOCK
        offsets = (((key_slot // part_slots) ^ my_part) * lanes + key_lane) * part_rows
        offsets += (key_slot % part_slots) * BLOCK
    else:
        offsets = (key_lane * slots + key_slot) * BLOCK
    offsets = offsets.reshape(lanes * 2, LISTED)
    received, offsets, bias = lax.optimization_barrier((received, offsets, bias))

    parts = jnp.arange(share, dtype=jnp.int32)
    sources = [received] + [xor_permute(received, "seq", k) for k in range(1, share)]
    if part_rows < BLOCK:
        kv_parts = jnp.stack([part[:, :part_rows] for part in sources])
        kv_parts = kv_parts[parts ^ my_part].transpose(1, 0, 2, 3)
        sources = [kv_parts.reshape(lanes, slots * BLOCK, 2 * DH)]
    kv_shape = (block_total * BLOCK, 2 * DH)
    pairs_shape = (lanes, pair_rows, 2 * DH)
    probs_shape = (lanes, 2, pair_rows, LISTED * BLOCK)

    attend_specs = [in_smem(), whole(received.shape)] + [whole(part.shape) for part in sources]
    ctx_pairs, probs = call(
        attend_kernel,
        (array(pairs_shape), array(probs_shape)),
        attend_specs + [whole(bias.shape)],
        [pltpu.VMEM(kv_shape, bf16)],
    )(offsets, received, *sources, bias)
    ctx_pairs = lax.all_to_all(ctx_pairs, "seq", 0, 0, tiled=True)

    context, attn_part = call(
        functools.partial(project_kernel, share),
        (array((rows, feat)), array((rows, D))),
        [whole(pairs_shape), proj_block],
    )(ctx_pairs, first_full)
    attn_sum = head_total(attn_part, head_other(attn_part))
    mid_rows = token_rows + attn_sum
    normed_two, unit_two, scale_two = norm_rows(mid_rows, vec_rows[2], vec_rows[3])
    low_two, down_full = lax.optimization_barrier((normed_two.astype(bf16), down_full))
    hidden = dot(low_two, up_full, 1, 0) + up_bias
    active = gelu_tanh(hidden).astype(bf16)
    act_grad = dot(grad_low, down_full, 1, 0)
    hidden_grad = jax.vjp(gelu_tanh, hidden)[1](act_grad)[0]
    hidden_low = hidden_grad.astype(bf16)
    two_part = dot(hidden_low, up_full, 1, 1).astype(bf16)
    two_other = head_other(two_part)
    ffn_grads = ffn_weight_grads((low_two, hidden_low), (grad_low, active), 0, 0)
    two_other, ffn_grads = lax.optimization_barrier((two_other, ffn_grads))
    ffn_owned = lax.psum_scatter(ffn_grads, "seq", scatter_dimension=0, tiled=True).astype(f32)
    two_grad = head_total(two_part, two_other)
    up_bias_grad = jnp.sum(hidden_grad, axis=0)

    mid_grad = grad_rows + norm_back(two_grad, unit_two, scale_two, vec_rows[2])
    attn_low = mid_grad.astype(bf16)
    dctx_pairs = call(
        functools.partial(dctx_kernel, share),
        array(pairs_shape),
        [whole((rows, D)), proj_block],
    )(attn_low, first_full)
    dctx_pairs = lax.all_to_all(dctx_pairs, "seq", 0, 0, tiled=True)
    dctx_pairs, ffn_grads = lax.optimization_barrier((dctx_pairs, ffn_grads))
    held_rows = lanes * part_rows
    away_rows = kv_shape[0] - held_rows
    if part_rows < BLOCK:
        back_shapes = (kv_shape[0] // 2,) * 2
    else:
        back_shapes = (held_rows, away_rows)
    dq_pairs, dkv_own, dkv_away = call(
        attend_back_kernel,
        (
            array(pairs_shape),
            array((back_shapes[0], 2 * DH), f32),
            array((back_shapes[1], 2 * DH)),
        ),
        attend_specs + [whole(probs_shape), whole(pairs_shape)],
        [pltpu.VMEM(kv_shape, bf16), pltpu.VMEM(kv_shape, f32)],
    )(offsets, received, *sources, probs, dctx_pairs)
    if part_rows < BLOCK:
        dkv_parts = jnp.concatenate([dkv_own, dkv_away.astype(f32)], axis=0)
        dkv_parts = dkv_parts.reshape(lanes, share, part_rows, 2 * DH)
        dkv_parts = dkv_parts[:, parts ^ my_part].transpose(1, 0, 2, 3)
        dkv_own = dkv_parts[0].reshape(held_rows, 2 * DH)
        dkv_away = dkv_parts[1:].astype(bf16)
    dkv_away = dkv_away.reshape(share - 1, held_rows, 2 * DH)
    others = jnp.stack([xor_permute(dkv_away[k - 1], "seq", k) for k in range(1, share)])
    others, active, attn_low = lax.optimization_barrier((others, active, attn_low))
    message = call(
        message_kernel,
        array((lanes, record, 2 * DH)),
        [whole((held_rows, 2 * DH)), whole(others.shape), whole(pairs_shape)],
    )(dkv_own, others, dq_pairs)
    returned = lax.all_to_all(message, "seq", 0, 0, tiled=True)
    attn_near = dot(attn_low, dot(place, place_near, 0, 0).astype(bf16), 1, 0).astype(bf16)
    proj_far = dot(attn_near[:, half:], context, 0, 0).astype(bf16)
    proj_sums = added(dot(attn_near[:, :half], context, 0, 0), [xor_permute(proj_far, "seq", 1)])
    proj_kept, proj_sent = y_parts(proj_sums)
    proj_other = y_others(proj_sent)
    ffn_part = dot(active, down_full, 1, 1).astype(bf16)
    ffn_other = head_other(ffn_part)
    early_rows = jnp.stack(
        [jnp.sum(two_grad * unit_two, axis=0), jnp.sum(two_grad, axis=0), jnp.sum(grad_rows, axis=0)]
    )
    early_rows = exact(early_rows, place.astype(f32), back)
    early_rows = jnp.concatenate([early_rows, up_bias_grad.reshape(units // D, D)], axis=0)
    returned, ffn_other, early_rows = lax.optimization_barrier((returned, ffn_other, early_rows))
    result = (mid_rows + head_total(ffn_part, ffn_other) + vec_rows[4]).astype(bf16)
    one_part, late_rows, dqkv = call(
        functools.partial(one_grad_kernel, share),
        (array((rows, D)), array((16, D), f32), array((rows, 3 * feat))),
        [whole(message.shape), whole(qkv_near.shape), whole(qkv_far.shape)]
        + [whole((rows, D)), whole((D, D))],
    )(returned, qkv_near, qkv_far, unit_one, place_near)
    one_other = head_other(one_part)
    vec_sums = jnp.concatenate([late_rows[:2], early_rows], axis=0)
    vec_sums, proj_other = lax.optimization_barrier((vec_sums, proj_other))
    proj_kept, proj_sent = z_parts(added(proj_kept, proj_other))
    proj_other = z_others(proj_sent)
    vec_sums = axis_sum(vec_sums, "seq")
    vec_sums, proj_other = lax.optimization_barrier((vec_sums, proj_other))
    proj_owned = added(proj_kept, proj_other)
    late_rows = axis_sum(vec_sums[:2], "head")
    early_rows = vec_sums[2:]

    chunk = 3 * feat // CHUNKS
    far_sums, near_sums = [], []
    for c in range(CHUNKS):
        cols = dqkv[:, c * chunk : (c + 1) * chunk]
        far_sums.append(xor_permute(dot(low_one[:, half:], cols, 0, 0).astype(bf16), "seq", 1))
        near_sums.append(dot(low_one[:, :half], cols, 0, 0))
    qkv_owned = []
    for near_sum, far_sum in zip(near_sums, far_sums):
        kept, sent = y_parts(added(near_sum, [far_sum]))
        kept, sent = z_parts(added(kept, y_others(sent)))
        qkv_owned.append((kept, z_others(sent)))
    qkv_last = qkv_owned.pop()
    qkv_owned = [added(*pair) for pair in qkv_owned]
    one_grad = head_total(one_part, one_other)

    layer_output = lax.dot_general(result, place, back, preferred_element_type=f32).astype(bf16)
    input_grad = exact(mid_grad, place.astype(f32), back) + exact(
        norm_back(one_grad, unit_one, scale_one, vec_near[0]), place_near.astype(f32), back
    )
    bias_rows = early_rows[3:]
    step = 1
    while step < head_groups:
        other = xor_permute(bias_rows, "head", step)
        high = (head_index & step) != 0
        bias_rows = jnp.where(
            high,
            jnp.concatenate([other, bias_rows], axis=0),
            jnp.concatenate([bias_rows, other], axis=0),
        )
        step *= 2
    vec_grad = jnp.concatenate([late_rows, early_rows[:3], bias_rows], axis=0)
    up_grad = ffn_owned[:, :units]
    down_grad = ffn_owned[:, units:].T
    proj_grad = proj_owned.T
    proj_new, proj_first_new, proj_second_new = adam_step(
        proj_weight, proj_grad, proj_first, proj_second, rate_proj
    )
    up_new, up_first_new, up_second_new = adam_step(up_weight, up_grad, up_first, up_second, rate_up)
    down_new, down_first_new, down_second_new = adam_step(
        down_weight, down_grad, down_first, down_second, rate_down
    )
    qkv_last, up_new, down_new, proj_new = lax.optimization_barrier(
        (qkv_last, up_new, down_new, proj_new)
    )
    qkv_owned.append(added(*qkv_last))
    qkv_grad = jnp.concatenate(qkv_owned, axis=1).reshape(width, 3, feat).transpose(1, 0, 2)
    qkv_new, qkv_first_new, qkv_second_new = adam_step(
        qkv_weight, qkv_grad, qkv_first, qkv_second, rate_qkv
    )
    vec_new, vec_first_new, vec_second_new = adam_step(
        vec_params, vec_grad, vec_first, vec_second, rate_vector
    )
    return (
        layer_output.reshape(slots, BLOCK, D),
        input_grad.reshape(slots, BLOCK, D),
        qkv_new,
        qkv_first_new,
        qkv_second_new,
        qkv_new.astype(bf16),
        proj_new,
        proj_first_new,
        proj_second_new,
        proj_new.astype(bf16),
        up_new,
        up_first_new,
        up_second_new,
        up_new.astype(bf16),
        down_new,
        down_first_new,
        down_second_new,
        down_new.astype(bf16),
        vec_new,
        vec_first_new,
        vec_second_new,
    )


def solution(mesh):
    rows_by_seq = P(None, "seq", None)
    cols = P("head", "seq")
    ups = P("seq", "head")
    qkvs = P(None, "seq", "head")
    placed = (
        (rows_by_seq, rows_by_seq, P(None, "seq", "head", None), P(), P(), P())
        + (qkvs,) * 3
        + (cols,) * 3
        + (ups,) * 3
        + (cols,) * 3
        + (P(),) * 3
    )
    return jax.shard_map(
        body,
        mesh=mesh,
        in_specs=placed,
        out_specs=(rows_by_seq, rows_by_seq)
        + (qkvs,) * 4
        + (cols,) * 4
        + (ups,) * 4
        + (cols,) * 4
        + (P(),) * 3,
        check_vma=False,
    )
```
